32 devices in a mesh: dp: 8 (over y, x, core), tp: 4 (over z).
Axes of the slice: x: 2, y: 2, z: 4, core: 2. Of those that a mesh axis runs over, the one named last changes fastest.
Arguments:
- tokens: bfloat16 [16384, 768], P(('dp', 'tp')), may hold values from -6 to 6
- out_grad: bfloat16 [16384, 768], P(('dp', 'tp')), may hold values from -6 to 6
- segment_ids: int32 [16384], P(('dp', 'tp')), may hold values from 0 to 127, as said below
- attn_master: float32 [4, 768, 768], P(None, 'dp', 'tp')
- attn_first: float32 [4, 768, 768], P(None, 'dp', 'tp')
- attn_second: float32 [4, 768, 768], P(None, 'dp', 'tp')
- mlp_master: float32 [2, 768, 3072], P(None, 'dp', 'tp')
- mlp_first: float32 [2, 768, 3072], P(None, 'dp', 'tp')
- mlp_second: float32 [2, 768, 3072], P(None, 'dp', 'tp')
- vec_master: float32 [9216], replicated
- vec_first: float32 [9216], replicated
- vec_second: float32 [9216], replicated
Outputs:
- layer_out: bfloat16 [16384, 768], P(('dp', 'tp'))
- pooled: float32 [4096, 768], P(('dp', 'tp'))
- input_grad: bfloat16 [16384, 768], P(('dp', 'tp'))
- attn_first_new: float32 [4, 768, 768], P(None, 'dp', 'tp')
- attn_second_new: float32 [4, 768, 768], P(None, 'dp', 'tp')
- attn_new: float32 [4, 768, 768], P(None, 'dp', 'tp')
- attn_copy: bfloat16 [4, 768, 768], P(None, 'dp', 'tp')
- mlp_first_new: float32 [2, 768, 3072], P(None, 'dp', 'tp')
- mlp_second_new: float32 [2, 768, 3072], P(None, 'dp', 'tp')
- mlp_new: float32 [2, 768, 3072], P(None, 'dp', 'tp')
- mlp_copy: bfloat16 [2, 768, 3072], P(None, 'dp', 'tp')
- vec_first_new: float32 [9216], replicated
- vec_second_new: float32 [9216], replicated
- vec_new: float32 [9216], replicated
- vec_copy: bfloat16 [9216], replicated
The draws below stay inside these ranges and needn't reach their ends.
Inputs may be any that keep to these rules, and one draw needn't show every extreme that they name: `segment_ids`: within each document of 512 rows the ids start at 0, never fall and rise by at most one from a row to the next; a document has 5 to 128 segments, and some document has 128 in every draw.
All inputs are finite; a program needn't handle non-finite values.
Results may differ from the reference program's by a relative error of at most 0.02.
Values may be sent and summed in bfloat16 or wider, within the bound.
No kernel may reach another device: no remote copies, remote signals or barrier semaphores. Data moves between devices by JAX's collectives and lax.ppermute only.
A program may use at most 128 MiB of HBM per device.

```python
import math
import jax
import jax.numpy as jnp
from jax import lax

D = 768
HEADS = 12
HEAD_DIM = 64
FF = 3072
SEQ = 512
SEGS = 128
STEP = 10
DOCS = 32
TOKENS = 16384
VEC = 9216


def first_state(key, shape, factors):
    return jax.random.normal(key, shape, jnp.float32) * (factors * (0.1 / 0.9) * math.sqrt(TOKENS))


def second_state(key, shape, factors):
    spread = jnp.exp(jax.random.uniform(key, shape, jnp.float32, math.log(0.5), math.log(8.0)))
    return spread * (factors * factors * (0.001 / 0.999) * TOKENS)


def attn_factors():
    return jnp.array([0.3, 0.3, 0.7, 0.07], jnp.float32)[:, None, None]


def mlp_factors():
    return jnp.array([0.3, 0.4], jnp.float32)[:, None, None]


def vector_factors():
    return jnp.concatenate([jnp.full((D,), 0.3, jnp.float32), jnp.full((D,), 0.7, jnp.float32), jnp.full((FF,), 0.2, jnp.float32), jnp.full((D,), 0.7, jnp.float32), jnp.full((D,), 0.7, jnp.float32), jnp.full((D,), 0.7, jnp.float32), jnp.full((D,), 0.7, jnp.float32), jnp.full((D,), 1.0, jnp.float32), jnp.full((D,), 1.0, jnp.float32)])


def draw_segment_ids(key, part):
    key = jax.random.fold_in(key, 5)
    key_first, key_second, key_chosen, key_order = jax.random.split(key, 4)
    spare = SEGS - 5
    first_pick = jax.random.randint(key_first, (DOCS,), 0, spare + 1)
    second_pick = jax.random.randint(key_second, (DOCS,), 0, spare + 1)
    counts = 5 + first_pick * second_pick // spare
    chosen = jax.random.randint(key_chosen, (), 0, DOCS)
    counts = jnp.where(jnp.arange(DOCS, dtype=jnp.int32) == chosen, SEGS, counts)
    ranking = jax.random.randint(key_order, (DOCS, SEQ - 1), 0, 1 << 20) * SEQ + jnp.arange(SEQ - 1, dtype=jnp.int32)[None, :]
    order = jnp.argsort(ranking, axis=1)
    places = jnp.argsort(order, axis=1)
    cuts = (places < counts[:, None] - 1).astype(jnp.int32)
    ids = jnp.concatenate([jnp.zeros((DOCS, 1), jnp.int32), jnp.cumsum(cuts, axis=1).astype(jnp.int32)], axis=1)
    return ids.reshape(TOKENS)


def draw_attn_master(key, part):
    key = jax.random.fold_in(key, 11)
    spread = jnp.array([D ** (-0.5), D ** (-0.5), D ** (-0.5), max(D // 64, 1) ** (-0.5)], jnp.float32)
    return jax.random.normal(key, (4, D, D), jnp.float32) * spread[:, None, None]


def draw_attn_first(key, part):
    key = jax.random.fold_in(key, 12)
    return first_state(key, (4, D, D), attn_factors())


def draw_attn_second(key, part):
    key = jax.random.fold_in(key, 13)
    return second_state(key, (4, D, D), attn_factors())


def draw_mlp_master(key, part):
    key = jax.random.fold_in(key, 21)
    spread = jnp.array([D ** (-0.5), FF ** (-0.5)], jnp.float32)
    return jax.random.normal(key, (2, D, FF), jnp.float32) * spread[:, None, None]


def draw_mlp_first(key, part):
    key = jax.random.fold_in(key, 22)
    return first_state(key, (2, D, FF), mlp_factors())


def draw_mlp_second(key, part):
    key = jax.random.fold_in(key, 23)
    return second_state(key, (2, D, FF), mlp_factors())


def draw_vec_master(key, part):
    key = jax.random.fold_in(key, 31)
    noise_key, gain_key = jax.random.split(key)
    position = jnp.arange(VEC, dtype=jnp.int32)
    offset = 2 * D + FF
    is_gain = (position >= offset + 2 * D) & (position < offset + 3 * D) | (position >= offset + 4 * D) & (position < offset + 5 * D)
    gains = jax.random.uniform(gain_key, (VEC,), jnp.float32, 0.6, 1.4)
    biases = 0.2 * jax.random.normal(noise_key, (VEC,), jnp.float32)
    return jnp.where(is_gain, gains, biases)


def draw_vec_first(key, part):
    key = jax.random.fold_in(key, 32)
    return first_state(key, (VEC,), vector_factors())


def draw_vec_second(key, part):
    key = jax.random.fold_in(key, 33)
    return second_state(key, (VEC,), vector_factors())


def level_of(own_key, shape, pieces, low, top_value):
    loudness, own = 1.0, jax.random.fold_in(own_key, 6)
    for dim, shards_of in pieces:
        heights = jnp.exp(jax.random.uniform(jax.random.fold_in(own, dim), (shards_of,), jnp.float32, low / len(pieces), top_value / len(pieces)))
        loudness = loudness * jnp.repeat(heights, shape[dim] // shards_of).reshape([-1 if axis == dim else 1 for axis in range(len(shape))])
    return loudness


def scatter_about(own_key, extent, deviation, most, cuts=(), held_as=jnp.bfloat16):
    factor_of = level_of(own_key, extent, cuts, -0.22, 0.18) if cuts else 1.0
    values = jax.random.normal(own_key, extent, jnp.float32) * deviation * factor_of
    return jnp.minimum(jnp.maximum(values, -most), most).astype(held_as)


def setup_inputs(seed: int = 0) -> dict:
    key_of = jax.random.split(jax.random.key(seed), 13)
    return {
        "tokens": scatter_about(key_of[0], (TOKENS, D), 1.0, 6.0, ((0, 32),)),
        "out_grad": scatter_about(key_of[1], (TOKENS, D), 1.0, 6.0, ((0, 32),)),
        "segment_ids": draw_segment_ids(jax.random.fold_in(key_of[12], 71), 0),
        "attn_master": draw_attn_master(jax.random.fold_in(key_of[12], 71), 0),
        "attn_first": draw_attn_first(jax.random.fold_in(key_of[12], 71), 0),
        "attn_second": draw_attn_second(jax.random.fold_in(key_of[12], 71), 0),
        "mlp_master": draw_mlp_master(jax.random.fold_in(key_of[12], 71), 0),
        "mlp_first": draw_mlp_first(jax.random.fold_in(key_of[12], 71), 0),
        "mlp_second": draw_mlp_second(jax.random.fold_in(key_of[12], 71), 0),
        "vec_master": draw_vec_master(jax.random.fold_in(key_of[12], 71), 0),
        "vec_first": draw_vec_first(jax.random.fold_in(key_of[12], 71), 0),
        "vec_second": draw_vec_second(jax.random.fold_in(key_of[12], 71), 0),
    }


NORM_EPS = 1e-12
BETA_ONE = 0.9
BETA_TWO = 0.999
ADAM_EPS = 1e-06
MATRIX_RATE = 0.1
VECTOR_RATE = 0.3
MATRIX_DECAY = 0.01
HIGHEST = lax.Precision.HIGHEST

@jax.custom_vjp
def low(v):
    return lax.optimization_barrier(v.astype(jnp.bfloat16)).astype(jnp.float32)

@jax.custom_vjp
def low_back(v):
    return v

def low_keep(v):
    return (low(v), None)

def low_pass(kept, grad):
    return (grad,)

def back_keep(v):
    return (v, None)

def back_low(kept, grad):
    return (low(grad),)
low.defvjp(low_keep, low_pass)
low_back.defvjp(back_keep, back_low)

def layer_norm(inputs, norm_gain, norm_shift):
    row_mean = lax.optimization_barrier(jnp.mean(inputs, axis=-1, keepdims=True))
    centred = inputs - row_mean
    row_var = lax.optimization_barrier(jnp.mean(centred * centred, axis=-1, keepdims=True))
    return centred * lax.rsqrt(row_var + NORM_EPS) * norm_gain + norm_shift

def attention_block(queries, key_rows, values):
    scores = low_back(jnp.einsum('nqhd,nkhd->nhqk', queries, key_rows, precision=HIGHEST) * HEAD_DIM ** (-0.5))
    attn_probs = jax.nn.softmax(scores, axis=-1)
    return jnp.einsum('nhqk,nkhd->nqhd', low(attn_probs), values, precision=HIGHEST)

def forward(token_rows, attn_weights, mlp_weights, vec_weights):
    attn_low = low(attn_weights)
    mlp_low = low(mlp_weights)
    vec_low = low(vec_weights)
    offset = 2 * D + FF
    bias_query = vec_low[0:D]
    bias_value = vec_low[D:2 * D]
    bias_hidden = vec_low[2 * D:offset]
    bias_out = vec_low[offset:offset + D]
    bias_two = vec_low[offset + D:offset + 2 * D]
    gain_one = vec_low[offset + 2 * D:offset + 3 * D]
    shift_one = vec_low[offset + 3 * D:offset + 4 * D]
    gain_two = vec_low[offset + 4 * D:offset + 5 * D]
    shift_two = vec_low[offset + 5 * D:offset + 6 * D]
    row_total = token_rows.shape[0]
    shaped = (row_total // SEQ, SEQ, HEADS, HEAD_DIM)
    queries = low_back(low(jnp.dot(token_rows, attn_low[0], precision=HIGHEST) + bias_query))
    key_rows = low_back(low(jnp.dot(token_rows, attn_low[1], precision=HIGHEST)))
    values = low_back(low(jnp.dot(token_rows, attn_low[2], precision=HIGHEST) + bias_value))
    context = jax.checkpoint(attention_block)(queries.reshape(shaped), key_rows.reshape(shaped), values.reshape(shaped))
    context = low_back(low(context.reshape(row_total, D)))
    attn_sum = low_back(jnp.dot(context, attn_low[3].T, precision=HIGHEST))
    middle = layer_norm(token_rows + attn_sum + bias_out, gain_one, shift_one)
    pre_act = low_back(jnp.dot(low(middle), mlp_low[0], precision=HIGHEST) + bias_hidden)
    hidden = low(jax.nn.gelu(pre_act, approximate=False))
    mlp_sum = low_back(jnp.dot(hidden, mlp_low[1].T, precision=HIGHEST))
    return layer_norm(middle + mlp_sum + bias_two, gain_two, shift_two)

def adam_update(weight, moment_one, moment_two, gradient, step_rate, decay_rate):
    first_new = BETA_ONE * moment_one + (1.0 - BETA_ONE) * gradient
    second_new = BETA_TWO * moment_two + (1.0 - BETA_TWO) * gradient * gradient
    fix_one = 1.0 - BETA_ONE ** STEP
    fix_two = 1.0 - BETA_TWO ** STEP
    direction = first_new / fix_one / (jnp.sqrt(second_new / fix_two) + ADAM_EPS)
    weight_new = weight - step_rate * (direction + decay_rate * weight)
    return (first_new, second_new, weight_new, weight_new.astype(jnp.bfloat16))

def reference(tokens, out_grad, segment_ids, attn_master, attn_first, attn_second, mlp_master, mlp_first, mlp_second, vec_master, vec_first, vec_second):
    group_docs = 8
    groups = DOCS // group_docs
    group_rows = group_docs * SEQ
    token_groups = tokens.astype(jnp.float32).reshape(groups, group_rows, D)
    grad_groups = out_grad.astype(jnp.float32).reshape(groups, group_rows, D)
    id_groups = segment_ids.reshape(groups, group_docs, SEQ)

    def one_group(running, inputs):
        token_rows, grad_rows, id_rows = inputs
        layer_rows, pullback = jax.vjp(forward, token_rows, attn_master, mlp_master, vec_master)
        grad_tokens, grad_attn, grad_mlp, grad_vec = pullback(grad_rows)
        onehot = (id_rows[:, :, None] == jnp.arange(SEGS, dtype=jnp.int32)[None, None, :]).astype(jnp.float32)
        seg_sums = jnp.einsum('nts,ntd->nsd', onehot, layer_rows.reshape(group_docs, SEQ, D), precision=HIGHEST)
        counts = lax.optimization_barrier(jnp.sum(onehot, axis=1))
        pooled = seg_sums / jnp.maximum(counts, 1.0)[:, :, None]
        running = (running[0] + grad_attn, running[1] + grad_mlp, running[2] + grad_vec)
        return (running, (layer_rows.astype(jnp.bfloat16), pooled, grad_tokens.astype(jnp.bfloat16)))
    start = (jnp.zeros(attn_master.shape, jnp.float32), jnp.zeros(mlp_master.shape, jnp.float32), jnp.zeros(vec_master.shape, jnp.float32))
    totals, outputs = lax.scan(one_group, start, (token_groups, grad_groups, id_groups))
    attn_step = adam_update(attn_master, attn_first, attn_second, totals[0], MATRIX_RATE, MATRIX_DECAY)
    mlp_step = adam_update(mlp_master, mlp_first, mlp_second, totals[1], MATRIX_RATE, MATRIX_DECAY)
    vec_step = adam_update(vec_master, vec_first, vec_second, totals[2], VECTOR_RATE, 0.0)
    return (outputs[0].reshape(TOKENS, D), outputs[1].reshape(DOCS * SEGS, D), outputs[2].reshape(TOKENS, D), attn_step[0], attn_step[1], attn_step[2], attn_step[3], mlp_step[0], mlp_step[1], mlp_step[2], mlp_step[3], vec_step[0], vec_step[1], vec_step[2], vec_step[3])
```

```python
import jax
import jax.numpy as jnp
from jax import lax
from jax.sharding import PartitionSpec as P

HEAD_DIM = 64
FF = 3072
SEQ = 512
SEGS = 128
STEP = 10


NORM_EPS = 1e-12
BETA_ONE = 0.9
BETA_TWO = 0.999
ADAM_EPS = 1e-06
MATRIX_RATE = 0.1
VECTOR_RATE = 0.3
MATRIX_DECAY = 0.01
HIGHEST = lax.Precision.HIGHEST
CONTRACT_COLS = (((1,), (1,)), ((), ()))
CONTRACT_ROWS = (((0,), (0,)), ((), ()))


def layer_norm(inputs, norm_gain, norm_shift):
    row_mean = jnp.mean(inputs, axis=-1, keepdims=True)
    centred = inputs - row_mean
    row_var = jnp.mean(centred * centred, axis=-1, keepdims=True)
    return centred * lax.rsqrt(row_var + NORM_EPS) * norm_gain + norm_shift


def exact_gelu(inputs):
    return jax.nn.gelu(inputs, approximate=False)


def adam_update(weight, moment_one, moment_two, gradient, step_rate, decay_rate):
    first_new = BETA_ONE * moment_one + (1.0 - BETA_ONE) * gradient
    second_new = BETA_TWO * moment_two + (1.0 - BETA_TWO) * gradient * gradient
    fix_one = 1.0 - BETA_ONE**STEP
    fix_two = 1.0 - BETA_TWO**STEP
    direction = first_new / fix_one / (jnp.sqrt(second_new / fix_two) + ADAM_EPS)
    weight_new = weight - step_rate * (direction + decay_rate * weight)
    return (first_new, second_new, weight_new, weight_new.astype(jnp.bfloat16))


def attend(doc_block):
    queries, key_rows, values = doc_block
    scores = jnp.einsum(
        "qhd,khd->hqk", queries, key_rows, preferred_element_type=jnp.float32
    ) * HEAD_DIM ** (-0.5)
    row_max = jnp.max(scores, axis=-1, keepdims=True)
    expanded = jnp.exp(scores - row_max)
    row_total = jnp.sum(expanded, axis=-1, keepdims=True)
    attn_probs = expanded / row_total
    context = jnp.einsum(
        "hqk,khd->qhd", attn_probs.astype(jnp.bfloat16), values, preferred_element_type=jnp.float32
    )
    return (context.astype(jnp.bfloat16), row_max + jnp.log(row_total))


def attend_back(doc_block):
    queries, key_rows, values, log_total, grad_context = doc_block
    scale_factor = HEAD_DIM ** (-0.5)
    scores = (
        jnp.einsum("qhd,khd->hqk", queries, key_rows, preferred_element_type=jnp.float32)
        * scale_factor
    )
    attn_probs = jnp.exp(scores - log_total)
    grad_probs = jnp.einsum(
        "qhd,khd->hqk", grad_context, values, preferred_element_type=jnp.float32
    )
    grad_values = jnp.einsum(
        "hqk,qhd->khd",
        attn_probs.astype(jnp.bfloat16),
        grad_context,
        preferred_element_type=jnp.float32,
    )
    row_dot = jnp.sum(attn_probs * grad_probs, axis=-1, keepdims=True)
    grad_scores = (attn_probs * (grad_probs - row_dot)).astype(jnp.bfloat16)
    grad_queries = (
        jnp.einsum("hqk,khd->qhd", grad_scores, key_rows, preferred_element_type=jnp.float32)
        * scale_factor
    )
    grad_keys = (
        jnp.einsum("hqk,qhd->khd", grad_scores, queries, preferred_element_type=jnp.float32)
        * scale_factor
    )
    return (
        grad_queries.astype(jnp.bfloat16),
        grad_keys.astype(jnp.bfloat16),
        grad_values.astype(jnp.bfloat16),
    )


def on_device(
    tokens,
    out_grad,
    segment_ids,
    attn_master,
    attn_first,
    attn_second,
    mlp_master,
    mlp_first,
    mlp_second,
    vec_master,
    vec_first,
    vec_second,
):
    rows_dev = tokens.shape[0]
    model_width = tokens.shape[1]
    dp_count = lax.axis_size("dp")
    tp_count = lax.axis_size("tp")
    row_dev = attn_master.shape[1]
    col_dev = attn_master.shape[2]
    hidden_dev = mlp_master.shape[2]
    docs_dev = rows_dev // SEQ
    heads = model_width // HEAD_DIM
    shaped = (docs_dev, SEQ, heads, HEAD_DIM)
    both = ("dp", "tp")

    def whole(shard, cols):
        mats = shard.shape[0]
        low = shard.astype(jnp.bfloat16)
        out = lax.all_gather(low, both, axis=0, tiled=False)
        out = out.reshape(dp_count, tp_count, mats, row_dev, cols)
        return out.transpose(2, 0, 3, 1, 4).reshape(mats, model_width, tp_count * cols)

    def reduced(grad, cols):
        mats = grad.shape[0]
        parts = grad.astype(jnp.bfloat16).reshape(mats, dp_count, row_dev, tp_count, cols)
        parts = parts.transpose(1, 3, 0, 2, 4).reshape(dp_count * tp_count * mats, row_dev, cols)
        return lax.psum_scatter(parts, both, scatter_dimension=0, tiled=True).astype(jnp.float32)

    attn_low = whole(attn_master, col_dev)
    mlp_low = whole(mlp_master, hidden_dev)
    vec_low = lax.optimization_barrier(vec_master.astype(jnp.bfloat16)).astype(jnp.float32)
    offset = 2 * model_width + FF
    bias_query = vec_low[0:model_width]
    bias_value = vec_low[model_width : 2 * model_width]
    bias_hidden = vec_low[2 * model_width : offset]
    bias_out = vec_low[offset : offset + model_width]
    bias_two = vec_low[offset + model_width : offset + 2 * model_width]
    gain_one = vec_low[offset + 2 * model_width : offset + 3 * model_width]
    shift_one = vec_low[offset + 3 * model_width : offset + 4 * model_width]
    gain_two = vec_low[offset + 4 * model_width : offset + 5 * model_width]
    shift_two = vec_low[offset + 5 * model_width : offset + 6 * model_width]
    qkv_low = attn_low[0:3]
    out_proj = attn_low[3]
    up_proj = mlp_low[0]
    down_proj = mlp_low[1]
    projected = jnp.einsum("rd,kdc->krc", tokens, qkv_low, preferred_element_type=jnp.float32)
    queries = (projected[0] + bias_query).astype(jnp.bfloat16).reshape(shaped)
    key_rows = projected[1].astype(jnp.bfloat16).reshape(shaped)
    values = (projected[2] + bias_value).astype(jnp.bfloat16).reshape(shaped)
    context, log_total = lax.map(attend, (queries, key_rows, values))
    context = context.reshape(rows_dev, model_width)
    attn_sum = lax.dot_general(context, out_proj, CONTRACT_COLS, preferred_element_type=jnp.float32)
    first_in = tokens.astype(jnp.float32) + attn_sum + bias_out
    middle, norm_one_back = jax.vjp(layer_norm, first_in, gain_one, shift_one)
    middle_all = middle.astype(jnp.bfloat16)
    pre_act = jnp.dot(middle_all, up_proj, preferred_element_type=jnp.float32) + bias_hidden
    hidden, gelu_back = jax.vjp(exact_gelu, pre_act)
    hidden_low = hidden.astype(jnp.bfloat16)
    mlp_sum = lax.dot_general(
        hidden_low, down_proj, CONTRACT_COLS, preferred_element_type=jnp.float32
    )
    second_in = middle + mlp_sum + bias_two
    final, norm_two_back = jax.vjp(layer_norm, second_in, gain_two, shift_two)
    own_slots = rows_dev // SEQ * SEGS
    own_doc = jnp.arange(rows_dev, dtype=jnp.int32) // SEQ
    own_slot = own_doc * SEGS + segment_ids
    own_onehot = (jnp.arange(own_slots, dtype=jnp.int32)[:, None] == own_slot[None, :]).astype(
        jnp.float32
    )
    own_sums = jnp.dot(own_onehot, final, precision=HIGHEST)
    own_counts = jnp.sum(own_onehot, axis=1)
    pooled = own_sums / jnp.maximum(own_counts, 1.0)[:, None]
    grad_second, grad_gain_two, grad_shift_two = norm_two_back(out_grad.astype(jnp.float32))
    shard_piece = grad_second.astype(jnp.bfloat16)
    grad_hidden = jnp.dot(shard_piece, down_proj, preferred_element_type=jnp.float32)
    grad_down = lax.dot_general(
        shard_piece, hidden_low, CONTRACT_ROWS, preferred_element_type=jnp.float32
    )
    grad_pre = gelu_back(grad_hidden)[0].astype(jnp.bfloat16)
    grad_up = lax.dot_general(
        middle_all, grad_pre, CONTRACT_ROWS, preferred_element_type=jnp.float32
    )
    grad_bias_hidden = jnp.sum(grad_pre.astype(jnp.float32), axis=0)
    mlp_reduced = reduced(jnp.stack([grad_up, grad_down]), hidden_dev)
    grad_middle = grad_second + lax.dot_general(
        grad_pre, up_proj, CONTRACT_COLS, preferred_element_type=jnp.float32
    )
    grad_first, grad_gain_one, grad_shift_one = norm_one_back(grad_middle)
    shard_piece = grad_first.astype(jnp.bfloat16)
    grad_context = jnp.dot(shard_piece, out_proj, preferred_element_type=jnp.float32)
    grad_out_proj = lax.dot_general(
        shard_piece, context, CONTRACT_ROWS, preferred_element_type=jnp.float32
    )
    grad_context_low = grad_context.astype(jnp.bfloat16).reshape(shaped)
    grad_queries, grad_keys, grad_values = lax.map(
        attend_back, (queries, key_rows, values, log_total, grad_context_low)
    )
    grad_qkv = jnp.stack(
        [
            grad_queries.reshape(rows_dev, model_width),
            grad_keys.reshape(rows_dev, model_width),
            grad_values.reshape(rows_dev, model_width),
        ]
    )
    grad_qkv_proj = jnp.einsum("rd,krc->kdc", tokens, grad_qkv, preferred_element_type=jnp.float32)
    grad_bias_query = jnp.sum(grad_qkv[0].astype(jnp.float32), axis=0)
    grad_bias_value = jnp.sum(grad_qkv[2].astype(jnp.float32), axis=0)
    grad_tokens = grad_first + jnp.einsum(
        "krc,kdc->rd", grad_qkv, qkv_low, preferred_element_type=jnp.float32
    )
    attn_reduced = reduced(jnp.concatenate([grad_qkv_proj, grad_out_proj[None]], axis=0), col_dev)
    vec_terms = jnp.concatenate(
        [
            grad_bias_query,
            grad_bias_value,
            grad_bias_hidden,
            jnp.sum(grad_first, axis=0),
            jnp.sum(grad_second, axis=0),
            grad_gain_one,
            grad_shift_one,
            grad_gain_two,
            grad_shift_two,
        ]
    )
    vec_grad = jnp.sum(lax.all_gather(vec_terms, both, axis=0, tiled=False), axis=0)
    attn_step = adam_update(
        attn_master, attn_first, attn_second, attn_reduced, MATRIX_RATE, MATRIX_DECAY
    )
    mlp_step = adam_update(
        mlp_master, mlp_first, mlp_second, mlp_reduced, MATRIX_RATE, MATRIX_DECAY
    )
    vec_step = adam_update(vec_master, vec_first, vec_second, vec_grad, VECTOR_RATE, 0.0)
    return (
        final.astype(jnp.bfloat16),
        pooled,
        grad_tokens.astype(jnp.bfloat16),
        *attn_step,
        *mlp_step,
        *vec_step,
    )


def solution(mesh):
    in_specs = (
        P(("dp", "tp"), None),
        P(("dp", "tp"), None),
        P(("dp", "tp")),
        P(None, "dp", "tp"),
        P(None, "dp", "tp"),
        P(None, "dp", "tp"),
        P(None, "dp", "tp"),
        P(None, "dp", "tp"),
        P(None, "dp", "tp"),
        P(),
        P(),
        P(),
    )
    out_specs = (
        P(("dp", "tp"), None),
        P(("dp", "tp"), None),
        P(("dp", "tp"), None),
        P(None, "dp", "tp"),
        P(None, "dp", "tp"),
        P(None, "dp", "tp"),
        P(None, "dp", "tp"),
        P(None, "dp", "tp"),
        P(None, "dp", "tp"),
        P(None, "dp", "tp"),
        P(None, "dp", "tp"),
        P(),
        P(),
        P(),
        P(),
    )
    return jax.shard_map(
        on_device, mesh=mesh, in_specs=in_specs, out_specs=out_specs, check_vma=False
    )
```

```python
import functools

import jax
import jax.numpy as jnp
from jax import lax
from jax.experimental import pallas as pl
from jax.experimental.pallas import tpu as pltpu
from jax.sharding import PartitionSpec as P

HEAD_DIM = 64
SEQ = 512
SEGS = 128
STEP = 10


NORM_EPS = 1e-12
BETA_ONE = 0.9
BETA_TWO = 0.999
ADAM_EPS = 1e-06
MATRIX_RATE = 0.1
VECTOR_RATE = 0.3
MATRIX_DECAY = 0.01
SCALE = HEAD_DIM ** (-0.5)
HALF_ROOT = 0.7071067811865476
PDF_SCALE = 0.3989422804014327
NT = (((1,), (1,)), ((), ()))
BF = jnp.bfloat16
F32 = jnp.float32
MIB = 1 << 20
ROW_CHUNK = 128


def dot(left, right):
    return jnp.dot(left, right, preferred_element_type=F32)


def dot_nt(left, right):
    return lax.dot_general(left, right, NT, preferred_element_type=F32)


def adam_update(weight, moment_one, moment_two, gradient, step_rate, decay_rate):
    first_new = BETA_ONE * moment_one + (1.0 - BETA_ONE) * gradient
    second_new = BETA_TWO * moment_two + (1.0 - BETA_TWO) * gradient * gradient
    fix_one = 1.0 - BETA_ONE**STEP
    fix_two = 1.0 - BETA_TWO**STEP
    direction = first_new / fix_one / (jnp.sqrt(second_new / fix_two) + ADAM_EPS)
    weight_new = weight - step_rate * (direction + decay_rate * weight)
    return (first_new, second_new, weight_new, weight_new.astype(BF))


def piece_copy(place, pieces, held, sems, slot, j):
    rows = pieces[j].shape[1]
    start = pl.multiple_of(place[j] * rows, rows)
    return pltpu.make_async_copy(
        pieces[j].at[slot], held.at[slot, pl.ds(start, rows), :], sems.at[slot, j]
    )


def start_pieces(place, pieces, held, sems):
    for slot in range(held.shape[0]):
        for j in range(len(pieces)):
            piece_copy(place, pieces, held, sems, slot, j).start()


def wait_pieces(place, pieces, held, sems, slot):
    for j in range(len(pieces)):
        piece_copy(place, pieces, held, sems, slot, j).wait()


def write_pieces(place, grad, outs):
    j = 0
    for out in outs:
        rows = out.shape[2]
        for k in range(out.shape[0]):
            start = pl.multiple_of(place[j] * rows, rows)
            out[k, 0] = grad[pl.ds(start, rows), :]
            j += 1


def attn_forward_kernel(count, place, x_ref, bias_ref, vec_ref, *refs):
    pieces, (qkv_ref, probs_ref, ctx_ref, norm_ref, inv_ref), (held, total, sems) = (
        refs[:count],
        refs[count : count + 5],
        refs[count + 5 :],
    )
    slot = pl.program_id(0)
    groups = pl.num_programs(0)
    width = bias_ref.shape[1]
    part = width // 3

    @pl.when(slot == 0)
    def _():
        start_pieces(place, pieces, held, sems)
        total[...] = jnp.zeros_like(total)

    wait_pieces(place, pieces, held, sems, slot)
    own = place[count] ^ slot
    projected = dot(x_ref[...], held[slot, :, 0:width]) + bias_ref[pl.ds(own, 1), :]
    low = projected.astype(BF)
    qkv_ref[0] = low
    parts = []
    for h in range(part // HEAD_DIM):
        lo = h * HEAD_DIM
        q = low[:, lo : lo + HEAD_DIM] * BF(SCALE)
        k = low[:, part + lo : part + lo + HEAD_DIM]
        v = low[:, 2 * part + lo : 2 * part + lo + HEAD_DIM]
        scores = dot_nt(q, k)
        expanded = jnp.exp(scores - jnp.max(scores, axis=-1, keepdims=True))
        inverse = 1.0 / jnp.sum(expanded, axis=-1, keepdims=True)
        probs = (expanded * inverse).astype(BF)
        probs_ref[0, h] = probs
        parts.append(dot(probs, v))
    context = jnp.concatenate(parts, axis=1).astype(BF)
    ctx_ref[0] = context
    total[...] += dot_nt(context, held[slot, :, width:])

    @pl.when(slot == groups - 1)
    def _():
        first_in = x_ref[...].astype(F32) + total[...] + vec_ref[0:1, :]
        centred = first_in - jnp.mean(first_in, axis=-1, keepdims=True)
        inverse = lax.rsqrt(jnp.mean(centred * centred, axis=-1, keepdims=True) + NORM_EPS)
        norm_ref[...] = centred * inverse
        inv_ref[...] = inverse


def mlp_up_kernel(count, place, norm_ref, vec_ref, bias_ref, *refs):
    pieces, (hid_ref, slope_ref), (held, low_ref, sems) = (
        refs[:count],
        refs[count : count + 2],
        refs[count + 2 :],
    )
    slot = pl.program_id(0)

    @pl.when(slot == 0)
    def _():
        start_pieces(place, pieces, held, sems)
        low_ref[...] = (norm_ref[...] * vec_ref[2:3, :] + vec_ref[3:4, :]).astype(BF)

    wait_pieces(place, pieces, held, sems, slot)
    bias = bias_ref[pl.ds(place[count] ^ slot, 1), :]

    def rows(i, carry):
        at = pl.ds(pl.multiple_of(i * ROW_CHUNK, ROW_CHUNK), ROW_CHUNK)
        u = dot(low_ref[at, :], held[slot]) + bias
        cdf = 0.5 + 0.5 * lax.erf(u * HALF_ROOT)
        hid_ref[0, at, :] = (u * cdf).astype(BF)
        slope_ref[0, at, :] = (cdf + u * (jnp.exp(u * u * -0.5) * PDF_SCALE)).astype(BF)
        return carry

    lax.fori_loop(0, low_ref.shape[0] // ROW_CHUNK, rows, 0)


def mlp_down_kernel(count, outs, place, norm_ref, vec_ref, og_ref, ids_ref, hid_ref, *refs):
    pieces = refs[:count]
    out_ref, pool_ref, dres_ref, dlow_ref, sums_ref = refs[count : count + 5]
    grads = refs[count + 5 : count + 5 + outs]
    held, total, dlow_t, grad_low, sems = refs[count + 5 + outs :]
    step = pl.program_id(0)
    groups = pl.num_programs(0) // 2

    @pl.when(step == 0)
    def _():
        start_pieces(place, pieces, held, sems)
        total[...] = norm_ref[...] * vec_ref[2:3, :] + vec_ref[3:4, :] + vec_ref[1:2, :]

    @pl.when(step < groups)
    def _():
        wait_pieces(place, pieces, held, sems, step)
        total[...] += dot_nt(hid_ref[0], held[step])

    @pl.when(step == groups - 1)
    def _():
        second_in = total[...]
        centred = second_in - jnp.mean(second_in, axis=-1, keepdims=True)
        inverse = lax.rsqrt(jnp.mean(centred * centred, axis=-1, keepdims=True) + NORM_EPS)
        normed = centred * inverse
        gain = vec_ref[4:5, :]
        final = normed * gain + vec_ref[5:6, :]
        high = final.astype(BF)
        out_ref[...] = high
        docs = pool_ref.shape[0] // SEGS
        for n in range(docs):
            slots = lax.broadcasted_iota(jnp.int32, (SEGS, SEQ), 0)
            match = slots == ids_ref[n : n + 1, :]
            onehot = jnp.where(match, 1.0, 0.0)
            counts = jnp.sum(onehot, axis=1, keepdims=True)
            marks = onehot.astype(BF)
            at = slice(n * SEQ, (n + 1) * SEQ)
            rest = (final[at] - high[at].astype(F32)).astype(BF)
            sums = dot(marks, high[at]) + dot(marks, rest)
            pool_ref[n * SEGS : (n + 1) * SEGS, :] = sums / jnp.maximum(counts, 1.0)
        cot = og_ref[...].astype(F32)
        scaled = cot * gain
        mean_one = jnp.mean(scaled, axis=-1, keepdims=True)
        mean_two = jnp.mean(scaled * normed, axis=-1, keepdims=True)
        dres = (scaled - mean_one - normed * mean_two) * inverse
        dres_ref[...] = dres
        low = dres.astype(BF)
        dlow_ref[...] = low
        dlow_t[...] = low.T
        sums_ref[0:1, :] = jnp.sum(dres, axis=0, keepdims=True)
        sums_ref[1:2, :] = jnp.sum(cot * normed, axis=0, keepdims=True)
        sums_ref[2:3, :] = jnp.sum(cot, axis=0, keepdims=True)

    @pl.when(step >= groups)
    def _():
        grad_low[...] = dot(dlow_t[...], hid_ref[0]).astype(BF)
        write_pieces(place, grad_low, grads)


def mlp_back_kernel(count, outs, place, norm_ref, inv_ref, vec_ref, dres_ref, dlow_ref, slope_ref, *refs):
    ups, downs = refs[:count], refs[count : 2 * count]
    dfirst_ref, dctx_ref, sums_ref, dbias_ref = refs[2 * count : 2 * count + 4]
    grads = refs[2 * count + 4 : 2 * count + 4 + outs]
    up, down, total, low_t, grad_low, up_sems, down_sems = refs[2 * count + 4 + outs :]
    slot = pl.program_id(0)
    groups = pl.num_programs(0)

    @pl.when(slot == 0)
    def _():
        start_pieces(place, downs, down, down_sems)
        start_pieces(place, ups, up, up_sems)
        low_t[...] = (norm_ref[...] * vec_ref[2:3, :] + vec_ref[3:4, :]).astype(BF).T
        total[...] = dres_ref[...]

    wait_pieces(place, downs, down, down_sems, slot)
    dpre = (dot(dlow_ref[...], down[slot]) * slope_ref[0].astype(F32)).astype(BF)
    grad_low[...] = dot(low_t[...], dpre).astype(BF)
    write_pieces(place, grad_low, grads)
    dbias_ref[pl.ds(place[count] ^ slot, 1), :] = jnp.sum(dpre.astype(F32), axis=0, keepdims=True)
    wait_pieces(place, ups, up, up_sems, slot)
    total[...] += dot_nt(dpre, up[slot])

    @pl.when(slot == groups - 1)
    def _():
        cot = total[...]
        normed = norm_ref[...]
        scaled = cot * vec_ref[2:3, :]
        mean_one = jnp.mean(scaled, axis=-1, keepdims=True)
        mean_two = jnp.mean(scaled * normed, axis=-1, keepdims=True)
        dfirst = (scaled - mean_one - normed * mean_two) * inv_ref[...]
        dfirst_ref[...] = dfirst
        dctx_ref[...] = dfirst.astype(BF)
        sums_ref[0:1, :] = jnp.sum(dfirst, axis=0, keepdims=True)
        sums_ref[1:2, :] = jnp.sum(cot * normed, axis=0, keepdims=True)
        sums_ref[2:3, :] = jnp.sum(cot, axis=0, keepdims=True)


def attn_back_kernel(count, outs, place, x_ref, dout_ref, qkv_ref, probs_ref, ctx_ref, *refs):
    pieces = refs[:count]
    dqkv_ref, dbias_ref = refs[count : count + 2]
    grads = refs[count + 2 : count + 2 + outs]
    held, x_t, dout_t, grad_low, sems = refs[count + 2 + outs :]
    slot = pl.program_id(0)
    width = qkv_ref.shape[2]
    part = width // 3

    @pl.when(slot == 0)
    def _():
        start_pieces(place, pieces, held, sems)
        x_t[...] = x_ref[...].T
        dout_t[...] = dout_ref[...].T

    wait_pieces(place, pieces, held, sems, slot)
    context = ctx_ref[0]
    grad_low[:, width:] = dot(dout_t[...], context).astype(BF)
    dctx = dot(dout_ref[...], held[slot, :, width:]).astype(BF)
    dctx_t = dctx.T
    row_dots = dctx.astype(F32) * context.astype(F32)
    q_t = qkv_ref[0, :, 0:part].T
    dq, dk_t, dv_t = [], [], []
    for h in range(part // HEAD_DIM):
        at = slice(h * HEAD_DIM, (h + 1) * HEAD_DIM)
        k = qkv_ref[0, :, part + h * HEAD_DIM : part + (h + 1) * HEAD_DIM]
        v = qkv_ref[0, :, 2 * part + h * HEAD_DIM : 2 * part + (h + 1) * HEAD_DIM]
        probs = probs_ref[0, h]
        row_dot = jnp.sum(row_dots[:, at], axis=-1, keepdims=True)
        dprobs = dot_nt(dctx[:, at], v)
        dscores = (probs.astype(F32) * (dprobs - row_dot)).astype(BF)
        dv_t.append(dot(dctx_t[at], probs))
        dq.append(dot(dscores, k) * SCALE)
        dk_t.append(dot(q_t[at], dscores) * SCALE)
    dqkv = jnp.concatenate(
        [
            jnp.concatenate(dq, axis=1).astype(BF),
            jnp.concatenate(dk_t, axis=0).astype(BF).T,
            jnp.concatenate(dv_t, axis=0).astype(BF).T,
        ],
        axis=1,
    )
    dqkv_ref[0] = dqkv
    dbias_ref[pl.ds(place[count] ^ slot, 1), :] = jnp.sum(dqkv.astype(F32), axis=0, keepdims=True)
    grad_low[:, 0:width] = dot(x_t[...], dqkv).astype(BF)
    write_pieces(place, grad_low, grads)


def input_grad_kernel(count, place, dfirst_ref, dqkv_ref, *refs):
    pieces, (out_ref,), (held, total, sems) = refs[:count], refs[count : count + 1], refs[count + 1 :]
    slot = pl.program_id(0)
    groups = pl.num_programs(0)
    width = dqkv_ref.shape[2]

    @pl.when(slot == 0)
    def _():
        start_pieces(place, pieces, held, sems)
        total[...] = dfirst_ref[...]

    wait_pieces(place, pieces, held, sems, slot)
    total[...] += dot_nt(dqkv_ref[0], held[slot, :, 0:width])

    @pl.when(slot == groups - 1)
    def _():
        out_ref[...] = total[...].astype(BF)


def whole(shape):
    return pl.BlockSpec(shape, lambda i, place: (0,) * len(shape))


def by_slot(shape, index=lambda i: i):
    return pl.BlockSpec((1,) + shape, lambda i, place: (index(i),) + (0,) * len(shape))


def by_piece(shape, index=lambda i: i):
    return pl.BlockSpec(
        (shape[0], 1) + shape[2:], lambda i, place: (0, index(i)) + (0,) * len(shape[2:])
    )


ANY = pl.BlockSpec(memory_space=pl.ANY)


def call(kernel, name, grid, place, inputs, outputs, scratch, flops, moved, vmem):
    return pl.pallas_call(
        kernel,
        name=name,
        out_shape=[jax.ShapeDtypeStruct(shape, dtype) for shape, dtype, _ in outputs],
        grid_spec=pltpu.PrefetchScalarGridSpec(
            num_scalar_prefetch=1,
            grid=(grid,),
            in_specs=[spec for _, spec in inputs],
            out_specs=[spec for _, _, spec in outputs],
            scratch_shapes=scratch,
        ),
        compiler_params=pltpu.CompilerParams(
            dimension_semantics=("arbitrary",), vmem_limit_bytes=vmem * MIB
        ),
        cost_estimate=pl.CostEstimate(flops=flops, bytes_accessed=moved, transcendentals=0),
    )(place, *[value for value, _ in inputs])


def xor_pairs(count, mask):
    return [(i, i ^ mask) for i in range(count)]


class PlaneTransfers:
    def __init__(self, tp_count):
        self.count = 8
        self.groups = tp_count
        self.first = [(i, i ^ (4 if i & 1 else 2)) for i in range(8)]
        self.second = [(i, i ^ (2 if i & 1 else 4)) for i in range(8)]
        self.cores = xor_pairs(8, 1)
        me = lax.axis_index("dp")
        one = jnp.where(me % 2 == 1, 4, 2)
        two = 6 - one
        self.place = jnp.stack(
            [
                me,
                me ^ one,
                me ^ two,
                me ^ 6,
                me ^ 1,
                me ^ 1 ^ two,
                me ^ 1 ^ one,
                me ^ 7,
                lax.axis_index("tp"),
            ]
        ).astype(jnp.int32)
        self.out_counts = (4, 4)

    def across(self, shard):
        return [shard] + [
            lax.ppermute(shard, "tp", xor_pairs(self.groups, k)) for k in range(1, self.groups)
        ]

    def gather(self, shards):
        one = lax.ppermute(shards, "dp", self.first)
        two = lax.ppermute(shards, "dp", self.second)
        three = lax.ppermute(one, "dp", self.second)
        mine = [shards, one, two, three]
        return mine + [lax.ppermute(piece, "dp", self.cores) for piece in mine]

    def reduce(self, grads):
        keep, send = grads
        other = lax.ppermute(send, "dp", self.cores)

        def kept(k):
            return keep[k].astype(F32) + other[k].astype(F32)

        pair = (keep[2:4].astype(F32) + other[2:4].astype(F32)).astype(BF)
        pair = lax.ppermute(pair, "dp", self.second)
        near = (kept(1) + pair[1].astype(F32)).astype(BF)
        near = lax.ppermute(near, "dp", self.first)
        own = kept(0) + pair[0].astype(F32) + near.astype(F32)
        total = own[0]
        low = own.astype(BF)
        for k in range(1, self.groups):
            total = total + lax.ppermute(low[k], "tp", xor_pairs(self.groups, k)).astype(F32)
        return total


class PlainTransfers:
    def __init__(self, dp_count, tp_count):
        self.dp = dp_count
        self.tp = tp_count
        self.count = 1
        self.place = jnp.zeros((2,), jnp.int32)
        self.out_counts = (1,)

    def across(self, shard):
        return shard

    def gather(self, shards):
        rows, columns = shards.shape
        out = lax.all_gather(shards, ("dp", "tp"), axis=0, tiled=False)
        out = out.reshape(self.dp, self.tp, rows, columns).transpose(1, 0, 2, 3)
        return [out.reshape(self.tp, self.dp * rows, columns)]

    def reduce(self, grads):
        _, groups, rows, columns = grads[0].shape
        parts = grads[0].reshape(groups, self.dp, rows // self.dp, columns).transpose(1, 0, 2, 3)
        parts = parts.reshape(self.dp * groups, rows // self.dp, columns)
        out = lax.psum_scatter(parts, ("dp", "tp"), scatter_dimension=0, tiled=True)
        return out[0].astype(F32)


def on_device(
    tokens,
    out_grad,
    segment_ids,
    attn_master,
    attn_first,
    attn_second,
    mlp_master,
    mlp_first,
    mlp_second,
    vec_master,
    vec_first,
    vec_second,
):
    rows, width = tokens.shape
    dp_count = lax.axis_size("dp")
    groups = lax.axis_size("tp")
    mats, row_dev, col_dev = attn_master.shape
    hidden = mlp_master.shape[2]
    docs = rows // SEQ
    heads = col_dev // HEAD_DIM
    wide = 3 * col_dev
    plane = dp_count == 8 and groups & (groups - 1) == 0 and row_dev % 16 == 0
    moves = PlaneTransfers(groups) if plane else PlainTransfers(dp_count, groups)
    place = moves.place
    count = moves.count
    outs = len(moves.out_counts)
    block = width // count

    attn_low = jnp.concatenate([attn_master[k] for k in range(mats)], axis=1).astype(BF)
    mlp_low = mlp_master.astype(BF)
    vec_low = lax.optimization_barrier(vec_master.astype(BF)).astype(F32)
    bias_query = vec_low[0:width].reshape(groups, col_dev)
    bias_value = vec_low[width : 2 * width].reshape(groups, col_dev)
    bias_qkv = jnp.concatenate([bias_query, jnp.zeros_like(bias_query), bias_value], axis=1)
    ffn = groups * hidden
    bias_hidden = vec_low[2 * width : 2 * width + ffn].reshape(groups, hidden)
    norm_vecs = vec_low[2 * width + ffn :].reshape(6, width)

    if plane:
        attn_across = jnp.stack(moves.across(attn_low))
        mlp_across = moves.across(mlp_low)
        attn_pieces = moves.gather(attn_across)
        up_pieces = moves.gather(jnp.stack([part[0] for part in mlp_across]))
        down_pieces = moves.gather(jnp.stack([part[1] for part in mlp_across]))
    else:
        attn_pieces = moves.gather(attn_low)
        up_pieces = moves.gather(mlp_low[0])
        down_pieces = moves.gather(mlp_low[1])

    full = (rows, width)
    weight = (groups, width, mats * col_dev)
    hid_weight = (groups, width, hidden)
    sems = pltpu.SemaphoreType.DMA((groups, count))
    row_vec = (rows, 1)
    base = 2 * rows * width

    qkv, probs, context, norm_one, inv_one = call(
        functools.partial(attn_forward_kernel, count),
        "attn_forward",
        groups,
        place,
        [(tokens, whole(full)), (bias_qkv, whole(bias_qkv.shape)), (norm_vecs, whole((6, width)))]
        + [(piece, ANY) for piece in attn_pieces],
        [
            ((groups, rows, wide), BF, by_slot((rows, wide))),
            ((groups, heads, rows, rows), BF, by_slot((heads, rows, rows))),
            ((groups, rows, col_dev), BF, by_slot((rows, col_dev))),
            (full, F32, whole(full)),
            (row_vec, F32, whole(row_vec)),
        ],
        [pltpu.VMEM(weight, BF), pltpu.VMEM(full, F32), sems],
        base * groups * (wide + col_dev) + 4 * groups * heads * rows * rows * HEAD_DIM * 4,
        16 * MIB,
        48,
    )
    hid, slope = call(
        functools.partial(mlp_up_kernel, count),
        "mlp_up",
        groups,
        place,
        [
            (norm_one, whole(full)),
            (norm_vecs, whole((6, width))),
            (bias_hidden, whole((groups, hidden))),
        ]
        + [(piece, ANY) for piece in up_pieces],
        [
            ((groups, rows, hidden), BF, by_slot((rows, hidden))),
            ((groups, rows, hidden), BF, by_slot((rows, hidden))),
        ],
        [pltpu.VMEM(hid_weight, BF), pltpu.VMEM(full, BF), sems],
        base * groups * hidden * 3,
        16 * MIB,
        40,
    )

    def grad_outs(columns, index=lambda i: i):
        return [
            ((n, groups, block, columns), BF, by_piece((n, groups, block, columns), index))
            for n in moves.out_counts
        ]

    layer_out, pooled, dres, dres_low, sums_two, *down_grads = call(
        functools.partial(mlp_down_kernel, count, outs),
        "mlp_down",
        2 * groups,
        place,
        [
            (norm_one, whole(full)),
            (norm_vecs, whole((6, width))),
            (out_grad, whole(full)),
            (segment_ids.reshape(docs, SEQ), whole((docs, SEQ))),
            (hid, by_slot((rows, hidden), lambda i: i % groups)),
        ]
        + [(piece, ANY) for piece in down_pieces],
        [
            (full, BF, whole(full)),
            ((docs * SEGS, width), F32, whole((docs * SEGS, width))),
            (full, F32, whole(full)),
            (full, BF, whole(full)),
            ((3, width), F32, whole((3, width))),
        ]
        + grad_outs(hidden, lambda i: jnp.maximum(i - groups, 0)),
        [
            pltpu.VMEM(hid_weight, BF),
            pltpu.VMEM(full, F32),
            pltpu.VMEM((width, rows), BF),
            pltpu.VMEM((width, hidden), BF),
            sems,
        ],
        base * groups * hidden * 2,
        16 * MIB,
        48,
    )
    dfirst, dout, sums_one, dbias_hidden, *up_grads = call(
        functools.partial(mlp_back_kernel, count, outs),
        "mlp_back",
        groups,
        place,
        [
            (norm_one, whole(full)),
            (inv_one, whole(row_vec)),
            (norm_vecs, whole((6, width))),
            (dres, whole(full)),
            (dres_low, whole(full)),
            (slope, by_slot((rows, hidden))),
        ]
        + [(piece, ANY) for piece in up_pieces + down_pieces],
        [
            (full, F32, whole(full)),
            (full, BF, whole(full)),
            ((3, width), F32, whole((3, width))),
            ((groups, hidden), F32, whole((groups, hidden))),
        ]
        + grad_outs(hidden),
        [
            pltpu.VMEM(hid_weight, BF),
            pltpu.VMEM(hid_weight, BF),
            pltpu.VMEM(full, F32),
            pltpu.VMEM((width, rows), BF),
            pltpu.VMEM((width, hidden), BF),
            sems,
            sems,
        ],
        base * groups * hidden * 3,
        24 * MIB,
        56,
    )
    down_sum = moves.reduce(down_grads)
    dqkv, dbias_qkv, *attn_grads = call(
        functools.partial(attn_back_kernel, count, outs),
        "attn_back",
        groups,
        place,
        [
            (tokens, whole(full)),
            (dout, whole(full)),
            (qkv, by_slot((rows, wide))),
            (probs, by_slot((heads, rows, rows))),
            (context, by_slot((rows, col_dev))),
        ]
        + [(piece, ANY) for piece in attn_pieces],
        [
            ((groups, rows, wide), BF, by_slot((rows, wide))),
            ((groups, wide), F32, whole((groups, wide))),
        ]
        + grad_outs(mats * col_dev),
        [
            pltpu.VMEM(weight, BF),
            pltpu.VMEM((width, rows), BF),
            pltpu.VMEM((width, rows), BF),
            pltpu.VMEM((width, mats * col_dev), BF),
            sems,
        ],
        base * groups * (wide + 2 * col_dev) + 8 * groups * heads * rows * rows * HEAD_DIM * 4,
        24 * MIB,
        56,
    )
    up_sum = moves.reduce(up_grads)
    (input_grad,) = call(
        functools.partial(input_grad_kernel, count),
        "input_grad",
        groups,
        place,
        [(dfirst, whole(full)), (dqkv, by_slot((rows, wide)))]
        + [(piece, ANY) for piece in attn_pieces],
        [(full, BF, whole(full))],
        [pltpu.VMEM(weight, BF), pltpu.VMEM(full, F32), sems],
        base * groups * wide,
        12 * MIB,
        40,
    )
    attn_sum = moves.reduce(attn_grads)
    early = jnp.concatenate([dbias_hidden.reshape(-1), sums_two.reshape(-1)])
    late = jnp.concatenate(
        [
            dbias_qkv[:, 0:col_dev].reshape(-1),
            dbias_qkv[:, 2 * col_dev :].reshape(-1),
            sums_one.reshape(-1),
        ]
    )
    early = jnp.sum(lax.all_gather(early, ("dp", "tp"), axis=0, tiled=False), axis=0)
    late = jnp.sum(lax.all_gather(late, ("dp", "tp"), axis=0, tiled=False), axis=0)
    bias_grads = late[0 : 2 * width]
    dout_bias, dgain_one, dshift_one = (late[k * width : (k + 1) * width] for k in (2, 3, 4))
    dtwo_bias, dgain_two, dshift_two = (
        early[ffn + k * width : ffn + (k + 1) * width] for k in (0, 1, 2)
    )
    vec_grad = jnp.concatenate(
        [
            bias_grads,
            early[0:ffn],
            dout_bias,
            dtwo_bias,
            dgain_one,
            dshift_one,
            dgain_two,
            dshift_two,
        ]
    )
    attn_grad = jnp.stack([attn_sum[:, k * col_dev : (k + 1) * col_dev] for k in range(mats)])
    mlp_grad = jnp.stack([up_sum, down_sum])
    attn_step = adam_update(
        attn_master, attn_first, attn_second, attn_grad, MATRIX_RATE, MATRIX_DECAY
    )
    mlp_step = adam_update(mlp_master, mlp_first, mlp_second, mlp_grad, MATRIX_RATE, MATRIX_DECAY)
    vec_step = adam_update(vec_master, vec_first, vec_second, vec_grad, VECTOR_RATE, 0.0)
    return (layer_out, pooled, input_grad, *attn_step, *mlp_step, *vec_step)


def solution(mesh):
    in_specs = (
        P(("dp", "tp"), None),
        P(("dp", "tp"), None),
        P(("dp", "tp")),
        P(None, "dp", "tp"),
        P(None, "dp", "tp"),
        P(None, "dp", "tp"),
        P(None, "dp", "tp"),
        P(None, "dp", "tp"),
        P(None, "dp", "tp"),
        P(),
        P(),
        P(),
    )
    out_specs = (
        P(("dp", "tp"), None),
        P(("dp", "tp"), None),
        P(("dp", "tp"), None),
        P(None, "dp", "tp"),
        P(None, "dp", "tp"),
        P(None, "dp", "tp"),
        P(None, "dp", "tp"),
        P(None, "dp", "tp"),
        P(None, "dp", "tp"),
        P(None, "dp", "tp"),
        P(None, "dp", "tp"),
        P(),
        P(),
        P(),
        P(),
    )
    return jax.shard_map(
        on_device, mesh=mesh, in_specs=in_specs, out_specs=out_specs, check_vma=False
    )
```

```python
import functools

import jax
import jax.numpy as jnp
from jax import lax
from jax.experimental import pallas as pl
from jax.experimental.pallas import tpu as pltpu
from jax.sharding import PartitionSpec as P

HEAD_DIM = 64
SEQ = 512
SEGS = 128
STEP = 10


NORM_EPS = 1e-12
BETA_ONE = 0.9
BETA_TWO = 0.999
ADAM_EPS = 1e-06
MATRIX_RATE = 0.1
VECTOR_RATE = 0.3
MATRIX_DECAY = 0.01
SCALE = HEAD_DIM ** (-0.5)
HALF_ROOT = 0.7071067811865476
PDF_SCALE = 0.3989422804014327
NT = (((1,), (1,)), ((), ()))
BF = jnp.bfloat16
F32 = jnp.float32
MIB = 1 << 20
ROW_CHUNK = 128
BIAS_OUT, BIAS_TWO, GAIN_ONE, SHIFT_ONE, GAIN_TWO, SHIFT_TWO = range(-6, 0)


def dot(left, right):
    return jnp.dot(left, right, preferred_element_type=F32)


def dot_nt(left, right):
    return lax.dot_general(left, right, NT, preferred_element_type=F32)


def adam_update(weight, moment_one, moment_two, gradient, step_rate, decay_rate):
    first_new = BETA_ONE * moment_one + (1.0 - BETA_ONE) * gradient
    second_new = BETA_TWO * moment_two + (1.0 - BETA_TWO) * gradient * gradient
    fix_one = 1.0 - BETA_ONE**STEP
    fix_two = 1.0 - BETA_TWO**STEP
    direction = first_new / fix_one / (jnp.sqrt(second_new / fix_two) + ADAM_EPS)
    weight_new = weight - step_rate * (direction + decay_rate * weight)
    return (first_new, second_new, weight_new, weight_new.astype(BF))


def split_blocks(pieces):
    blocks = []
    for piece in pieces:
        blocks += [piece.at[k] for k in range(piece.shape[0])] if len(piece.shape) == 4 else [piece]
    return blocks


def weight_copies(form, first, place, pieces, held, sems):
    groups, count = held.shape[0], held.shape[1]
    if form == "one":
        return [
            pltpu.make_async_copy(pieces[0].at[k], held.at[k, 0], sems.at[k]) for k in range(groups)
        ]
    near = [
        pltpu.make_async_copy(piece.at[first], held.at[0, place[j]], sems.at[j])
        for j, piece in enumerate(pieces[:count])
    ]
    far = [
        pltpu.make_async_copy(piece, held.at[pl.ds(1, groups - 1), place[j]], sems.at[count + j])
        for j, piece in enumerate(split_blocks(pieces[count:]))
    ]
    return near + far


def bring_weight(copies, step):
    @pl.when(step == 0)
    def _():
        for copy in copies:
            copy.start()
        for copy in copies:
            copy.wait()


def keep_weight(held, out, sem, step, last, start, slots):
    copy = pltpu.make_async_copy(
        held.at[pl.ds(start, slots)], out.at[pl.ds(start, slots)], sem
    )
    pl.when(step == 0)(copy.start)
    pl.when(step == last)(copy.wait)


def flat(value):
    return value.reshape(value.shape[0] * value.shape[1], value.shape[2])


def rounded(vec_ref, row):
    at = row % vec_ref.shape[0]
    return vec_ref[at : at + 1, :].astype(BF).astype(F32)


def own_part(row, own, size):
    out = row[:, 0:size]
    for k in range(1, row.shape[1] // size):
        out = jnp.where(own == k, row[:, k * size : (k + 1) * size], out)
    return out


def write_pieces(place, grad, outs):
    j = 0
    for out in outs:
        for k in range(out.shape[0]):
            out[k, 0] = grad[place[j]]
            j += 1


def normed_rows(value):
    centred = value - jnp.mean(value, axis=-1, keepdims=True)
    inverse = lax.rsqrt(jnp.mean(centred * centred, axis=-1, keepdims=True) + NORM_EPS)
    return centred * inverse, inverse


def norm_back(cot, normed, inverse, gain):
    scaled = cot * gain
    mean_one = jnp.mean(scaled, axis=-1, keepdims=True)
    mean_two = jnp.mean(scaled * normed, axis=-1, keepdims=True)
    return (scaled - mean_one - normed * mean_two) * inverse


def column_sum(value):
    return jnp.sum(value, axis=0, keepdims=True)


def attn_forward_kernel(form, n, start, groups, place, x_ref, vec_ref, *refs):
    pieces = refs[:n]
    if start:
        total_in, refs = refs[n], refs[n + 5 :]
    else:
        total_in, refs = None, refs[n:]
    qkv_ref, probs_ref, ctx_ref, kept_ref = refs[:4]
    held, total, sems, kept_sem = refs[-4:]
    outs = refs[4:-4]
    step = pl.program_id(0)
    steps = pl.num_programs(0)
    slot = step + start
    own = place[place.shape[0] - 1]
    width = qkv_ref.shape[2]
    part = width // 3
    slots = groups - start if len(outs) == 2 else 1

    bring_weight(weight_copies(form, 0, place, pieces, held, sems), step)
    keep_weight(held, kept_ref, kept_sem, step, steps - 1, start, slots)
    bias_q = own_part(rounded(vec_ref, 0), own ^ slot, part)
    bias_v = own_part(rounded(vec_ref, 1), own ^ slot, part)
    bias = jnp.concatenate([bias_q, jnp.zeros_like(bias_q), bias_v], axis=1)
    projected = dot(x_ref[...], flat(held[slot, :, :, 0:width])) + bias
    low = projected.astype(BF)
    qkv_ref[0] = low
    parts = []
    for h in range(part // HEAD_DIM):
        lo = h * HEAD_DIM
        q = low[:, lo : lo + HEAD_DIM] * BF(SCALE)
        k = low[:, part + lo : part + lo + HEAD_DIM]
        v = low[:, 2 * part + lo : 2 * part + lo + HEAD_DIM]
        scores = dot_nt(q, k)
        expanded = jnp.exp(scores - jnp.max(scores, axis=-1, keepdims=True))
        inverse = 1.0 / jnp.sum(expanded, axis=-1, keepdims=True)
        probs = (expanded * inverse).astype(BF)
        probs_ref[0, h] = probs
        parts.append(dot(probs, v))
    context = jnp.concatenate(parts, axis=1).astype(BF)
    ctx_ref[0] = context
    added = dot_nt(context, flat(held[slot, :, :, width:]))

    @pl.when(step == 0)
    def _():
        if start:
            total[...] = total_in[...] + added
        else:
            total[...] = x_ref[...].astype(F32) + rounded(vec_ref, BIAS_OUT) + added

    @pl.when(step > 0)
    def _():
        total[...] += added

    @pl.when(step == steps - 1)
    def _():
        if start + slots == groups:
            outs[0][...], outs[1][...] = normed_rows(total[...])
        else:
            outs[0][...] = total[...]


def middle_rows(norm_ref, vec_ref):
    return norm_ref[...] * rounded(vec_ref, GAIN_ONE) + rounded(vec_ref, SHIFT_ONE)


def mlp_up_kernel(form, n, start, slots, place, norm_ref, vec_ref, *refs):
    pieces = refs[:n]
    hid_ref, slope_ref, kept_ref = refs[n + 3 : n + 6] if start else refs[n : n + 3]
    held, low_ref, sems, kept_sem = refs[-4:]
    step = pl.program_id(0)
    slot = step + start
    own = place[place.shape[0] - 1]

    bring_weight(weight_copies(form, 1, place, pieces, held, sems), step)
    keep_weight(held, kept_ref, kept_sem, step, slots - 1, start, slots)

    @pl.when(step == 0)
    def _():
        low_ref[...] = middle_rows(norm_ref, vec_ref).astype(BF)

    bias = vec_ref[pl.ds(2 + (own ^ slot), 1), :].astype(BF).astype(F32)

    def rows(i, carry):
        at = pl.ds(pl.multiple_of(i * ROW_CHUNK, ROW_CHUNK), ROW_CHUNK)
        u = dot(low_ref[at, :], flat(held[slot])) + bias
        cdf = 0.5 + 0.5 * lax.erf(u * HALF_ROOT)
        hid_ref[0, at, :] = (u * cdf).astype(BF)
        slope_ref[0, at, :] = (cdf + u * (jnp.exp(u * u * -0.5) * PDF_SCALE)).astype(BF)
        return carry

    lax.fori_loop(0, low_ref.shape[0] // ROW_CHUNK, rows, 0)


def mlp_down_kernel(form, n, outs, place, norm_ref, vec_ref, og_ref, ids_ref, hid_ref, *refs):
    pieces = refs[:n]
    out_ref, pool_ref, dres_ref, dlow_ref, sums_ref, kept_ref = refs[n : n + 6]
    grads = refs[n + 6 : n + 6 + outs]
    held, total, dlow_t, grad_low, sems, kept_sem = refs[n + 6 + outs :]
    step = pl.program_id(0)
    groups = held.shape[0]

    bring_weight(weight_copies(form, 2, place, pieces, held, sems), step)
    keep_weight(held, kept_ref, kept_sem, step, 2 * groups - 1, 0, groups)

    @pl.when(step == 0)
    def _():
        total[...] = middle_rows(norm_ref, vec_ref) + rounded(vec_ref, BIAS_TWO)

    @pl.when(step < groups)
    def _():
        total[...] += dot_nt(hid_ref[0], flat(held[step]))

    @pl.when(step == groups - 1)
    def _():
        normed, inverse = normed_rows(total[...])
        gain = rounded(vec_ref, GAIN_TWO)
        final = normed * gain + rounded(vec_ref, SHIFT_TWO)
        high = final.astype(BF)
        out_ref[...] = high
        docs = pool_ref.shape[0] // SEGS
        for d in range(docs):
            slots = lax.broadcasted_iota(jnp.int32, (SEGS, SEQ), 0)
            onehot = jnp.where(slots == ids_ref[d : d + 1, :], 1.0, 0.0)
            counts = jnp.sum(onehot, axis=1, keepdims=True)
            marks = onehot.astype(BF)
            at = slice(d * SEQ, (d + 1) * SEQ)
            rest = (final[at] - high[at].astype(F32)).astype(BF)
            sums = dot(marks, high[at]) + dot(marks, rest)
            pool_ref[d * SEGS : (d + 1) * SEGS, :] = sums / jnp.maximum(counts, 1.0)
        cot = og_ref[...].astype(F32)
        dres = norm_back(cot, normed, inverse, gain)
        dres_ref[...] = dres
        low = dres.astype(BF)
        dlow_ref[...] = low
        dlow_t[...] = low.T
        sums_ref[0:1, :] = column_sum(dres)
        sums_ref[1:2, :] = column_sum(cot * normed)
        sums_ref[2:3, :] = column_sum(cot)

    @pl.when(step >= groups)
    def _():
        grad_low[...] = dot(dlow_t[...], hid_ref[0]).astype(BF).reshape(grad_low.shape)
        write_pieces(place, grad_low, grads)


def mlp_back_kernel(outs, place, norm_ref, vec_ref, dlow_ref, slope_ref, down_ref, *refs):
    dpre_ref, dbias_ref = refs[:2]
    grads = refs[2 : 2 + outs]
    low_t, grad_low = refs[2 + outs :]
    slot = pl.program_id(0)
    own = place[place.shape[0] - 1]

    @pl.when(slot == 0)
    def _():
        low_t[...] = middle_rows(norm_ref, vec_ref).astype(BF).T

    dpre = (dot(dlow_ref[...], flat(down_ref[0])) * slope_ref[0].astype(F32)).astype(BF)
    dpre_ref[0] = dpre
    dbias_ref[pl.ds(own ^ slot, 1), :] = column_sum(dpre.astype(F32))
    grad_low[...] = dot(low_t[...], dpre).astype(BF).reshape(grad_low.shape)
    write_pieces(place, grad_low, grads)


def norm_back_kernel(place, norm_ref, inv_ref, vec_ref, dres_ref, dpre_ref, up_ref, *refs):
    dfirst_ref, dout_ref, sums_ref, total = refs
    slot = pl.program_id(0)
    added = dot_nt(dpre_ref[0], flat(up_ref[0]))

    @pl.when(slot == 0)
    def _():
        total[...] = dres_ref[...] + added

    @pl.when(slot > 0)
    def _():
        total[...] += added

    @pl.when(slot == pl.num_programs(0) - 1)
    def _():
        cot = total[...]
        normed = norm_ref[...]
        dfirst = norm_back(cot, normed, inv_ref[...], rounded(vec_ref, GAIN_ONE))
        dfirst_ref[...] = dfirst
        dout_ref[...] = dfirst.astype(BF)
        sums_ref[0:1, :] = column_sum(dfirst)
        sums_ref[1:2, :] = column_sum(cot * normed)
        sums_ref[2:3, :] = column_sum(cot)


def attn_back_kernel(outs, groups, start, place, x_ref, dout_ref, qkv_ref, probs_ref, ctx_ref, weight_ref, *refs):
    dqkv_ref, dbias_ref = refs[:2]
    grads = refs[2 : 2 + outs]
    x_t, dout_t, grad_low = refs[2 + outs :]
    step = pl.program_id(0)
    slot = (step + start) % groups
    own = place[place.shape[0] - 1]
    width = qkv_ref.shape[2]
    part = width // 3
    block = grad_low.shape[0:2]

    @pl.when(step == 0)
    def _():
        x_t[...] = x_ref[...].T
        dout_t[...] = dout_ref[...].T
        dbias_ref[...] = jnp.zeros_like(dbias_ref)

    context = ctx_ref[0]
    grad_out = dot(dout_t[...], context).astype(BF)
    grad_low[:, :, width:] = grad_out.reshape(block + (part,))
    dctx = dot(dout_ref[...], flat(weight_ref[0, :, :, width:])).astype(BF)
    dctx_t = dctx.T
    row_dots = dctx.astype(F32) * context.astype(F32)
    q_t = qkv_ref[0, :, 0:part].T
    dq, dk_t, dv_t = [], [], []
    for h in range(part // HEAD_DIM):
        at = slice(h * HEAD_DIM, (h + 1) * HEAD_DIM)
        k = qkv_ref[0, :, part + h * HEAD_DIM : part + (h + 1) * HEAD_DIM]
        v = qkv_ref[0, :, 2 * part + h * HEAD_DIM : 2 * part + (h + 1) * HEAD_DIM]
        probs = probs_ref[0, h]
        row_dot = jnp.sum(row_dots[:, at], axis=-1, keepdims=True)
        dprobs = dot_nt(dctx[:, at], v)
        dscores = (probs.astype(F32) * (dprobs - row_dot)).astype(BF)
        dv_t.append(dot(dctx_t[at], probs))
        dq.append(dot(dscores, k) * SCALE)
        dk_t.append(dot(q_t[at], dscores) * SCALE)
    dqkv = jnp.concatenate(
        [
            jnp.concatenate(dq, axis=1).astype(BF),
            jnp.concatenate(dk_t, axis=0).astype(BF).T,
            jnp.concatenate(dv_t, axis=0).astype(BF).T,
        ],
        axis=1,
    )
    dqkv_ref[0] = dqkv
    dbias = column_sum(dqkv.astype(F32))
    for z in range(dbias_ref.shape[1] // part):
        cols = slice(z * part, (z + 1) * part)
        mine = own ^ slot == z
        dbias_ref[0:1, cols] += jnp.where(mine, dbias[:, 0:part], 0.0)
        dbias_ref[1:2, cols] += jnp.where(mine, dbias[:, 2 * part :], 0.0)
    grad_low[:, :, 0:width] = dot(x_t[...], dqkv).astype(BF).reshape(block + (width,))
    write_pieces(place, grad_low, grads)


def input_grad_kernel(place, dfirst_ref, dqkv_ref, weight_ref, out_ref, total):
    slot = pl.program_id(0)
    width = dqkv_ref.shape[2]
    added = dot_nt(dqkv_ref[0], flat(weight_ref[0, :, :, 0:width]))

    @pl.when(slot == 0)
    def _():
        total[...] = dfirst_ref[...] + added

    @pl.when(slot > 0)
    def _():
        total[...] += added

    @pl.when(slot == pl.num_programs(0) - 1)
    def _():
        out_ref[...] = total[...].astype(out_ref.dtype)


def whole(shape):
    return pl.BlockSpec(shape, lambda i, place: (0,) * len(shape))


def by_slot(shape, index=lambda i: i):
    return pl.BlockSpec((1,) + shape, lambda i, place: (index(i),) + (0,) * len(shape))


def by_piece(shape, index=lambda i, place: i):
    return pl.BlockSpec(
        (shape[0], 1) + shape[2:], lambda i, place: (0, index(i, place)) + (0,) * len(shape[2:])
    )


ANY = pl.BlockSpec(memory_space=pltpu.HBM)
FREE = pl.BlockSpec(memory_space=pl.ANY)
VMEM_LIMIT = 28 * MIB


def pinned(value, spec, space=None):
    if space == "vmem":
        return pltpu.with_memory_space_constraint(value, pltpu.VMEM)
    if space == "hbm":
        return pltpu.with_memory_space_constraint(value, pltpu.HBM)
    return value


def placed(shape, dtype, space=None):
    if space == "vmem":
        return pltpu.VMEM(shape, dtype)
    if space == "hbm":
        return pltpu.HBM(shape, dtype)
    return jax.ShapeDtypeStruct(shape, dtype)


def call(kernel, name, grid, place, inputs, outputs, scratch, flops, moved, aliases=None):
    return pl.pallas_call(
        kernel,
        name=name,
        out_shape=[placed(out[0], out[1], *out[3:]) for out in outputs],
        grid_spec=pltpu.PrefetchScalarGridSpec(
            num_scalar_prefetch=1,
            grid=(grid,),
            in_specs=[given[1] for given in inputs],
            out_specs=[out[2] for out in outputs],
            scratch_shapes=scratch,
        ),
        compiler_params=pltpu.CompilerParams(
            dimension_semantics=("arbitrary",), vmem_limit_bytes=VMEM_LIMIT
        ),
        input_output_aliases=aliases or {},
        cost_estimate=pl.CostEstimate(flops=1000, bytes_accessed=1000, transcendentals=0),
    )(place, *[pinned(*given) for given in inputs])


def after(value, *deps):
    deps = [dep for dep in deps if dep is not None]
    return lax.optimization_barrier((value, *deps))[0] if deps else value


def after_all(values, *deps):
    return list(lax.optimization_barrier((*values, *deps)))[: len(values)]


def xor_pairs(count, mask):
    return [(i, i ^ mask) for i in range(count)]


class PlaneTransfers:
    forms = ("pieces", "pieces", "pieces")

    def __init__(self, tp_count):
        self.count = 8
        self.groups = tp_count
        self.first = [(i, i ^ (4 if i & 1 else 2)) for i in range(8)]
        self.second = [(i, i ^ (2 if i & 1 else 4)) for i in range(8)]
        self.cores = xor_pairs(8, 1)
        me = lax.axis_index("dp")
        one = jnp.where(me % 2 == 1, 4, 2)
        two = 6 - one
        self.place = jnp.stack(
            [
                me,
                me ^ one,
                me ^ two,
                me ^ 6,
                me ^ 1,
                me ^ 1 ^ two,
                me ^ 1 ^ one,
                me ^ 7,
                lax.axis_index("tp"),
            ]
        ).astype(jnp.int32)
        self.out_counts = (4, 2, 2)

    def shifted(self, shard, mask):
        return lax.ppermute(shard, "tp", xor_pairs(self.groups, mask))

    def across(self, shard):
        return [self.shifted(shard, k) for k in range(1, self.groups)]

    def both(self, mine):
        return mine + [lax.ppermute(piece, "dp", self.cores) for piece in mine]

    def first_chip(self, shards):
        return lax.ppermute(shards, "dp", self.first)

    def second_chip(self, shards):
        return lax.ppermute(shards, "dp", self.second)

    def total(self, vec, deps):
        vec = vec + lax.ppermute(vec, "dp", self.cores)
        vec = after(vec, deps[0])
        x, y, xy = (lax.ppermute(vec, "dp", xor_pairs(self.count, mask)) for mask in (2, 4, 6))
        vec = after((vec + x) + (y + xy), deps[1])
        mask = 1
        while mask < self.groups:
            vec = vec + lax.ppermute(vec, "tp", xor_pairs(self.groups, mask))
            mask *= 2
        return vec


    def swap_far(self, grads):
        return lax.ppermute(grads[2], "dp", self.cores)

    def swap_near(self, grads):
        return lax.ppermute(grads[1], "dp", self.cores)

    def pair_ready(self, grads, far):
        return (grads[0][2:4].astype(F32) + far.astype(F32)).astype(BF)

    def pair(self, sent):
        return lax.ppermute(sent, "dp", self.second)

    def near_ready(self, grads, other, pair):
        one = grads[0][1].astype(F32) + other[1].astype(F32) + pair[1].astype(F32)
        return one.astype(BF)

    def near(self, sent):
        return lax.ppermute(sent, "dp", self.first)

    def block(self, grads, other, pair, near):
        own = grads[0][0].astype(F32) + other[0].astype(F32)
        return own + pair[0].astype(F32) + near.astype(F32)

    def scatter_sum(self, block):
        out = lax.psum_scatter(block.astype(BF), "tp", scatter_dimension=0, tiled=True)
        return out[0].astype(F32)

    def across_parts(self, block):
        return [self.shifted(block[k].astype(BF), k) for k in range(1, self.groups)]

    def across_total(self, block, parts):
        total = block[0]
        for part in parts:
            total = total + part.astype(F32)
        return total


class PlainTransfers:
    forms = ("one", "one", "one")

    def __init__(self, dp_count, tp_count):
        self.dp = dp_count
        self.tp = tp_count
        self.count = 1
        self.groups = tp_count
        self.place = jnp.zeros((2,), jnp.int32)
        self.out_counts = (1,)

    def one(self, shards):
        rows, columns = shards.shape
        out = lax.all_gather(shards, ("dp", "tp"), axis=0, tiled=False)
        out = out.reshape(self.dp, self.tp, rows, columns).transpose(1, 0, 2, 3)
        return [out.reshape(self.tp, self.dp * rows, columns)]

    def gather(self, attn, mlp):
        return self.one(attn), self.one(mlp[0]), self.one(mlp[1])

    def total(self, vec, deps):
        return lax.psum(vec, ("dp", "tp"))

    def sum(self, grads):
        _, groups, rows, columns = grads[0].shape
        parts = grads[0].reshape(groups, self.dp, rows // self.dp, columns).transpose(1, 0, 2, 3)
        parts = parts.reshape(self.dp * groups, rows // self.dp, columns)
        out = lax.psum_scatter(parts, ("dp", "tp"), scatter_dimension=0, tiled=True)
        return out[0].astype(F32)


def on_device(
    tokens,
    out_grad,
    segment_ids,
    attn_master,
    attn_first,
    attn_second,
    mlp_master,
    mlp_first,
    mlp_second,
    vec_master,
    vec_first,
    vec_second,
):
    rows, width = tokens.shape
    dp_count = lax.axis_size("dp")
    groups = lax.axis_size("tp")
    mats, row_dev, col_dev = attn_master.shape
    hidden = mlp_master.shape[2]
    docs = rows // SEQ
    heads = col_dev // HEAD_DIM
    wide = 3 * col_dev
    cols = mats * col_dev
    plane = dp_count == 8 and groups & (groups - 1) == 0 and row_dev % 16 == 0
    moves = PlaneTransfers(groups) if plane else PlainTransfers(dp_count, groups)
    place = moves.place
    count = moves.count
    outs = len(moves.out_counts)
    block = width // count

    attn_low = jnp.concatenate([attn_master[k] for k in range(mats)], axis=1).astype(BF)
    vecs = vec_master.reshape(-1, width)
    mlp_low = mlp_master.astype(BF)
    forms = moves.forms

    full = (rows, width)
    flat_t = (width, rows)
    row_vec = (rows, 1)
    weight = (groups, count, block, cols)
    hid_weight = (groups, count, block, hidden)
    slot_weight = by_slot((count, block, cols))
    slot_hid_weight = by_slot((count, block, hidden))
    slot_hid = by_slot((rows, hidden))
    slot_wide = by_slot((rows, wide))
    base = 2 * rows * width
    dma = pltpu.SemaphoreType.DMA
    vec_in = (vecs, whole(vecs.shape))

    def arriving(pieces):
        return [(piece, ANY, "hbm") for piece in pieces]

    def grad_outs(columns, base_step=0):
        def index(i, place):
            return jnp.maximum(i - base_step, 0)

        return [
            ((k, groups, block, columns), BF, by_piece((k, groups, block, columns), index), "hbm")
            for k in moves.out_counts
        ]

    def attn_forward(start, slots, given, pieces, so_far=()):
        def shifted(shape):
            return by_slot(shape, lambda i: i + start)

        parts = [
            ((groups, rows, wide), BF, shifted((rows, wide)), "hbm"),
            ((groups, heads, rows, rows), BF, shifted((heads, rows, rows)), "hbm"),
            ((groups, rows, col_dev), BF, shifted((rows, col_dev)), "hbm"),
            (weight, BF, ANY, "hbm"),
        ]
        if start + slots == groups:
            last = [(full, F32, whole(full), "vmem"), (row_vec, F32, whole(row_vec), "vmem")]
        else:
            last = [(full, F32, whole(full), "vmem")]
        inputs = [(given, whole(full)), vec_in] + arriving(pieces)
        base_in = len(inputs) + 1
        aliases = {}
        if start:
            *so_far, total = so_far
            inputs.append((total, whole(full), "vmem"))
            inputs += [(part, ANY, "hbm") for part in so_far]
            aliases = {base_in + 1 + k: k for k in range(4)}
        return call(
            functools.partial(attn_forward_kernel, forms[0], len(pieces), start, groups),
            "attn_forward",
            slots,
            place,
            inputs,
            parts + last,
            [pltpu.VMEM(weight, BF), pltpu.VMEM(full, F32), dma((max(2 * count, groups),)), dma],
            (base * (wide + col_dev) + 16 * heads * rows * rows * HEAD_DIM) * slots,
            4 * slots * MIB,
            aliases,
        )

    def mlp_up(start, slots, given, pieces, so_far=()):
        parts = [
            (
                (groups, rows, hidden),
                BF,
                by_slot((rows, hidden), lambda i: i + start),
                "hbm",
            )
        ] * 2 + [(hid_weight, BF, ANY, "hbm")]
        inputs = [(given, whole(full), "vmem"), vec_in] + arriving(pieces)
        aliases = {}
        if start:
            aliases = {len(inputs) + 1 + k: k for k in range(3)}
            inputs += [(part, ANY, "hbm") for part in so_far]
        return call(
            functools.partial(mlp_up_kernel, forms[1], len(pieces), start, slots),
            "mlp_up",
            slots,
            place,
            inputs,
            parts,
            [pltpu.VMEM(hid_weight, BF), pltpu.VMEM(full, BF), dma((max(2 * count, groups),)), dma],
            base * slots * hidden * 3,
            4 * slots * MIB,
            aliases,
        )

    if plane:
        own = jnp.concatenate([attn_low[None], mlp_low])
        own_one, own_two = moves.first_chip(own), moves.second_chip(own)
        own_one, own_two, *attn_far = after_all((own_one, own_two, *moves.across(attn_low)))

        attn_far = jnp.stack(attn_far)
        attn_one = moves.first_chip(attn_far)
        own_three = moves.second_chip(own_one)
        up_far = moves.across(after(mlp_low[0], attn_far))
        attn_one, own_three, *up_far = after_all((attn_one, own_three, *up_far))

        attn_pair = moves.second_chip(jnp.stack([attn_far, attn_one]))
        up_far = jnp.stack(up_far)
        up_one = moves.first_chip(up_far)
        down_far = moves.across(after(mlp_low[1], up_far))
        attn_pair, up_one, *down_far = after_all((attn_pair, up_one, *down_far))

        up_sent = jnp.stack([up_far, up_one])
        up_pair = moves.second_chip(up_sent)
        down_far = jnp.stack(down_far)
        down_one = moves.first_chip(down_far)
        own_pieces = moves.both([own, own_one, own_two, own_three])
        attn_pieces = own_pieces + moves.both(after_all([attn_far, attn_one, attn_pair], up_sent))
        qkv, probs, context, attn_kept, norm_one, inv_one = attn_forward(
            0, groups, after(tokens, down_far), attn_pieces
        )
        norm_one, up_far, up_one, up_pair, down_one = after_all(
            (norm_one, up_far, up_one, up_pair, down_one)
        )

        down_sent = jnp.stack([down_far, down_one])
        down_pair = moves.second_chip(down_sent)
        up_pieces = own_pieces + moves.both([up_far, up_one, up_pair])
        hid, slope, up_kept = mlp_up(0, groups, after(norm_one, down_sent), up_pieces)
        hid, *down_pieces = after_all((hid, down_far, down_one, down_pair))
        down_pieces = own_pieces + moves.both(down_pieces)
    else:
        attn_pieces, up_pieces, down_pieces = moves.gather(attn_low, mlp_low)
        qkv, probs, context, attn_kept, norm_one, inv_one = attn_forward(
            0, groups, tokens, attn_pieces
        )
        hid, slope, up_kept = mlp_up(0, groups, norm_one, up_pieces)
    down_in = arriving(down_pieces)
    layer_out, pooled, dres, dres_low, sums_two, down_kept, *down_grads = call(
        functools.partial(mlp_down_kernel, forms[2], len(down_in), outs),
        "mlp_down",
        2 * groups,
        place,
        [
            (norm_one, whole(full), "vmem"),
            vec_in,
            (out_grad, whole(full)),
            (segment_ids.reshape(docs, SEQ), whole((docs, SEQ))),
            (hid, by_slot((rows, hidden), lambda i: i % groups), "hbm"),
        ]
        + down_in,
        [
            (full, BF, whole(full)),
            ((docs * SEGS, width), F32, whole((docs * SEGS, width))),
            (full, F32, whole(full), "vmem"),
            (full, BF, whole(full), "vmem"),
            ((3, width), F32, whole((3, width))),
            (hid_weight, BF, ANY, "hbm"),
        ]
        + grad_outs(hidden, groups),
        [
            pltpu.VMEM(hid_weight, BF),
            pltpu.VMEM(full, F32),
            pltpu.VMEM(flat_t, BF),
            pltpu.VMEM((count, block, hidden), BF),
            dma((max(2 * count, groups),)),
            dma,
        ],
        base * groups * hidden * 2,
        16 * MIB,
    )
    down_far = moves.swap_far(down_grads) if plane else None
    down_other = moves.swap_near(down_grads) if plane else None
    dpre, dbias_hidden, *up_grads = call(
        functools.partial(mlp_back_kernel, outs),
        "mlp_back",
        groups,
        place,
        [
            (norm_one, whole(full), "vmem"),
            vec_in,
            (dres_low, whole(full), "vmem"),
            (slope, slot_hid, "hbm"),
            (down_kept, slot_hid_weight, "hbm"),
        ],
        [
            ((groups, rows, hidden), BF, slot_hid, "vmem"),
            ((groups, hidden), F32, whole((groups, hidden))),
        ]
        + grad_outs(hidden),
        [pltpu.VMEM(flat_t, BF), pltpu.VMEM((count, block, hidden), BF)],
        base * groups * hidden * 2,
        24 * MIB,
    )
    if plane:
        down_sent = moves.pair_ready(down_grads, down_far)
        dres = after(dres, down_sent)
        down_pair = moves.pair(down_sent)
        up_far = moves.swap_far(up_grads)
        up_other = moves.swap_near(up_grads)
    dfirst, dout, sums_one = call(
        norm_back_kernel,
        "norm_back",
        groups,
        place,
        [
            (norm_one, whole(full), "vmem"),
            (inv_one, whole(row_vec), "vmem"),
            vec_in,
            (dres, whole(full), "vmem"),
            (dpre, slot_hid, "vmem"),
            (up_kept, slot_hid_weight, "hbm"),
        ],
        [
            (full, F32, whole(full), "vmem"),
            (full, BF, whole(full), "vmem"),
            ((3, width), F32, whole((3, width))),
        ],
        [pltpu.VMEM(full, F32)],
        base * groups * hidden,
        16 * MIB,
    )
    def attn_back(start, slots, dout):
        def shifted(shape):
            return by_slot(shape, lambda i: (i + start) % groups)

        outputs = [
            ((slots, rows, wide), BF, by_slot((rows, wide)), "hbm"),
            ((2, width), F32, whole((2, width))),
        ]
        for k in moves.out_counts:
            shape = (k, slots, block, cols)
            outputs.append((shape, BF, by_piece(shape), "hbm"))
        return call(
            functools.partial(attn_back_kernel, outs, groups, start),
            "attn_back",
            slots,
            place,
            [
                (tokens, whole(full)),
                (dout, whole(full), "vmem"),
                (qkv, shifted((rows, wide)), "hbm"),
                (probs, shifted((heads, rows, rows)), "hbm"),
                (context, shifted((rows, col_dev)), "hbm"),
                (attn_kept, shifted((count, block, cols)), "hbm"),
            ],
            outputs,
            [pltpu.VMEM(flat_t, BF), pltpu.VMEM(flat_t, BF), pltpu.VMEM((count, block, cols), BF)],
            (base * (wide + 2 * col_dev) + 8 * heads * rows * rows * HEAD_DIM * 4) * slots,
            6 * slots * MIB,
        )

    if plane:
        up_sent = moves.pair_ready(up_grads, up_far)
        up_pair = moves.pair(up_sent)
        half = groups // 2
        dqkv_a, dbias_a, *a_grads = attn_back(1, half, after(dout, up_sent))
        a_far = moves.swap_far(a_grads)
        a_other = moves.swap_near(a_grads)
        down_near_sent = moves.near_ready(down_grads, down_other, after(down_pair, dbias_a))
        down_near = moves.near(down_near_sent)
        dqkv_b, dbias_b, *b_grads = attn_back(1 + half, groups - half, after(dout, down_near_sent))
        a_far, down_near, up_pair, dbias_b, *b_grads = after_all(
            (a_far, down_near, up_pair, dbias_b, *b_grads)
        )
        dbias_qv = dbias_a + dbias_b
        b_far = moves.swap_far(b_grads)
        b_other = moves.swap_near(b_grads)
        a_sent = moves.pair_ready(a_grads, a_far)
        a_pair = moves.pair(a_sent)
        up_near_sent = moves.near_ready(up_grads, up_other, after(up_pair, a_sent))
        up_near = moves.near(up_near_sent)
        dfirst = after(dfirst, a_sent, up_near_sent)
    else:
        dqkv_a, dbias_qv, *a_grads = attn_back(0, groups, dout)

    def input_part(given, part, start, space):
        slots = part.shape[0]
        out = (full, F32, whole(full), space) if space else (full, BF, whole(full))
        return call(
            input_grad_kernel,
            "input_grad",
            slots,
            place,
            [
                (given, whole(full), "vmem"),
                (part, slot_wide, "hbm"),
                (attn_kept, by_slot((count, block, cols), lambda i: (i + start) % groups), "hbm"),
            ],
            [out],
            [pltpu.VMEM(full, F32)],
            base * slots * wide,
            3 * slots * MIB,
        )[0]

    def vec_grads(dbias_qv):
        return jnp.concatenate(
            [
                dbias_qv,
                dbias_hidden,
                sums_one[0:1],
                sums_two[0:1],
                sums_one[1:3],
                sums_two[1:3],
            ],
            axis=0,
        )

    if plane:
        input_grad = input_part(dfirst, dqkv_a, 1, "vmem")
        input_grad, b_far, b_other = after_all((input_grad, b_far, b_other))
        down_block = moves.block(down_grads, down_other, down_pair, down_near)
        down_parts = moves.across_parts(down_block)
        b_sent = moves.pair_ready(b_grads, b_far)
        input_grad = input_part(after(input_grad, down_block, b_sent), dqkv_b, 1 + half, None)
        input_grad, up_near, a_pair = after_all((input_grad, up_near, a_pair))
        b_pair = moves.pair(after(b_sent, input_grad))
        a_near_sent = moves.near_ready(a_grads, a_other, after(a_pair, b_sent))
        a_near = moves.near(a_near_sent)
        first_vec = after(vec_grads(dbias_qv), b_sent)
        up_block = moves.block(up_grads, up_other, up_pair, up_near)
        up_block, *down_parts = after_all((up_block, *down_parts))
        up_parts = moves.across_parts(up_block)
        b_near_sent = moves.near_ready(b_grads, b_other, after(b_pair, up_block))
        b_near = moves.near(b_near_sent)
        a_block = moves.block(a_grads, a_other, a_pair, after(a_near, b_near_sent))
        b_block = moves.block(b_grads, b_other, b_pair, after(b_near, a_block))
        attn_parts = moves.across_parts(jnp.concatenate([b_block[-1:], a_block, b_block[:-1]]))
        down_sum = moves.across_total(down_block, after_all(down_parts, b_block))
        up_sum = moves.across_total(up_block, after_all(up_parts, b_block))
        attn_sum = moves.across_total(b_block[-1:], attn_parts)
        vec_grad = moves.total(first_vec, (input_grad, b_near_sent)).reshape(-1)
    else:
        input_grad = input_part(dfirst, dqkv_a, 0, None)
        down_sum, up_sum, attn_sum = (moves.sum(part) for part in (down_grads, up_grads, a_grads))
        vec_grad = moves.total(vec_grads(dbias_qv), None).reshape(-1)
    attn_grad = jnp.stack([attn_sum[:, k * col_dev : (k + 1) * col_dev] for k in range(mats)])
    mlp_grad = jnp.stack([up_sum, down_sum])
    attn_step = adam_update(
        attn_master, attn_first, attn_second, attn_grad, MATRIX_RATE, MATRIX_DECAY
    )
    mlp_step = adam_update(mlp_master, mlp_first, mlp_second, mlp_grad, MATRIX_RATE, MATRIX_DECAY)
    vec_step = adam_update(vec_master, vec_first, vec_second, vec_grad, VECTOR_RATE, 0.0)
    return (layer_out, pooled, input_grad, *attn_step, *mlp_step, *vec_step)


def solution(mesh):
    in_specs = (
        P(("dp", "tp"), None),
        P(("dp", "tp"), None),
        P(("dp", "tp")),
        P(None, "dp", "tp"),
        P(None, "dp", "tp"),
        P(None, "dp", "tp"),
        P(None, "dp", "tp"),
        P(None, "dp", "tp"),
        P(None, "dp", "tp"),
        P(),
        P(),
        P(),
    )
    out_specs = (
        P(("dp", "tp"), None),
        P(("dp", "tp"), None),
        P(("dp", "tp"), None),
        P(None, "dp", "tp"),
        P(None, "dp", "tp"),
        P(None, "dp", "tp"),
        P(None, "dp", "tp"),
        P(None, "dp", "tp"),
        P(None, "dp", "tp"),
        P(None, "dp", "tp"),
        P(None, "dp", "tp"),
        P(),
        P(),
        P(),
        P(),
    )
    return jax.shard_map(
        on_device, mesh=mesh, in_specs=in_specs, out_specs=out_specs, check_vma=False
    )
```

```python
import functools

import jax
import jax.numpy as jnp
from jax import lax
from jax.experimental import pallas as pl
from jax.experimental.pallas import tpu as pltpu
from jax.sharding import PartitionSpec as P

HEAD_DIM = 64
SEQ = 512
SEGS = 128
STEP = 10


NORM_EPS = 1e-12
BETA_ONE = 0.9
BETA_TWO = 0.999
ADAM_EPS = 1e-06
MATRIX_RATE = 0.1
VECTOR_RATE = 0.3
MATRIX_DECAY = 0.01
SCALE = HEAD_DIM ** (-0.5)
HALF_ROOT = 0.7071067811865476
PDF_SCALE = 0.3989422804014327
NT = (((1,), (1,)), ((), ()))
TN = (((0,), (0,)), ((), ()))
BF = jnp.bfloat16
F32 = jnp.float32
MIB = 1 << 20
BIAS_OUT, BIAS_TWO, GAIN_ONE, SHIFT_ONE, GAIN_TWO, SHIFT_TWO = range(-6, 0)


def dot(left, right):
    return jnp.dot(left, right, preferred_element_type=F32)


def dot_tn(left, right):
    return lax.dot_general(left, right, TN, preferred_element_type=F32)


def dot_nt(left, right):
    return lax.dot_general(left, right, NT, preferred_element_type=F32)


def adam_update(weight, moment_one, moment_two, gradient, step_rate, decay_rate):
    first_new = BETA_ONE * moment_one + (1.0 - BETA_ONE) * gradient
    second_new = BETA_TWO * moment_two + (1.0 - BETA_TWO) * gradient * gradient
    fix_one = 1.0 - BETA_ONE**STEP
    fix_two = 1.0 - BETA_TWO**STEP
    direction = first_new / fix_one / (jnp.sqrt(second_new / fix_two) + ADAM_EPS)
    weight_new = weight - step_rate * (direction + decay_rate * weight)
    return (first_new, second_new, weight_new, weight_new.astype(BF))


def split_blocks(pieces):
    blocks = []
    for piece in pieces:
        blocks += [piece.at[k] for k in range(piece.shape[0])] if len(piece.shape) == 4 else [piece]
    return blocks


def weight_copies(form, first, place, pieces, held, sems):
    groups, count = held.shape[0], held.shape[1]
    if form == "one":
        return [
            pltpu.make_async_copy(pieces[0].at[k], held.at[k, 0], sems.at[k]) for k in range(groups)
        ], 1
    near = [
        pltpu.make_async_copy(piece.at[first], held.at[0, place[j]], sems.at[j])
        for j, piece in enumerate(pieces[:count])
    ]
    far = [
        pltpu.make_async_copy(piece, held.at[pl.ds(1, groups - 1), place[j]], sems.at[count + j])
        for j, piece in enumerate(split_blocks(pieces[count:]))
    ]
    return near + far, count


def bring_weight(copies, first_part, step):
    @pl.when(step == 0)
    def _():
        for copy in copies:
            copy.start()
        for copy in copies[:first_part]:
            copy.wait()

    @pl.when(step == 1)
    def _():
        for copy in copies[first_part:]:
            copy.wait()


def keep_weight(held, out, sem, step, last):
    copy = pltpu.make_async_copy(held, out, sem)
    pl.when(step == 1)(copy.start)
    pl.when(step == last)(copy.wait)


def flat(value):
    return value.reshape(value.shape[0] * value.shape[1], value.shape[2])


def rounded(vec_ref, row):
    at = row % vec_ref.shape[0]
    return vec_ref[at : at + 1, :].astype(BF).astype(F32)


def own_part(row, own, size):
    out = row[:, 0:size]
    for k in range(1, row.shape[1] // size):
        out = jnp.where(own == k, row[:, k * size : (k + 1) * size], out)
    return out


def write_pieces(place, grad, outs):
    j = 0
    for out in outs:
        for k in range(out.shape[0]):
            out[k, 0] = grad[place[j]]
            j += 1


def normed_rows(value):
    centred = value - jnp.mean(value, axis=-1, keepdims=True)
    inverse = lax.rsqrt(jnp.mean(centred * centred, axis=-1, keepdims=True) + NORM_EPS)
    return centred * inverse, inverse


def norm_back(cot, normed, inverse, gain):
    scaled = cot * gain
    mean_one = jnp.mean(scaled, axis=-1, keepdims=True)
    mean_two = jnp.mean(scaled * normed, axis=-1, keepdims=True)
    return (scaled - mean_one - normed * mean_two) * inverse


def column_sum(value):
    return jnp.sum(value, axis=0, keepdims=True)


def attn_forward_kernel(form, n, place, x_ref, vec_ref, *refs):
    pieces = refs[:n]
    qkv_ref, probs_ref, ctx_ref, kept_ref, norm_ref, inv_ref = refs[n : n + 6]
    held, total, sems, kept_sem = refs[n + 6 :]
    slot = step = pl.program_id(0)
    steps = pl.num_programs(0)
    own = place[place.shape[0] - 1]
    width = qkv_ref.shape[2]
    part = width // 3

    bring_weight(*weight_copies(form, 0, place, pieces, held, sems), step)
    keep_weight(held, kept_ref, kept_sem, step, steps - 1)
    bias_q = own_part(rounded(vec_ref, 0), own ^ slot, part)
    bias_v = own_part(rounded(vec_ref, 1), own ^ slot, part)
    bias = jnp.concatenate([bias_q, jnp.zeros_like(bias_q), bias_v], axis=1)
    projected = dot(x_ref[...], flat(held[slot, :, :, 0:width])) + bias
    low = projected.astype(BF)
    qkv_ref[0] = low
    parts = []
    for h in range(part // HEAD_DIM):
        lo = h * HEAD_DIM
        q = low[:, lo : lo + HEAD_DIM] * BF(SCALE)
        k = low[:, part + lo : part + lo + HEAD_DIM]
        v = low[:, 2 * part + lo : 2 * part + lo + HEAD_DIM]
        scores = dot_nt(q, k)
        expanded = jnp.exp(scores - jnp.max(scores, axis=-1, keepdims=True))
        inverse = 1.0 / jnp.sum(expanded, axis=-1, keepdims=True)
        probs = (expanded * inverse).astype(BF)
        probs_ref[0, h] = probs
        parts.append(dot(probs, v))
    context = jnp.concatenate(parts, axis=1).astype(BF)
    ctx_ref[0] = context
    added = dot_nt(context, flat(held[slot, :, :, width:]))

    @pl.when(step == 0)
    def _():
        total[...] = x_ref[...].astype(F32) + rounded(vec_ref, BIAS_OUT) + added

    @pl.when(step > 0)
    def _():
        total[...] += added

    @pl.when(step == steps - 1)
    def _():
        norm_ref[...], inv_ref[...] = normed_rows(total[...])


def middle_rows(norm_ref, vec_ref):
    return norm_ref[...] * rounded(vec_ref, GAIN_ONE) + rounded(vec_ref, SHIFT_ONE)


def mlp_up_kernel(form, n, place, norm_ref, vec_ref, *refs):
    pieces = refs[:n]
    hid_ref, slope_ref, kept_ref = refs[n : n + 3]
    held, low_ref, sems, kept_sem = refs[n + 3 :]
    step = pl.program_id(0)
    slot = step
    own = place[place.shape[0] - 1]

    bring_weight(*weight_copies(form, 1, place, pieces, held, sems), step)
    keep_weight(held, kept_ref, kept_sem, step, pl.num_programs(0) - 1)

    @pl.when(step == 0)
    def _():
        low_ref[...] = middle_rows(norm_ref, vec_ref).astype(BF)

    bias = vec_ref[pl.ds(2 + (own ^ slot), 1), :].astype(BF).astype(F32)

    u = dot(low_ref[...], flat(held[slot])) + bias
    cdf = 0.5 + 0.5 * lax.erf(u * HALF_ROOT)
    hid_ref[0] = (u * cdf).astype(BF)
    slope_ref[0] = (cdf + u * (jnp.exp(u * u * -0.5) * PDF_SCALE)).astype(BF)


def mlp_down_kernel(form, n, outs, place, norm_ref, vec_ref, og_ref, ids_ref, hid_ref, *refs):
    pieces = refs[:n]
    out_ref, pool_ref, dres_ref, dlow_ref, sums_ref, kept_ref = refs[n : n + 6]
    grads = refs[n + 6 : n + 6 + outs]
    held, total, grad_low, sems, kept_sem = refs[n + 6 + outs :]
    step = pl.program_id(0)
    groups = held.shape[0]

    bring_weight(*weight_copies(form, 2, place, pieces, held, sems), step)
    keep_weight(held, kept_ref, kept_sem, step, 2 * groups - 1)

    @pl.when(step == 0)
    def _():
        total[...] = middle_rows(norm_ref, vec_ref) + rounded(vec_ref, BIAS_TWO)

    @pl.when(step < groups)
    def _():
        total[...] += dot_nt(hid_ref[0], flat(held[step]))

    @pl.when(step == groups - 1)
    def _():
        normed, inverse = normed_rows(total[...])
        gain = rounded(vec_ref, GAIN_TWO)
        final = normed * gain + rounded(vec_ref, SHIFT_TWO)
        high = final.astype(BF)
        out_ref[...] = high
        docs = pool_ref.shape[0] // SEGS
        for d in range(docs):
            slots = lax.broadcasted_iota(jnp.int32, (SEGS, SEQ), 0)
            onehot = jnp.where(slots == ids_ref[d : d + 1, :], 1.0, 0.0)
            counts = jnp.sum(onehot, axis=1, keepdims=True)
            marks = onehot.astype(BF)
            at = slice(d * SEQ, (d + 1) * SEQ)
            rest = (final[at] - high[at].astype(F32)).astype(BF)
            sums = dot(marks, high[at]) + dot(marks, rest)
            pool_ref[d * SEGS : (d + 1) * SEGS, :] = sums / jnp.maximum(counts, 1.0)
        cot = og_ref[...].astype(F32)
        dres = norm_back(cot, normed, inverse, gain)
        dres_ref[...] = dres
        low = dres.astype(BF)
        dlow_ref[...] = low
        sums_ref[0:1, :] = column_sum(dres)
        sums_ref[1:2, :] = column_sum(cot * normed)
        sums_ref[2:3, :] = column_sum(cot)

    @pl.when(step >= groups)
    def _():
        grad_low[...] = dot_tn(dlow_ref[...], hid_ref[0]).astype(BF).reshape(grad_low.shape)
        write_pieces(place, grad_low, grads)


def mlp_back_kernel(outs, place, norm_ref, vec_ref, dlow_ref, slope_ref, down_ref, *refs):
    dpre_ref, dbias_ref = refs[:2]
    grads = refs[2 : 2 + outs]
    low_ref, grad_low = refs[2 + outs :]
    slot = pl.program_id(0)
    own = place[place.shape[0] - 1]

    @pl.when(slot == 0)
    def _():
        low_ref[...] = middle_rows(norm_ref, vec_ref).astype(BF)

    dpre = (dot(dlow_ref[...], flat(down_ref[0])) * slope_ref[0].astype(F32)).astype(BF)
    dpre_ref[0] = dpre
    dbias_ref[pl.ds(own ^ slot, 1), :] = column_sum(dpre.astype(F32))
    grad_low[...] = dot_tn(low_ref[...], dpre).astype(BF).reshape(grad_low.shape)
    write_pieces(place, grad_low, grads)


def norm_back_kernel(place, norm_ref, inv_ref, vec_ref, dres_ref, dpre_ref, up_ref, *refs):
    dfirst_ref, dout_ref, sums_ref, total = refs
    slot = pl.program_id(0)
    added = dot_nt(dpre_ref[0], flat(up_ref[0]))

    @pl.when(slot == 0)
    def _():
        total[...] = dres_ref[...] + added

    @pl.when(slot > 0)
    def _():
        total[...] += added

    @pl.when(slot == pl.num_programs(0) - 1)
    def _():
        cot = total[...]
        normed = norm_ref[...]
        dfirst = norm_back(cot, normed, inv_ref[...], rounded(vec_ref, GAIN_ONE))
        dfirst_ref[...] = dfirst
        low = dfirst.astype(BF)
        dout_ref[...] = low
        sums_ref[0:1, :] = column_sum(dfirst)
        sums_ref[1:2, :] = column_sum(cot * normed)
        sums_ref[2:3, :] = column_sum(cot)


def attn_back_kernel(
    outs, groups, start, place, x_ref, dout_ref, qkv_ref, probs_ref, ctx_ref, weight_ref, *refs
):
    dqkv_ref, dbias_ref = refs[:2]
    grads = refs[2 : 2 + outs]
    grad_low = refs[2 + outs]
    step = pl.program_id(0)
    slot = (step + start) % groups
    own = place[place.shape[0] - 1]
    width = qkv_ref.shape[2]
    part = width // 3
    block = grad_low.shape[0:2]

    @pl.when(step == 0)
    def _():
        dbias_ref[...] = jnp.zeros_like(dbias_ref)

    context = ctx_ref[0]
    grad_out = dot_tn(dout_ref[...], context).astype(BF)
    grad_low[:, :, width:] = grad_out.reshape(block + (part,))
    dctx = dot(dout_ref[...], flat(weight_ref[0, :, :, width:])).astype(BF)
    dctx_t = dctx.T
    row_dots = dctx.astype(F32) * context.astype(F32)
    q_t = qkv_ref[0, :, 0:part].T
    dq, dk_t, dv_t = [], [], []
    for h in range(part // HEAD_DIM):
        at = slice(h * HEAD_DIM, (h + 1) * HEAD_DIM)
        k = qkv_ref[0, :, part + h * HEAD_DIM : part + (h + 1) * HEAD_DIM]
        v = qkv_ref[0, :, 2 * part + h * HEAD_DIM : 2 * part + (h + 1) * HEAD_DIM]
        probs = probs_ref[0, h]
        row_dot = jnp.sum(row_dots[:, at], axis=-1, keepdims=True)
        dprobs = dot_nt(dctx[:, at], v)
        dscores = (probs.astype(F32) * (dprobs - row_dot)).astype(BF)
        dv_t.append(dot(dctx_t[at], probs))
        dq.append(dot(dscores, k) * SCALE)
        dk_t.append(dot(q_t[at], dscores) * SCALE)
    dqkv = jnp.concatenate(
        [
            jnp.concatenate(dq, axis=1).astype(BF),
            jnp.concatenate(dk_t, axis=0).astype(BF).T,
            jnp.concatenate(dv_t, axis=0).astype(BF).T,
        ],
        axis=1,
    )
    dqkv_ref[0] = dqkv
    dbias = column_sum(dqkv.astype(F32))
    for z in range(dbias_ref.shape[1] // part):
        cols = slice(z * part, (z + 1) * part)
        mine = own ^ slot == z
        dbias_ref[0:1, cols] += jnp.where(mine, dbias[:, 0:part], 0.0)
        dbias_ref[1:2, cols] += jnp.where(mine, dbias[:, 2 * part :], 0.0)
    grad_low[:, :, 0:width] = dot_tn(x_ref[...], dqkv).astype(BF).reshape(block + (width,))
    write_pieces(place, grad_low, grads)


def input_grad_kernel(place, dfirst_ref, dqkv_ref, weight_ref, out_ref, total):
    slot = pl.program_id(0)
    width = dqkv_ref.shape[2]
    added = dot_nt(dqkv_ref[0], flat(weight_ref[0, :, :, 0:width]))

    @pl.when(slot == 0)
    def _():
        total[...] = dfirst_ref[...] + added

    @pl.when(slot > 0)
    def _():
        total[...] += added

    @pl.when(slot == pl.num_programs(0) - 1)
    def _():
        out_ref[...] = total[...].astype(out_ref.dtype)


def whole(shape):
    return pl.BlockSpec(shape, lambda i, place: (0,) * len(shape))


def by_slot(shape, index=lambda i: i):
    return pl.BlockSpec((1,) + shape, lambda i, place: (index(i),) + (0,) * len(shape))


def by_piece(shape, index=lambda i, place: i):
    return pl.BlockSpec(
        (shape[0], 1) + shape[2:], lambda i, place: (0, index(i, place)) + (0,) * len(shape[2:])
    )


ANY = pl.BlockSpec(memory_space=pltpu.HBM)
FREE = pl.BlockSpec(memory_space=pl.ANY)
VMEM_LIMIT = 28 * MIB


def pinned(value, spec, space=None):
    if space == "vmem":
        return pltpu.with_memory_space_constraint(value, pltpu.VMEM)
    if space == "hbm":
        return pltpu.with_memory_space_constraint(value, pltpu.HBM)
    return value


def placed(shape, dtype, space=None):
    if space == "vmem":
        return pltpu.VMEM(shape, dtype)
    if space == "hbm":
        return pltpu.HBM(shape, dtype)
    return jax.ShapeDtypeStruct(shape, dtype)


def call(kernel, name, grid, place, inputs, outputs, scratch, aliases=None):
    return pl.pallas_call(
        kernel,
        name=name,
        out_shape=[placed(out[0], out[1], *out[3:]) for out in outputs],
        grid_spec=pltpu.PrefetchScalarGridSpec(
            num_scalar_prefetch=1,
            grid=(grid,),
            in_specs=[given[1] for given in inputs],
            out_specs=[out[2] for out in outputs],
            scratch_shapes=scratch,
        ),
        compiler_params=pltpu.CompilerParams(
            dimension_semantics=("arbitrary",), vmem_limit_bytes=VMEM_LIMIT
        ),
        input_output_aliases=aliases or {},
        cost_estimate=pl.CostEstimate(flops=1000, bytes_accessed=1000, transcendentals=0),
    )(place, *[pinned(*given) for given in inputs])


def after(value, *deps):
    deps = [dep for dep in deps if dep is not None]
    return lax.optimization_barrier((value, *deps))[0] if deps else value


def after_all(values, *deps):
    return list(lax.optimization_barrier((*values, *deps)))[: len(values)]


def xor_pairs(count, mask):
    return [(i, i ^ mask) for i in range(count)]


class PlaneTransfers:
    forms = ("pieces", "pieces", "pieces")

    def __init__(self, tp_count):
        self.count = 8
        self.groups = tp_count
        self.first = [(i, i ^ (4 if i & 1 else 2)) for i in range(8)]
        self.second = [(i, i ^ (2 if i & 1 else 4)) for i in range(8)]
        self.cores = xor_pairs(8, 1)
        me = lax.axis_index("dp")
        one = jnp.where(me % 2 == 1, 4, 2)
        two = 6 - one
        self.place = jnp.stack(
            [
                me,
                me ^ one,
                me ^ two,
                me ^ 6,
                me ^ 1,
                me ^ 1 ^ two,
                me ^ 1 ^ one,
                me ^ 7,
                lax.axis_index("tp"),
            ]
        ).astype(jnp.int32)
        self.out_counts = (4, 2, 2)
        self.last_counts = (4, 4)

    def shifted(self, shard, mask):
        return lax.ppermute(shard, "tp", xor_pairs(self.groups, mask))

    def across(self, shard):
        return [self.shifted(shard, k) for k in range(1, self.groups)]

    def cores_of(self, mine):
        return [lax.ppermute(piece, "dp", self.cores) for piece in mine]

    def both(self, mine):
        return mine + [lax.ppermute(piece, "dp", self.cores) for piece in mine]

    def first_chip(self, shards):
        return lax.ppermute(shards, "dp", self.first)

    def second_chip(self, shards):
        return lax.ppermute(shards, "dp", self.second)

    def vec_step(self, vec, axis, mask):
        size = self.count if axis == "dp" else self.groups
        return vec + lax.ppermute(vec, axis, xor_pairs(size, mask))


    def swap_far(self, grads):
        return lax.ppermute(grads[2], "dp", self.cores)

    def swap_near(self, grads):
        return lax.ppermute(grads[1], "dp", self.cores)

    def pair_ready(self, grads, far):
        return (grads[0][2:4].astype(F32) + far.astype(F32)).astype(BF)

    def pair(self, sent):
        return lax.ppermute(sent, "dp", self.second)

    def near_ready(self, grads, other, pair):
        one = grads[0][1].astype(F32) + other[1].astype(F32) + pair[1].astype(F32)
        return one.astype(BF)

    def near(self, sent):
        return lax.ppermute(sent, "dp", self.first)

    def block(self, grads, other, pair, near):
        own = grads[0][0].astype(F32) + other[0].astype(F32)
        return own + pair[0].astype(F32) + near.astype(F32)


    def across_first(self, block):
        return self.shifted(jnp.stack([block[1], block[3]]).astype(BF), 1)

    def across_half(self, block, got):
        return block[0] + got[0].astype(F32), (block[2] + got[1].astype(F32)).astype(BF)

    def across_last(self, half):
        return self.shifted(half[1], 2)


class PlainTransfers:
    forms = ("one", "one", "one")

    def __init__(self, dp_count, tp_count):
        self.dp = dp_count
        self.tp = tp_count
        self.count = 1
        self.groups = tp_count
        self.place = jnp.zeros((2,), jnp.int32)
        self.out_counts = (1,)

    def one(self, shards):
        rows, columns = shards.shape
        out = lax.all_gather(shards, ("dp", "tp"), axis=0, tiled=False)
        out = out.reshape(self.dp, self.tp, rows, columns).transpose(1, 0, 2, 3)
        return [out.reshape(self.tp, self.dp * rows, columns)]

    def gather(self, attn, mlp):
        return self.one(attn), self.one(mlp[0]), self.one(mlp[1])

    def total(self, vec):
        return lax.psum(vec, ("dp", "tp"))

    def sum(self, grads):
        _, groups, rows, columns = grads[0].shape
        parts = grads[0].reshape(groups, self.dp, rows // self.dp, columns).transpose(1, 0, 2, 3)
        parts = parts.reshape(self.dp * groups, rows // self.dp, columns)
        out = lax.psum_scatter(parts, ("dp", "tp"), scatter_dimension=0, tiled=True)
        return out[0].astype(F32)


def on_device(
    tokens,
    out_grad,
    segment_ids,
    attn_master,
    attn_first,
    attn_second,
    mlp_master,
    mlp_first,
    mlp_second,
    vec_master,
    vec_first,
    vec_second,
):
    rows, width = tokens.shape
    dp_count = lax.axis_size("dp")
    groups = lax.axis_size("tp")
    mats, row_dev, col_dev = attn_master.shape
    hidden = mlp_master.shape[2]
    docs = rows // SEQ
    heads = col_dev // HEAD_DIM
    wide = 3 * col_dev
    cols = mats * col_dev
    plane = dp_count == 8 and groups == 4 and row_dev % 16 == 0
    moves = PlaneTransfers(groups) if plane else PlainTransfers(dp_count, groups)
    place = moves.place
    count = moves.count
    outs = len(moves.out_counts)
    block = width // count

    attn_low = jnp.concatenate([attn_master[k] for k in range(mats)], axis=1).astype(BF)
    vecs = vec_master.reshape(-1, width)
    mlp_low = mlp_master.astype(BF)
    forms = moves.forms

    full = (rows, width)
    row_vec = (rows, 1)
    weight = (groups, count, block, cols)
    hid_weight = (groups, count, block, hidden)
    slot_weight = by_slot((count, block, cols))
    slot_hid_weight = by_slot((count, block, hidden))
    slot_hid = by_slot((rows, hidden))
    slot_wide = by_slot((rows, wide))
    base = 2 * rows * width
    dma = pltpu.SemaphoreType.DMA
    vec_in = (vecs, whole(vecs.shape))

    def arriving(pieces):
        return [(piece, ANY, "hbm") for piece in pieces]

    def grad_outs(columns, base_step=0):
        def index(i, place):
            return jnp.maximum(i - base_step, 0)

        return [
            ((k, groups, block, columns), BF, by_piece((k, groups, block, columns), index), "hbm")
            for k in moves.out_counts
        ]

    def attn_forward(given, pieces):
        return call(
            functools.partial(attn_forward_kernel, forms[0], len(pieces)),
            "attn_forward",
            groups,
            place,
            [(given, whole(full)), vec_in] + arriving(pieces),
            [
                ((groups, rows, wide), BF, slot_wide, "hbm"),
                ((groups, heads, rows, rows), BF, by_slot((heads, rows, rows)), "hbm"),
                ((groups, rows, col_dev), BF, by_slot((rows, col_dev)), "hbm"),
                (weight, BF, ANY, "hbm"),
                (full, F32, whole(full), "vmem"),
                (row_vec, F32, whole(row_vec), "vmem"),
            ],
            [pltpu.VMEM(weight, BF), pltpu.VMEM(full, F32), dma((max(2 * count, groups),)), dma],
        )

    def mlp_up(given, pieces):
        return call(
            functools.partial(mlp_up_kernel, forms[1], len(pieces)),
            "mlp_up",
            groups,
            place,
            [(given, whole(full), "vmem"), vec_in] + arriving(pieces),
            [((groups, rows, hidden), BF, slot_hid, "hbm")] * 2 + [(hid_weight, BF, ANY, "hbm")],
            [pltpu.VMEM(hid_weight, BF), pltpu.VMEM(full, BF), dma((max(2 * count, groups),)), dma],
        )

    if plane:
        own = jnp.concatenate([attn_low[None], mlp_low])
        own_one, own_two = moves.first_chip(own), moves.second_chip(own)
        own_one, own_two, *attn_far = after_all((own_one, own_two, *moves.across(attn_low)))

        attn_far = jnp.stack(attn_far)
        attn_one = moves.first_chip(attn_far)
        own_three = moves.second_chip(own_one)
        up_far = moves.across(after(mlp_low[0], attn_far))
        attn_one, own_three, *up_far = after_all((attn_one, own_three, *up_far))

        attn_pair = moves.second_chip(jnp.stack([attn_far, attn_one]))
        up_far = jnp.stack(up_far)
        up_one = moves.first_chip(up_far)
        down_far = moves.across(after(mlp_low[1], up_far))
        attn_pair, up_one, *down_far = after_all((attn_pair, up_one, *down_far))

        up_sent = jnp.stack([up_far, up_one])
        up_pair = moves.second_chip(up_sent)
        down_far = jnp.stack(down_far)
        down_one = moves.first_chip(down_far)
        own_pieces = moves.both(after_all([own, own_one, own_two, own_three], attn_pair))
        attn_pieces = own_pieces + moves.both(after_all([attn_far, attn_one, attn_pair], attn_pair))
        qkv, probs, context, attn_kept, norm_one, inv_one = attn_forward(
            after(tokens, down_far), attn_pieces
        )
        up_swapped = moves.cores_of([up_far, up_one])
        norm_one, up_pair, down_one, *up_swapped = after_all(
            (norm_one, up_pair, down_one, *up_swapped)
        )

        down_sent = jnp.stack([down_far, down_one])
        down_pair = moves.second_chip(down_sent)
        up_pieces = own_pieces + [up_far, up_one, up_pair, *up_swapped, *moves.cores_of([up_pair])]
        down_swapped = moves.cores_of([after(down_far, norm_one), down_one])
        hid, slope, up_kept = mlp_up(after(norm_one, down_sent), up_pieces)
        hid, down_pair, *down_swapped = after_all((hid, down_pair, *down_swapped))
        down_pieces = own_pieces + [down_far, down_one, down_pair]
        down_pieces += down_swapped + moves.cores_of([down_pair])
    else:
        attn_pieces, up_pieces, down_pieces = moves.gather(attn_low, mlp_low)
        qkv, probs, context, attn_kept, norm_one, inv_one = attn_forward(tokens, attn_pieces)
        hid, slope, up_kept = mlp_up(norm_one, up_pieces)
    down_in = arriving(down_pieces)
    layer_out, pooled, dres, dres_low, sums_two, down_kept, *down_grads = call(
        functools.partial(mlp_down_kernel, forms[2], len(down_in), outs),
        "mlp_down",
        2 * groups,
        place,
        [
            (norm_one, whole(full), "vmem"),
            vec_in,
            (out_grad, whole(full)),
            (segment_ids.reshape(docs, SEQ), whole((docs, SEQ))),
            (hid, by_slot((rows, hidden), lambda i: i % groups), "hbm"),
        ]
        + down_in,
        [
            (full, BF, whole(full)),
            ((docs * SEGS, width), F32, whole((docs * SEGS, width))),
            (full, F32, whole(full), "vmem"),
            (full, BF, whole(full), "vmem"),
            ((3, width), F32, whole((3, width))),
            (hid_weight, BF, ANY, "hbm"),
        ]
        + grad_outs(hidden, groups),
        [
            pltpu.VMEM(hid_weight, BF),
            pltpu.VMEM(full, F32),
            pltpu.VMEM((count, block, hidden), BF),
            dma((max(2 * count, groups),)),
            dma,
        ],
    )
    down_far = moves.swap_far(down_grads) if plane else None
    down_other = moves.swap_near(down_grads) if plane else None
    dpre, dbias_hidden, *up_grads = call(
        functools.partial(mlp_back_kernel, outs),
        "mlp_back",
        groups,
        place,
        [
            (norm_one, whole(full), "vmem"),
            vec_in,
            (dres_low, whole(full), "vmem"),
            (slope, slot_hid, "hbm"),
            (down_kept, slot_hid_weight, "hbm"),
        ],
        [
            ((groups, rows, hidden), BF, slot_hid, "vmem"),
            ((groups, hidden), F32, whole((groups, hidden))),
        ]
        + grad_outs(hidden),
        [pltpu.VMEM(full, BF), pltpu.VMEM((count, block, hidden), BF)],
    )
    if plane:
        down_sent = moves.pair_ready(down_grads, down_far)
        dres = after(dres, down_sent)
        down_pair = moves.pair(down_sent)
        up_far = moves.swap_far(up_grads)
        up_other = moves.swap_near(up_grads)
    dfirst, dout, sums_one = call(
        norm_back_kernel,
        "norm_back",
        groups,
        place,
        [
            (norm_one, whole(full), "vmem"),
            (inv_one, whole(row_vec), "vmem"),
            vec_in,
            (dres, whole(full), "vmem"),
            (dpre, slot_hid, "vmem"),
            (up_kept, slot_hid_weight, "hbm"),
        ],
        [
            (full, F32, whole(full), "vmem"),
            (full, BF, whole(full), "vmem"),
            ((3, width), F32, whole((3, width))),
        ],
        [pltpu.VMEM(full, F32)],
    )
    def attn_back(start, slots, dout, counts=moves.out_counts):
        def shifted(shape):
            return by_slot(shape, lambda i: (i + start) % groups)

        outputs = [
            ((slots, rows, wide), BF, slot_wide, "hbm"),
            ((2, width), F32, whole((2, width))),
        ]
        for k in counts:
            shape = (k, slots, block, cols)
            outputs.append((shape, BF, by_piece(shape), "hbm"))
        inputs = [
            (tokens, whole(full)),
            (dout, whole(full), "vmem"),
            (qkv, shifted((rows, wide)), "hbm"),
            (probs, shifted((heads, rows, rows)), "hbm"),
            (context, shifted((rows, col_dev)), "hbm"),
            (attn_kept, shifted((count, block, cols)), "hbm"),
        ]
        return call(
            functools.partial(attn_back_kernel, len(counts), groups, start),
            "attn_back",
            slots,
            place,
            inputs,
            outputs,
            [pltpu.VMEM((count, block, cols), BF)],
        )

    def vec_grads(dbias_qv):
        return jnp.concatenate(
            [
                dbias_qv,
                dbias_hidden,
                sums_one[0:1],
                sums_two[0:1],
                sums_one[1:3],
                sums_two[1:3],
            ],
            axis=0,
        )

    if plane:
        up_sent = moves.pair_ready(up_grads, up_far)
        up_pair = moves.pair(up_sent)
        half = groups // 2
        dqkv_a, dbias_a, *a_grads = attn_back(1, half, after(dout, up_sent))
        dbias_a, down_pair, down_other, *a_grads = after_all(
            (dbias_a, down_pair, down_other, *a_grads)
        )

        down_near_sent = moves.near_ready(down_grads, down_other, down_pair)
        down_near = moves.near(down_near_sent)
        a_far = moves.swap_far(a_grads)
        a_other = moves.swap_near(a_grads)
        dqkv_b, dbias_b, *b_grads = attn_back(
            1 + half, half, after(dout, down_near_sent), moves.last_counts
        )
        dbias_b, down_near, up_pair, up_other, a_far, a_other, *b_grads = after_all(
            (dbias_b, down_near, up_pair, up_other, a_far, a_other, *b_grads)
        )

        b_other = moves.swap_near(b_grads)
        up_near_sent = moves.near_ready(up_grads, up_other, up_pair)
        up_near = moves.near(up_near_sent)
        a_sent = moves.pair_ready(a_grads, a_far)
        a_pair = moves.pair(a_sent)
        down_block = moves.block(down_grads, down_other, down_pair, down_near)
        down_got = moves.across_first(down_block)
        vec_one = moves.vec_step(vec_grads(dbias_a + dbias_b), "tp", 1)
        dfirst = after(dfirst, up_near_sent, a_sent, down_block)
    else:
        dqkv_a, dbias_qv, *a_grads = attn_back(0, groups, dout)

    def input_part(given, part, start, space):
        slots = part.shape[0]
        out = (full, F32, whole(full), space) if space else (full, BF, whole(full))
        return call(
            input_grad_kernel,
            "input_grad",
            slots,
            place,
            [
                (given, whole(full), "vmem"),
                (part, slot_wide, "hbm"),
                (attn_kept, by_slot((count, block, cols), lambda i: (i + start) % groups), "hbm"),
            ],
            [out],
            [pltpu.VMEM(full, F32)],
        )[0]

    if plane:
        input_grad = input_part(dfirst, dqkv_a, 1, "vmem")
        input_grad, b_other, up_near, a_pair, down_got, vec_one = after_all(
            (input_grad, b_other, up_near, a_pair, down_got, vec_one)
        )

        b_sent = moves.pair_ready(b_grads, b_other[2:4])
        b_pair = moves.pair(b_sent)
        a_near_sent = moves.near_ready(a_grads, a_other, a_pair)
        a_near = moves.near(a_near_sent)
        down_half = moves.across_half(down_block, down_got)
        down_got = moves.across_last(down_half)
        up_block = moves.block(up_grads, up_other, up_pair, up_near)
        up_got = moves.across_first(up_block)
        vec_two = moves.vec_step(vec_one, "tp", 2)
        input_grad = input_part(
            after(input_grad, b_sent, a_near_sent, *down_half, up_block), dqkv_b, 1 + half, None
        )
        input_grad, a_near, b_pair, down_got, up_got, vec_two = after_all(
            (input_grad, a_near, b_pair, down_got, up_got, vec_two)
        )

        b_near_sent = moves.near_ready(b_grads, b_other, b_pair)
        b_near = moves.near(b_near_sent)
        a_block = moves.block(a_grads, a_other, a_pair, a_near)
        a_parts = [moves.shifted(a_block[k].astype(BF), k + 1) for k in range(half)]
        up_half = moves.across_half(up_block, up_got)
        up_got = moves.across_last(up_half)
        vec_three = moves.vec_step(vec_two, "dp", 1)
        b_near, vec_three = after_all((b_near, vec_three))

        b_block = moves.block(b_grads, b_other, b_pair, b_near)
        b_part = moves.shifted(b_block[0].astype(BF), half + 1)
        vec_four = moves.vec_step(vec_three, "dp", 2)
        vec_four, up_got = after_all((vec_four, up_got))
        vec_grad = moves.vec_step(vec_four, "dp", 4).reshape(-1)
        down_sum = down_half[0] + down_got.astype(F32)
        up_sum = up_half[0] + up_got.astype(F32)
        attn_sum = b_block[1]
        for part in (*a_parts, b_part):
            attn_sum = attn_sum + part.astype(F32)
    else:
        input_grad = input_part(dfirst, dqkv_a, 0, None)
        down_sum, up_sum, attn_sum = (moves.sum(part) for part in (down_grads, up_grads, a_grads))
        vec_grad = moves.total(vec_grads(dbias_qv)).reshape(-1)
    attn_grad = jnp.stack([attn_sum[:, k * col_dev : (k + 1) * col_dev] for k in range(mats)])
    mlp_grad = jnp.stack([up_sum, down_sum])
    attn_step = adam_update(
        attn_master, attn_first, attn_second, attn_grad, MATRIX_RATE, MATRIX_DECAY
    )
    mlp_step = adam_update(mlp_master, mlp_first, mlp_second, mlp_grad, MATRIX_RATE, MATRIX_DECAY)
    vec_step = adam_update(vec_master, vec_first, vec_second, vec_grad, VECTOR_RATE, 0.0)
    return (layer_out, pooled, input_grad, *attn_step, *mlp_step, *vec_step)


def solution(mesh):
    in_specs = (
        P(("dp", "tp"), None),
        P(("dp", "tp"), None),
        P(("dp", "tp")),
        P(None, "dp", "tp"),
        P(None, "dp", "tp"),
        P(None, "dp", "tp"),
        P(None, "dp", "tp"),
        P(None, "dp", "tp"),
        P(None, "dp", "tp"),
        P(),
        P(),
        P(),
    )
    out_specs = (
        P(("dp", "tp"), None),
        P(("dp", "tp"), None),
        P(("dp", "tp"), None),
        P(None, "dp", "tp"),
        P(None, "dp", "tp"),
        P(None, "dp", "tp"),
        P(None, "dp", "tp"),
        P(None, "dp", "tp"),
        P(None, "dp", "tp"),
        P(None, "dp", "tp"),
        P(None, "dp", "tp"),
        P(),
        P(),
        P(),
        P(),
    )
    return jax.shard_map(
        on_device, mesh=mesh, in_specs=in_specs, out_specs=out_specs, check_vma=False
    )
```

```python
import functools

import jax
import jax.numpy as jnp
from jax import lax
from jax.experimental import pallas as pl
from jax.experimental.pallas import tpu as pltpu
from jax.sharding import PartitionSpec as P

HEAD_DIM = 64
SEQ = 512
SEGS = 128
STEP = 10


NORM_EPS = 1e-12
BETA_ONE = 0.9
BETA_TWO = 0.999
ADAM_EPS = 1e-06
MATRIX_RATE = 0.1
VECTOR_RATE = 0.3
MATRIX_DECAY = 0.01
SCALE = HEAD_DIM ** (-0.5)
HALF_ROOT = 0.7071067811865476
PDF_SCALE = 0.3989422804014327
NT = (((1,), (1,)), ((), ()))
TN = (((0,), (0,)), ((), ()))
BF = jnp.bfloat16
F32 = jnp.float32
MIB = 1 << 20
BIAS_OUT, BIAS_TWO, GAIN_ONE, SHIFT_ONE, GAIN_TWO, SHIFT_TWO = range(-6, 0)


def dot(left, right):
    return jnp.dot(left, right, preferred_element_type=F32)


def dot_tn(left, right):
    return lax.dot_general(left, right, TN, preferred_element_type=F32)


def dot_nt(left, right):
    return lax.dot_general(left, right, NT, preferred_element_type=F32)


def adam_update(weight, moment_one, moment_two, gradient, step_rate, decay_rate):
    first_new = BETA_ONE * moment_one + (1.0 - BETA_ONE) * gradient
    second_new = BETA_TWO * moment_two + (1.0 - BETA_TWO) * gradient * gradient
    fix_one = 1.0 - BETA_ONE**STEP
    fix_two = 1.0 - BETA_TWO**STEP
    direction = first_new / fix_one / (jnp.sqrt(second_new / fix_two) + ADAM_EPS)
    weight_new = weight - step_rate * (direction + decay_rate * weight)
    return (first_new, second_new, weight_new, weight_new.astype(BF))


def split_blocks(pieces):
    blocks = []
    for piece in pieces:
        blocks += [piece.at[k] for k in range(piece.shape[0])] if len(piece.shape) == 4 else [piece]
    return blocks


def weight_copies(form, first, place, pieces, held, sems):
    groups, count = held.shape[0], held.shape[1]
    if form == "one":
        return [
            pltpu.make_async_copy(pieces[0].at[k], held.at[k, 0], sems.at[k]) for k in range(groups)
        ], 1
    near = [
        pltpu.make_async_copy(piece.at[first], held.at[0, place[j]], sems.at[j])
        for j, piece in enumerate(pieces[:count])
    ]
    far = [
        pltpu.make_async_copy(piece, held.at[pl.ds(1, groups - 1), place[j]], sems.at[count + j])
        for j, piece in enumerate(split_blocks(pieces[count:]))
    ]
    return near + far, count


def bring_weight(copies, first_part, step):
    @pl.when(step == 0)
    def _():
        for copy in copies:
            copy.start()
        for copy in copies[:first_part]:
            copy.wait()

    @pl.when(step == 1)
    def _():
        for copy in copies[first_part:]:
            copy.wait()


def keep_weight(held, out, sem, step, last):
    copy = pltpu.make_async_copy(held, out, sem)
    pl.when(step == 1)(copy.start)
    pl.when(step == last)(copy.wait)


def flat(value):
    return value.reshape(value.shape[0] * value.shape[1], value.shape[2])


def rounded(vec_ref, row):
    at = row % vec_ref.shape[0]
    return vec_ref[at : at + 1, :].astype(BF).astype(F32)


def own_part(row, own, size):
    out = row[:, 0:size]
    for k in range(1, row.shape[1] // size):
        out = jnp.where(own == k, row[:, k * size : (k + 1) * size], out)
    return out


def write_pieces(place, grad, outs):
    j = 0
    for out in outs:
        for k in range(out.shape[0]):
            out[k, 0] = grad[place[j]]
            j += 1


def normed_rows(value):
    centred = value - jnp.mean(value, axis=-1, keepdims=True)
    inverse = lax.rsqrt(jnp.mean(centred * centred, axis=-1, keepdims=True) + NORM_EPS)
    return centred * inverse, inverse


def norm_back(cot, normed, inverse, gain):
    scaled = cot * gain
    mean_one = jnp.mean(scaled, axis=-1, keepdims=True)
    mean_two = jnp.mean(scaled * normed, axis=-1, keepdims=True)
    return (scaled - mean_one - normed * mean_two) * inverse


def column_sum(value):
    return jnp.sum(value, axis=0, keepdims=True)


def attn_forward_kernel(form, n, place, x_ref, vec_ref, *refs):
    pieces = refs[:n]
    qkv_ref, probs_ref, ctx_ref, kept_ref, norm_ref, inv_ref = refs[n : n + 6]
    held, total, sems, kept_sem = refs[n + 6 :]
    slot = step = pl.program_id(0)
    steps = pl.num_programs(0)
    own = place[place.shape[0] - 1]
    width = qkv_ref.shape[2]
    part = width // 3

    bring_weight(*weight_copies(form, 0, place, pieces, held, sems), step)
    keep_weight(held, kept_ref, kept_sem, step, steps - 1)
    bias_q = own_part(rounded(vec_ref, 0), own ^ slot, part)
    bias_v = own_part(rounded(vec_ref, 1), own ^ slot, part)
    bias = jnp.concatenate([bias_q, jnp.zeros_like(bias_q), bias_v], axis=1)
    projected = dot(x_ref[...], flat(held[slot, :, :, 0:width])) + bias
    low = projected.astype(BF)
    qkv_ref[0] = low
    heads = range(part // HEAD_DIM)

    def head(k, h):
        return low[:, k * part + h * HEAD_DIM : k * part + (h + 1) * HEAD_DIM]

    scores = [dot_nt(head(0, h) * BF(SCALE), head(1, h)) for h in heads]
    for h in heads:
        expanded = jnp.exp(scores[h] - jnp.max(scores[h], axis=-1, keepdims=True))
        inverse = 1.0 / jnp.sum(expanded, axis=-1, keepdims=True)
        probs_ref[0, h] = (expanded * inverse).astype(BF)
    parts = [dot(probs_ref[0, h], head(2, h)) for h in heads]
    context = jnp.concatenate(parts, axis=1).astype(BF)
    ctx_ref[0] = context
    added = dot_nt(context, flat(held[slot, :, :, width:]))

    @pl.when(step == 0)
    def _():
        total[...] = x_ref[...].astype(F32) + rounded(vec_ref, BIAS_OUT) + added

    @pl.when(step > 0)
    def _():
        total[...] += added

    @pl.when(step == steps - 1)
    def _():
        norm_ref[...], inv_ref[...] = normed_rows(total[...])


def middle_rows(norm_ref, vec_ref):
    return norm_ref[...] * rounded(vec_ref, GAIN_ONE) + rounded(vec_ref, SHIFT_ONE)


def mlp_up_kernel(form, n, place, norm_ref, vec_ref, *refs):
    pieces = refs[:n]
    hid_ref, slope_ref, kept_ref = refs[n : n + 3]
    held, low_ref, sems, kept_sem = refs[n + 3 :]
    step = pl.program_id(0)
    slot = step
    own = place[place.shape[0] - 1]

    bring_weight(*weight_copies(form, 1, place, pieces, held, sems), step)
    keep_weight(held, kept_ref, kept_sem, step, pl.num_programs(0) - 1)

    @pl.when(step == 0)
    def _():
        low_ref[...] = middle_rows(norm_ref, vec_ref).astype(BF)

    bias = vec_ref[pl.ds(2 + (own ^ slot), 1), :].astype(BF).astype(F32)

    u = dot(low_ref[...], flat(held[slot])) + bias
    cdf = 0.5 + 0.5 * lax.erf(u * HALF_ROOT)
    hid_ref[0] = (u * cdf).astype(BF)
    slope_ref[0] = (cdf + u * (jnp.exp(u * u * -0.5) * PDF_SCALE)).astype(BF)


def mlp_down_kernel(form, n, outs, place, norm_ref, vec_ref, og_ref, ids_ref, hid_ref, *refs):
    pieces = refs[:n]
    out_ref, pool_ref, dres_ref, dlow_ref, sums_ref, kept_ref = refs[n : n + 6]
    grads = refs[n + 6 : n + 6 + outs]
    held, total, grad_low, sems, kept_sem = refs[n + 6 + outs :]
    step = pl.program_id(0)
    groups = held.shape[0]

    bring_weight(*weight_copies(form, 2, place, pieces, held, sems), step)
    keep_weight(held, kept_ref, kept_sem, step, 2 * groups - 1)

    @pl.when(step == 0)
    def _():
        total[...] = middle_rows(norm_ref, vec_ref) + rounded(vec_ref, BIAS_TWO)

    @pl.when(step < groups)
    def _():
        total[...] += dot_nt(hid_ref[0], flat(held[step]))

    @pl.when(step == groups - 1)
    def _():
        normed, inverse = normed_rows(total[...])
        gain = rounded(vec_ref, GAIN_TWO)
        final = normed * gain + rounded(vec_ref, SHIFT_TWO)
        high = final.astype(BF)
        out_ref[...] = high
        docs = pool_ref.shape[0] // SEGS
        for d in range(docs):
            slots = lax.broadcasted_iota(jnp.int32, (SEGS, SEQ), 0)
            onehot = jnp.where(slots == ids_ref[d : d + 1, :], 1.0, 0.0)
            counts = jnp.sum(onehot, axis=1, keepdims=True)
            marks = onehot.astype(BF)
            at = slice(d * SEQ, (d + 1) * SEQ)
            rest = (final[at] - high[at].astype(F32)).astype(BF)
            sums = dot(marks, high[at]) + dot(marks, rest)
            pool_ref[d * SEGS : (d + 1) * SEGS, :] = sums / jnp.maximum(counts, 1.0)
        cot = og_ref[...].astype(F32)
        dres = norm_back(cot, normed, inverse, gain)
        dres_ref[...] = dres
        low = dres.astype(BF)
        dlow_ref[...] = low
        sums_ref[0:1, :] = column_sum(dres)
        sums_ref[1:2, :] = column_sum(cot * normed)
        sums_ref[2:3, :] = column_sum(cot)

    @pl.when(step >= groups)
    def _():
        grad_low[...] = dot_tn(dlow_ref[...], hid_ref[0]).astype(BF).reshape(grad_low.shape)
        write_pieces(place, grad_low, grads)


def mlp_back_kernel(outs, place, norm_ref, vec_ref, dlow_ref, slope_ref, down_ref, *refs):
    dpre_ref, dbias_ref = refs[:2]
    grads = refs[2 : 2 + outs]
    low_ref, grad_low = refs[2 + outs :]
    slot = pl.program_id(0)
    own = place[place.shape[0] - 1]

    @pl.when(slot == 0)
    def _():
        low_ref[...] = middle_rows(norm_ref, vec_ref).astype(BF)

    dpre = (dot(dlow_ref[...], flat(down_ref[0])) * slope_ref[0].astype(F32)).astype(BF)
    dpre_ref[0] = dpre
    dbias_ref[pl.ds(own ^ slot, 1), :] = column_sum(dpre.astype(F32))
    grad_low[...] = dot_tn(low_ref[...], dpre).astype(BF).reshape(grad_low.shape)
    write_pieces(place, grad_low, grads)


def norm_back_kernel(place, norm_ref, inv_ref, vec_ref, dres_ref, dpre_ref, up_ref, *refs):
    dfirst_ref, dout_ref, sums_ref, total = refs
    slot = pl.program_id(0)
    added = dot_nt(dpre_ref[0], flat(up_ref[0]))

    @pl.when(slot == 0)
    def _():
        total[...] = dres_ref[...] + added

    @pl.when(slot > 0)
    def _():
        total[...] += added

    @pl.when(slot == pl.num_programs(0) - 1)
    def _():
        cot = total[...]
        normed = norm_ref[...]
        dfirst = norm_back(cot, normed, inv_ref[...], rounded(vec_ref, GAIN_ONE))
        dfirst_ref[...] = dfirst
        low = dfirst.astype(BF)
        dout_ref[...] = low
        sums_ref[0:1, :] = column_sum(dfirst)
        sums_ref[1:2, :] = column_sum(cot * normed)
        sums_ref[2:3, :] = column_sum(cot)


def attn_back_kernel(
    outs, groups, start, place, x_ref, dout_ref, qkv_ref, probs_ref, ctx_ref, weight_ref, *refs
):
    dqkv_ref, dbias_ref = refs[:2]
    grads = refs[2 : 2 + outs]
    grad_low = refs[2 + outs]
    step = pl.program_id(0)
    slot = (step + start) % groups
    own = place[place.shape[0] - 1]
    width = qkv_ref.shape[2]
    part = width // 3
    block = grad_low.shape[0:2]

    @pl.when(step == 0)
    def _():
        dbias_ref[...] = jnp.zeros_like(dbias_ref)

    context = ctx_ref[0]
    grad_out = dot_tn(dout_ref[...], context).astype(BF)
    grad_low[:, :, width:] = grad_out.reshape(block + (part,))
    dctx = dot(dout_ref[...], flat(weight_ref[0, :, :, width:])).astype(BF)
    dctx_t = dctx.T
    row_dots = dctx.astype(F32) * context.astype(F32)
    q_t = qkv_ref[0, :, 0:part].T
    dq, dk_t, dv_t = [], [], []
    for h in range(part // HEAD_DIM):
        at = slice(h * HEAD_DIM, (h + 1) * HEAD_DIM)
        k = qkv_ref[0, :, part + h * HEAD_DIM : part + (h + 1) * HEAD_DIM]
        v = qkv_ref[0, :, 2 * part + h * HEAD_DIM : 2 * part + (h + 1) * HEAD_DIM]
        probs = probs_ref[0, h]
        row_dot = jnp.sum(row_dots[:, at], axis=-1, keepdims=True)
        dprobs = dot_nt(dctx[:, at], v)
        dscores = (probs.astype(F32) * (dprobs - row_dot)).astype(BF)
        dv_t.append(dot(dctx_t[at], probs))
        dq.append(dot(dscores, k) * SCALE)
        dk_t.append(dot(q_t[at], dscores) * SCALE)
    dqkv = jnp.concatenate(
        [
            jnp.concatenate(dq, axis=1).astype(BF),
            jnp.concatenate(dk_t, axis=0).astype(BF).T,
            jnp.concatenate(dv_t, axis=0).astype(BF).T,
        ],
        axis=1,
    )
    dqkv_ref[0] = dqkv
    dbias = column_sum(dqkv.astype(F32))
    for z in range(dbias_ref.shape[1] // part):
        cols = slice(z * part, (z + 1) * part)
        mine = own ^ slot == z
        dbias_ref[0:1, cols] += jnp.where(mine, dbias[:, 0:part], 0.0)
        dbias_ref[1:2, cols] += jnp.where(mine, dbias[:, 2 * part :], 0.0)
    grad_low[:, :, 0:width] = dot_tn(x_ref[...], dqkv).astype(BF).reshape(block + (width,))
    write_pieces(place, grad_low, grads)


def input_grad_kernel(place, dfirst_ref, dqkv_ref, weight_ref, out_ref, total):
    slot = pl.program_id(0)
    width = dqkv_ref.shape[2]
    added = dot_nt(dqkv_ref[0], flat(weight_ref[0, :, :, 0:width]))

    @pl.when(slot == 0)
    def _():
        total[...] = dfirst_ref[...] + added

    @pl.when(slot > 0)
    def _():
        total[...] += added

    @pl.when(slot == pl.num_programs(0) - 1)
    def _():
        out_ref[...] = total[...].astype(out_ref.dtype)


def whole(shape):
    return pl.BlockSpec(shape, lambda i, place: (0,) * len(shape))


def by_slot(shape, index=lambda i: i):
    return pl.BlockSpec((1,) + shape, lambda i, place: (index(i),) + (0,) * len(shape))


def by_piece(shape, index=lambda i, place: i):
    return pl.BlockSpec(
        (shape[0], 1) + shape[2:], lambda i, place: (0, index(i, place)) + (0,) * len(shape[2:])
    )


ANY = pl.BlockSpec(memory_space=pltpu.HBM)
FREE = pl.BlockSpec(memory_space=pl.ANY)
VMEM_LIMIT = 28 * MIB


def pinned(value, spec, space=None):
    if space == "vmem":
        return pltpu.with_memory_space_constraint(value, pltpu.VMEM)
    if space == "hbm":
        return pltpu.with_memory_space_constraint(value, pltpu.HBM)
    return value


def placed(shape, dtype, space=None):
    if space == "vmem":
        return pltpu.VMEM(shape, dtype)
    if space == "hbm":
        return pltpu.HBM(shape, dtype)
    return jax.ShapeDtypeStruct(shape, dtype)


def call(kernel, name, grid, place, inputs, outputs, scratch, aliases=None):
    return pl.pallas_call(
        kernel,
        name=name,
        out_shape=[placed(out[0], out[1], *out[3:]) for out in outputs],
        grid_spec=pltpu.PrefetchScalarGridSpec(
            num_scalar_prefetch=1,
            grid=(grid,),
            in_specs=[given[1] for given in inputs],
            out_specs=[out[2] for out in outputs],
            scratch_shapes=scratch,
        ),
        compiler_params=pltpu.CompilerParams(
            dimension_semantics=("arbitrary",), vmem_limit_bytes=VMEM_LIMIT
        ),
        input_output_aliases=aliases or {},
        cost_estimate=pl.CostEstimate(flops=1000, bytes_accessed=1000, transcendentals=0),
    )(place, *[pinned(*given) for given in inputs])


def after(value, *deps):
    deps = [dep for dep in deps if dep is not None]
    return lax.optimization_barrier((value, *deps))[0] if deps else value


def after_all(values, *deps):
    return list(lax.optimization_barrier((*values, *deps)))[: len(values)]


def xor_pairs(count, mask):
    return [(i, i ^ mask) for i in range(count)]


class PlaneTransfers:
    forms = ("pieces", "pieces", "pieces")

    def __init__(self, tp_count):
        self.count = 8
        self.groups = tp_count
        self.first = [(i, i ^ (4 if i & 1 else 2)) for i in range(8)]
        self.second = [(i, i ^ (2 if i & 1 else 4)) for i in range(8)]
        self.cores = xor_pairs(8, 1)
        me = lax.axis_index("dp")
        one = jnp.where(me % 2 == 1, 4, 2)
        two = 6 - one
        self.place = jnp.stack(
            [
                me,
                me ^ one,
                me ^ two,
                me ^ 6,
                me ^ 1,
                me ^ 1 ^ two,
                me ^ 1 ^ one,
                me ^ 7,
                lax.axis_index("tp"),
            ]
        ).astype(jnp.int32)
        self.out_counts = (4, 2, 2)
        self.last_counts = (4, 4)

    def shifted(self, shard, mask):
        return lax.ppermute(shard, "tp", xor_pairs(self.groups, mask))

    def across(self, shard):
        return [self.shifted(shard, k) for k in range(1, self.groups)]

    def cores_of(self, mine):
        return [lax.ppermute(piece, "dp", self.cores) for piece in mine]

    def both(self, mine):
        return mine + [lax.ppermute(piece, "dp", self.cores) for piece in mine]

    def first_chip(self, shards):
        return lax.ppermute(shards, "dp", self.first)

    def second_chip(self, shards):
        return lax.ppermute(shards, "dp", self.second)

    def vec_step(self, vec, axis, mask):
        size = self.count if axis == "dp" else self.groups
        return vec + lax.ppermute(vec, axis, xor_pairs(size, mask))


    def swap_far(self, grads):
        return lax.ppermute(grads[2], "dp", self.cores)

    def swap_near(self, grads):
        return lax.ppermute(grads[1], "dp", self.cores)

    def pair_ready(self, grads, far):
        return (grads[0][2:4].astype(F32) + far.astype(F32)).astype(BF)

    def pair(self, sent):
        return lax.ppermute(sent, "dp", self.second)

    def near_ready(self, grads, other, pair):
        one = grads[0][1].astype(F32) + other[1].astype(F32) + pair[1].astype(F32)
        return one.astype(BF)

    def near(self, sent):
        return lax.ppermute(sent, "dp", self.first)

    def block(self, grads, other, pair, near):
        own = grads[0][0].astype(F32) + other[0].astype(F32)
        return own + pair[0].astype(F32) + near.astype(F32)


    def across_first(self, block):
        return self.shifted(jnp.stack([block[1], block[3]]).astype(BF), 1)

    def across_half(self, block, got):
        return block[0] + got[0].astype(F32), (block[2] + got[1].astype(F32)).astype(BF)

    def across_last(self, half):
        return self.shifted(half[1], 2)


class PlainTransfers:
    forms = ("one", "one", "one")

    def __init__(self, dp_count, tp_count):
        self.dp = dp_count
        self.tp = tp_count
        self.count = 1
        self.groups = tp_count
        self.place = jnp.zeros((2,), jnp.int32)
        self.out_counts = (1,)

    def one(self, shards):
        rows, columns = shards.shape
        out = lax.all_gather(shards, ("dp", "tp"), axis=0, tiled=False)
        out = out.reshape(self.dp, self.tp, rows, columns).transpose(1, 0, 2, 3)
        return [out.reshape(self.tp, self.dp * rows, columns)]

    def gather(self, attn, mlp):
        return self.one(attn), self.one(mlp[0]), self.one(mlp[1])

    def total(self, vec):
        return lax.psum(vec, ("dp", "tp"))

    def sum(self, grads):
        _, groups, rows, columns = grads[0].shape
        parts = grads[0].reshape(groups, self.dp, rows // self.dp, columns).transpose(1, 0, 2, 3)
        parts = parts.reshape(self.dp * groups, rows // self.dp, columns)
        out = lax.psum_scatter(parts, ("dp", "tp"), scatter_dimension=0, tiled=True)
        return out[0].astype(F32)


def on_device(
    tokens,
    out_grad,
    segment_ids,
    attn_master,
    attn_first,
    attn_second,
    mlp_master,
    mlp_first,
    mlp_second,
    vec_master,
    vec_first,
    vec_second,
):
    rows, width = tokens.shape
    dp_count = lax.axis_size("dp")
    groups = lax.axis_size("tp")
    mats, row_dev, col_dev = attn_master.shape
    hidden = mlp_master.shape[2]
    docs = rows // SEQ
    heads = col_dev // HEAD_DIM
    wide = 3 * col_dev
    cols = mats * col_dev
    plane = dp_count == 8 and groups == 4 and row_dev % 16 == 0
    moves = PlaneTransfers(groups) if plane else PlainTransfers(dp_count, groups)
    place = moves.place
    count = moves.count
    outs = len(moves.out_counts)
    block = width // count

    attn_low = jnp.concatenate([attn_master[k] for k in range(mats)], axis=1).astype(BF)
    vecs = vec_master.reshape(-1, width)
    mlp_low = mlp_master.astype(BF)
    forms = moves.forms

    full = (rows, width)
    row_vec = (rows, 1)
    weight = (groups, count, block, cols)
    hid_weight = (groups, count, block, hidden)
    slot_weight = by_slot((count, block, cols))
    slot_hid_weight = by_slot((count, block, hidden))
    slot_hid = by_slot((rows, hidden))
    slot_wide = by_slot((rows, wide))
    base = 2 * rows * width
    dma = pltpu.SemaphoreType.DMA
    vec_in = (vecs, whole(vecs.shape))

    def arriving(pieces):
        return [(piece, ANY, "hbm") for piece in pieces]

    def grad_outs(columns, base_step=0):
        def index(i, place):
            return jnp.maximum(i - base_step, 0)

        return [
            ((k, groups, block, columns), BF, by_piece((k, groups, block, columns), index), "hbm")
            for k in moves.out_counts
        ]

    def attn_forward(given, pieces):
        return call(
            functools.partial(attn_forward_kernel, forms[0], len(pieces)),
            "attn_forward",
            groups,
            place,
            [(given, whole(full)), vec_in] + arriving(pieces),
            [
                ((groups, rows, wide), BF, slot_wide, "hbm"),
                ((groups, heads, rows, rows), BF, by_slot((heads, rows, rows)), "hbm"),
                ((groups, rows, col_dev), BF, by_slot((rows, col_dev)), "hbm"),
                (weight, BF, ANY, "hbm"),
                (full, F32, whole(full), "vmem"),
                (row_vec, F32, whole(row_vec), "vmem"),
            ],
            [pltpu.VMEM(weight, BF), pltpu.VMEM(full, F32), dma((max(2 * count, groups),)), dma],
        )

    def mlp_up(given, pieces):
        return call(
            functools.partial(mlp_up_kernel, forms[1], len(pieces)),
            "mlp_up",
            groups,
            place,
            [(given, whole(full), "vmem"), vec_in] + arriving(pieces),
            [((groups, rows, hidden), BF, slot_hid, "hbm")] * 2 + [(hid_weight, BF, ANY, "hbm")],
            [pltpu.VMEM(hid_weight, BF), pltpu.VMEM(full, BF), dma((max(2 * count, groups),)), dma],
        )

    if plane:
        own = jnp.concatenate([attn_low[None], mlp_low])
        own_one, own_two = moves.first_chip(own), moves.second_chip(own)
        own_one, own_two, *attn_far = after_all((own_one, own_two, *moves.across(attn_low)))

        attn_far = jnp.stack(attn_far)
        attn_one = moves.first_chip(attn_far)
        own_three = moves.second_chip(own_one)
        up_far = moves.across(after(mlp_low[0], attn_far))
        attn_one, own_three, *up_far = after_all((attn_one, own_three, *up_far))

        attn_pair = moves.second_chip(jnp.stack([attn_far, attn_one]))
        up_far = jnp.stack(up_far)
        up_one = moves.first_chip(up_far)
        down_far = moves.across(after(mlp_low[1], up_far))
        attn_pair, up_one, *down_far = after_all((attn_pair, up_one, *down_far))

        up_sent = jnp.stack([up_far, up_one])
        up_pair = moves.second_chip(up_sent)
        down_far = jnp.stack(down_far)
        down_one = moves.first_chip(down_far)
        own_pieces = moves.both(after_all([own, own_one, own_two, own_three], attn_pair))
        attn_pieces = own_pieces + moves.both(after_all([attn_far, attn_one, attn_pair], attn_pair))
        qkv, probs, context, attn_kept, norm_one, inv_one = attn_forward(
            after(tokens, down_far), attn_pieces
        )
        up_swapped = moves.cores_of([up_far, up_one])
        norm_one, up_pair, down_one, *up_swapped = after_all(
            (norm_one, up_pair, down_one, *up_swapped)
        )

        down_sent = jnp.stack([down_far, down_one])
        down_pair = moves.second_chip(down_sent)
        up_pieces = own_pieces + [up_far, up_one, up_pair, *up_swapped, *moves.cores_of([up_pair])]
        down_swapped = moves.cores_of([after(down_far, norm_one), down_one])
        hid, slope, up_kept = mlp_up(after(norm_one, down_sent), up_pieces)
        hid, down_pair, *down_swapped = after_all((hid, down_pair, *down_swapped))
        down_pieces = own_pieces + [down_far, down_one, down_pair]
        down_pieces += down_swapped + moves.cores_of([down_pair])
    else:
        attn_pieces, up_pieces, down_pieces = moves.gather(attn_low, mlp_low)
        qkv, probs, context, attn_kept, norm_one, inv_one = attn_forward(tokens, attn_pieces)
        hid, slope, up_kept = mlp_up(norm_one, up_pieces)
    down_in = arriving(down_pieces)
    layer_out, pooled, dres, dres_low, sums_two, down_kept, *down_grads = call(
        functools.partial(mlp_down_kernel, forms[2], len(down_in), outs),
        "mlp_down",
        2 * groups,
        place,
        [
            (norm_one, whole(full), "vmem"),
            vec_in,
            (out_grad, whole(full)),
            (segment_ids.reshape(docs, SEQ), whole((docs, SEQ))),
            (hid, by_slot((rows, hidden), lambda i: i % groups), "hbm"),
        ]
        + down_in,
        [
            (full, BF, whole(full)),
            ((docs * SEGS, width), F32, whole((docs * SEGS, width))),
            (full, F32, whole(full), "vmem"),
            (full, BF, whole(full), "vmem"),
            ((3, width), F32, whole((3, width))),
            (hid_weight, BF, ANY, "hbm"),
        ]
        + grad_outs(hidden, groups),
        [
            pltpu.VMEM(hid_weight, BF),
            pltpu.VMEM(full, F32),
            pltpu.VMEM((count, block, hidden), BF),
            dma((max(2 * count, groups),)),
            dma,
        ],
    )
    down_far = moves.swap_far(down_grads) if plane else None
    down_other = moves.swap_near(down_grads) if plane else None
    dpre, dbias_hidden, *up_grads = call(
        functools.partial(mlp_back_kernel, outs),
        "mlp_back",
        groups,
        place,
        [
            (norm_one, whole(full), "vmem"),
            vec_in,
            (dres_low, whole(full), "vmem"),
            (slope, slot_hid, "hbm"),
            (down_kept, slot_hid_weight, "hbm"),
        ],
        [
            ((groups, rows, hidden), BF, slot_hid, "vmem"),
            ((groups, hidden), F32, whole((groups, hidden))),
        ]
        + grad_outs(hidden),
        [pltpu.VMEM(full, BF), pltpu.VMEM((count, block, hidden), BF)],
    )
    if plane:
        down_sent = moves.pair_ready(down_grads, down_far)
        dres = after(dres, down_sent)
        down_pair = moves.pair(down_sent)
        up_far = moves.swap_far(up_grads)
        up_other = moves.swap_near(up_grads)
    dfirst, dout, sums_one = call(
        norm_back_kernel,
        "norm_back",
        groups,
        place,
        [
            (norm_one, whole(full), "vmem"),
            (inv_one, whole(row_vec), "vmem"),
            vec_in,
            (dres, whole(full), "vmem"),
            (dpre, slot_hid, "vmem"),
            (up_kept, slot_hid_weight, "hbm"),
        ],
        [
            (full, F32, whole(full), "vmem"),
            (full, BF, whole(full), "vmem"),
            ((3, width), F32, whole((3, width))),
        ],
        [pltpu.VMEM(full, F32)],
    )
    def attn_back(start, slots, dout, counts=moves.out_counts):
        def shifted(shape):
            return by_slot(shape, lambda i: (i + start) % groups)

        outputs = [
            ((slots, rows, wide), BF, slot_wide, "hbm"),
            ((2, width), F32, whole((2, width))),
        ]
        for k in counts:
            shape = (k, slots, block, cols)
            outputs.append((shape, BF, by_piece(shape), "hbm"))
        inputs = [
            (tokens, whole(full)),
            (dout, whole(full), "vmem"),
            (qkv, shifted((rows, wide)), "hbm"),
            (probs, shifted((heads, rows, rows)), "hbm"),
            (context, shifted((rows, col_dev)), "hbm"),
            (attn_kept, shifted((count, block, cols)), "hbm"),
        ]
        return call(
            functools.partial(attn_back_kernel, len(counts), groups, start),
            "attn_back",
            slots,
            place,
            inputs,
            outputs,
            [pltpu.VMEM((count, block, cols), BF)],
        )

    def vec_grads(dbias_qv):
        return jnp.concatenate(
            [
                dbias_qv,
                dbias_hidden,
                sums_one[0:1],
                sums_two[0:1],
                sums_one[1:3],
                sums_two[1:3],
            ],
            axis=0,
        )

    if plane:
        dout, up_far = after_all((dout, up_far))
        up_sent = moves.pair_ready(up_grads, up_far)
        up_pair = moves.pair(up_sent)
        half = groups // 2
        dqkv_a, dbias_a, *a_grads = attn_back(half, half, after(dout, up_sent))
        dbias_a, down_pair, down_other, *a_grads = after_all(
            (dbias_a, down_pair, down_other, *a_grads)
        )

        down_near_sent = moves.near_ready(down_grads, down_other, down_pair)
        down_near = moves.near(down_near_sent)
        a_far = moves.swap_far(a_grads)
        a_other = moves.swap_near(a_grads)
        dqkv_b, dbias_b, *b_grads = attn_back(
            0, half, after(dout, down_near_sent), moves.last_counts
        )
        dbias_b, down_near, up_pair, up_other, a_far, a_other, *b_grads = after_all(
            (dbias_b, down_near, up_pair, up_other, a_far, a_other, *b_grads)
        )

        b_other = moves.swap_near(b_grads)
        up_near_sent = moves.near_ready(up_grads, up_other, up_pair)
        up_near = moves.near(up_near_sent)
        a_sent = moves.pair_ready(a_grads, a_far)
        a_pair = moves.pair(a_sent)
        down_block = moves.block(down_grads, down_other, down_pair, down_near)
        down_got = moves.across_first(down_block)
        vec_one = moves.vec_step(vec_grads(dbias_a + dbias_b), "dp", 1)
        dfirst = after(dfirst, up_near_sent, a_sent, down_block)
    else:
        dqkv_a, dbias_qv, *a_grads = attn_back(0, groups, dout)

    def input_part(given, part, start, space):
        slots = part.shape[0]
        out = (full, F32, whole(full), space) if space else (full, BF, whole(full))
        return call(
            input_grad_kernel,
            "input_grad",
            slots,
            place,
            [
                (given, whole(full), "vmem"),
                (part, slot_wide, "hbm"),
                (attn_kept, by_slot((count, block, cols), lambda i: (i + start) % groups), "hbm"),
            ],
            [out],
            [pltpu.VMEM(full, F32)],
        )[0]

    if plane:
        input_grad = input_part(dfirst, dqkv_a, half, "vmem")
        input_grad, vec_one = after_all((input_grad, vec_one))
        vec_two = moves.vec_step(vec_one, "tp", 1)
        input_grad = input_part(input_grad, dqkv_b, 0, None)
        input_grad, b_other, up_near, down_got, vec_two = after_all(
            (input_grad, b_other, up_near, down_got, vec_two)
        )

        b_sent = moves.pair_ready(b_grads, b_other[2:4])
        b_pair = moves.pair(b_sent)
        up_block = moves.block(up_grads, up_other, up_pair, up_near)
        up_got = moves.across_first(up_block)
        down_half = moves.across_half(down_block, down_got)
        down_got = moves.across_last(down_half)
        vec_three = moves.vec_step(vec_two, "tp", 2)
        a_pair = after(a_pair, b_sent, up_block)
        a_near_sent = moves.near_ready(a_grads, a_other, a_pair)
        a_near = moves.near(a_near_sent)
        a_near, b_pair, up_got, down_got, vec_three = after_all(
            (a_near, b_pair, up_got, down_got, vec_three)
        )

        b_near_sent = moves.near_ready(b_grads, b_other, b_pair)
        b_near = moves.near(b_near_sent)
        a_block = moves.block(a_grads, a_other, a_pair, after(a_near, b_near_sent))
        a_got = moves.shifted(a_block[1].astype(BF), 1)
        up_half = moves.across_half(up_block, up_got)
        up_got = moves.across_last(up_half)
        vec_four = moves.vec_step(vec_three, "dp", 2)
        b_near, a_got, vec_four = after_all((b_near, a_got, vec_four), *up_half)

        a_half = (a_block[0] + a_got.astype(F32)).astype(BF)
        a_got = moves.shifted(a_half, 2)
        b_block = moves.block(b_grads, b_other, b_pair, b_near)
        b_part = moves.shifted(b_block[1].astype(BF), 1)
        vec_grad = moves.vec_step(after(vec_four, a_half, b_block), "dp", 4).reshape(-1)
        up_got, vec_grad = after_all((up_got, vec_grad))
        down_sum = down_half[0] + down_got.astype(F32)
        up_sum = up_half[0] + up_got.astype(F32)
        attn_sum = b_block[0]
        for part in (a_got, b_part):
            attn_sum = attn_sum + part.astype(F32)
    else:
        input_grad = input_part(dfirst, dqkv_a, 0, None)
        down_sum, up_sum, attn_sum = (moves.sum(part) for part in (down_grads, up_grads, a_grads))
        vec_grad = moves.total(vec_grads(dbias_qv)).reshape(-1)
    attn_grad = jnp.stack([attn_sum[:, k * col_dev : (k + 1) * col_dev] for k in range(mats)])
    mlp_grad = jnp.stack([up_sum, down_sum])
    attn_step = adam_update(
        attn_master, attn_first, attn_second, attn_grad, MATRIX_RATE, MATRIX_DECAY
    )
    mlp_step = adam_update(mlp_master, mlp_first, mlp_second, mlp_grad, MATRIX_RATE, MATRIX_DECAY)
    vec_step = adam_update(vec_master, vec_first, vec_second, vec_grad, VECTOR_RATE, 0.0)
    return (layer_out, pooled, input_grad, *attn_step, *mlp_step, *vec_step)


def solution(mesh):
    in_specs = (
        P(("dp", "tp"), None),
        P(("dp", "tp"), None),
        P(("dp", "tp")),
        P(None, "dp", "tp"),
        P(None, "dp", "tp"),
        P(None, "dp", "tp"),
        P(None, "dp", "tp"),
        P(None, "dp", "tp"),
        P(None, "dp", "tp"),
        P(),
        P(),
        P(),
    )
    out_specs = (
        P(("dp", "tp"), None),
        P(("dp", "tp"), None),
        P(("dp", "tp"), None),
        P(None, "dp", "tp"),
        P(None, "dp", "tp"),
        P(None, "dp", "tp"),
        P(None, "dp", "tp"),
        P(None, "dp", "tp"),
        P(None, "dp", "tp"),
        P(None, "dp", "tp"),
        P(None, "dp", "tp"),
        P(),
        P(),
        P(),
        P(),
    )
    return jax.shard_map(
        on_device, mesh=mesh, in_specs=in_specs, out_specs=out_specs, check_vma=False
    )
```

```python
import functools

import jax
import jax.numpy as jnp
from jax import lax
from jax.experimental import pallas as pl
from jax.experimental.pallas import tpu as pltpu
from jax.sharding import PartitionSpec as P

HEAD_DIM = 64
SEQ = 512
SEGS = 128
STEP = 10


NORM_EPS = 1e-12
BETA_ONE = 0.9
BETA_TWO = 0.999
ADAM_EPS = 1e-06
MATRIX_RATE = 0.1
VECTOR_RATE = 0.3
MATRIX_DECAY = 0.01
SCALE = HEAD_DIM ** (-0.5)
HALF_ROOT = 0.7071067811865476
PDF_SCALE = 0.3989422804014327
NT = (((1,), (1,)), ((), ()))
TN = (((0,), (0,)), ((), ()))
BF = jnp.bfloat16
F32 = jnp.float32
MIB = 1 << 20
ROW_PART = 128
BIAS_OUT, BIAS_TWO, GAIN_ONE, SHIFT_ONE, GAIN_TWO, SHIFT_TWO = range(-6, 0)


def dot(left, right):
    return jnp.dot(left, right, preferred_element_type=F32)


def dot_tn(left, right):
    return lax.dot_general(left, right, TN, preferred_element_type=F32)


def dot_nt(left, right):
    return lax.dot_general(left, right, NT, preferred_element_type=F32)


def adam_update(weight, moment_one, moment_two, gradient, step_rate, decay_rate):
    first_new = BETA_ONE * moment_one + (1.0 - BETA_ONE) * gradient
    second_new = BETA_TWO * moment_two + (1.0 - BETA_TWO) * gradient * gradient
    fix_one = 1.0 - BETA_ONE**STEP
    fix_two = 1.0 - BETA_TWO**STEP
    direction = first_new / fix_one / (jnp.sqrt(second_new / fix_two) + ADAM_EPS)
    weight_new = weight - step_rate * (direction + decay_rate * weight)
    return (first_new, second_new, weight_new, weight_new.astype(BF))


def split_blocks(pieces):
    blocks = []
    for piece in pieces:
        blocks += [piece.at[k] for k in range(piece.shape[0])] if len(piece.shape) == 4 else [piece]
    return blocks


def weight_copies(form, first, place, pieces, held, sems):
    groups, count = held.shape[0], held.shape[1]
    if form == "one":
        return [
            pltpu.make_async_copy(pieces[0].at[k], held.at[k, 0], sems.at[k]) for k in range(groups)
        ], 1
    near = [
        pltpu.make_async_copy(piece.at[first], held.at[0, place[j]], sems.at[j])
        for j, piece in enumerate(pieces[:count])
    ]
    far = [
        pltpu.make_async_copy(piece, held.at[pl.ds(1, groups - 1), place[j]], sems.at[count + j])
        for j, piece in enumerate(split_blocks(pieces[count:]))
    ]
    return near + far, count


def start_weight(copies, step):
    @pl.when(step == 0)
    def _():
        for copy in copies:
            copy.start()


def wait_weight(copies, first_part, step):
    @pl.when(step == 0)
    def _():
        for copy in copies[:first_part]:
            copy.wait()

    @pl.when(step == 1)
    def _():
        for copy in copies[first_part:]:
            copy.wait()


def keep_weight(held, out, sem, step, last):
    copy = pltpu.make_async_copy(held, out, sem)
    pl.when(step == 1)(copy.start)
    pl.when(step == last)(copy.wait)


def flat(value):
    return value.reshape(value.shape[0] * value.shape[1], value.shape[2])


def rounded(vec_ref, row):
    at = row % vec_ref.shape[0]
    return vec_ref[at : at + 1, :].astype(BF).astype(F32)


def own_part(row, own, size):
    out = row[:, 0:size]
    for k in range(1, row.shape[1] // size):
        out = jnp.where(own == k, row[:, k * size : (k + 1) * size], out)
    return out


def write_pieces(place, grad, outs):
    j = 0
    for out in outs:
        for k in range(out.shape[0]):
            out[k, 0] = grad[place[j]]
            j += 1


def normed_rows(value):
    centred = value - jnp.mean(value, axis=-1, keepdims=True)
    inverse = lax.rsqrt(jnp.mean(centred * centred, axis=-1, keepdims=True) + NORM_EPS)
    return centred * inverse, inverse


def norm_back(cot, normed, inverse, gain):
    scaled = cot * gain
    mean_one = jnp.mean(scaled, axis=-1, keepdims=True)
    mean_two = jnp.mean(scaled * normed, axis=-1, keepdims=True)
    return (scaled - mean_one - normed * mean_two) * inverse


def column_sum(value):
    return jnp.sum(value, axis=0, keepdims=True)


def attn_forward_kernel(form, n, place, x_ref, vec_ref, *refs):
    pieces = refs[:n]
    qkv_ref, probs_ref, ctx_ref, kept_ref, norm_ref, inv_ref = refs[n : n + 6]
    held, total, sems, kept_sem = refs[n + 6 :]
    slot = step = pl.program_id(0)
    steps = pl.num_programs(0)
    own = place[place.shape[0] - 1]
    width = qkv_ref.shape[2]
    part = width // 3

    copies, first_part = weight_copies(form, 0, place, pieces, held, sems)
    start_weight(copies, step)

    @pl.when(step == 0)
    def _():
        total[...] = x_ref[...].astype(F32) + rounded(vec_ref, BIAS_OUT)

    wait_weight(copies, first_part, step)
    keep_weight(held, kept_ref, kept_sem, step, steps - 1)
    bias_q = own_part(rounded(vec_ref, 0), own ^ slot, part)
    bias_v = own_part(rounded(vec_ref, 1), own ^ slot, part)
    bias = jnp.concatenate([bias_q, jnp.zeros_like(bias_q), bias_v], axis=1)
    projected = dot(x_ref[...], flat(held[slot, :, :, 0:width])) + bias
    low = projected.astype(BF)
    qkv_ref[0] = low
    heads = range(part // HEAD_DIM)

    def head(k, h):
        return low[:, k * part + h * HEAD_DIM : k * part + (h + 1) * HEAD_DIM]

    scores = [dot_nt(head(0, h) * BF(SCALE), head(1, h)) for h in heads]
    for h in heads:
        expanded = jnp.exp(scores[h] - jnp.max(scores[h], axis=-1, keepdims=True))
        inverse = 1.0 / jnp.sum(expanded, axis=-1, keepdims=True)
        probs_ref[0, h] = (expanded * inverse).astype(BF)
    parts = [dot(probs_ref[0, h], head(2, h)) for h in heads]
    context = jnp.concatenate(parts, axis=1).astype(BF)
    ctx_ref[0] = context
    added = dot_nt(context, flat(held[slot, :, :, width:]))

    total[...] += added

    @pl.when(step == steps - 1)
    def _():
        norm_ref[...], inv_ref[...] = normed_rows(total[...])


def middle_rows(norm_ref, vec_ref):
    return norm_ref[...] * rounded(vec_ref, GAIN_ONE) + rounded(vec_ref, SHIFT_ONE)


def mlp_up_kernel(form, n, place, norm_ref, vec_ref, *refs):
    pieces = refs[:n]
    hid_ref, slope_ref, kept_ref = refs[n : n + 3]
    held, low_ref, sems, kept_sem = refs[n + 3 :]
    step = pl.program_id(0)
    slot = step
    own = place[place.shape[0] - 1]

    copies, first_part = weight_copies(form, 1, place, pieces, held, sems)
    start_weight(copies, step)

    @pl.when(step == 0)
    def _():
        low_ref[...] = middle_rows(norm_ref, vec_ref).astype(BF)

    wait_weight(copies, first_part, step)
    keep_weight(held, kept_ref, kept_sem, step, pl.num_programs(0) - 1)

    bias = vec_ref[pl.ds(2 + (own ^ slot), 1), :].astype(BF).astype(F32)

    weight = flat(held[slot])
    for start in range(0, low_ref.shape[0], ROW_PART):
        at = slice(start, start + ROW_PART)
        u = dot(low_ref[at, :], weight) + bias
        cdf = 0.5 + 0.5 * lax.erf(u * HALF_ROOT)
        hid_ref[0, at, :] = (u * cdf).astype(BF)
        slope_ref[0, at, :] = (cdf + u * (jnp.exp(u * u * -0.5) * PDF_SCALE)).astype(BF)


def mlp_down_kernel(form, n, outs, place, norm_ref, vec_ref, og_ref, ids_ref, hid_ref, *refs):
    pieces = refs[:n]
    out_ref, pool_ref, dres_ref, dlow_ref, sums_ref, kept_ref = refs[n : n + 6]
    grads = refs[n + 6 : n + 6 + outs]
    held, total, grad_low, sems, kept_sem = refs[n + 6 + outs :]
    step = pl.program_id(0)
    groups = held.shape[0]

    copies, first_part = weight_copies(form, 2, place, pieces, held, sems)
    start_weight(copies, step)

    @pl.when(step == 0)
    def _():
        total[...] = middle_rows(norm_ref, vec_ref) + rounded(vec_ref, BIAS_TWO)

    wait_weight(copies, first_part, step)
    keep_weight(held, kept_ref, kept_sem, step, 2 * groups - 1)

    @pl.when(step < groups)
    def _():
        total[...] += dot_nt(hid_ref[0], flat(held[step]))

    @pl.when(step == groups - 1)
    def _():
        normed, inverse = normed_rows(total[...])
        gain = rounded(vec_ref, GAIN_TWO)
        final = normed * gain + rounded(vec_ref, SHIFT_TWO)
        high = final.astype(BF)
        out_ref[...] = high
        docs = pool_ref.shape[0] // SEGS
        for d in range(docs):
            slots = lax.broadcasted_iota(jnp.int32, (SEGS, SEQ), 0)
            onehot = jnp.where(slots == ids_ref[d : d + 1, :], 1.0, 0.0)
            counts = jnp.sum(onehot, axis=1, keepdims=True)
            marks = onehot.astype(BF)
            at = slice(d * SEQ, (d + 1) * SEQ)
            rest = (final[at] - high[at].astype(F32)).astype(BF)
            sums = dot(marks, high[at]) + dot(marks, rest)
            pool_ref[d * SEGS : (d + 1) * SEGS, :] = sums / jnp.maximum(counts, 1.0)
        cot = og_ref[...].astype(F32)
        dres = norm_back(cot, normed, inverse, gain)
        dres_ref[...] = dres
        low = dres.astype(BF)
        dlow_ref[...] = low
        sums_ref[0:1, :] = column_sum(dres)
        sums_ref[1:2, :] = column_sum(cot * normed)
        sums_ref[2:3, :] = column_sum(cot)

    @pl.when(step >= groups)
    def _():
        grad_low[...] = dot_tn(dlow_ref[...], hid_ref[0]).astype(BF).reshape(grad_low.shape)
        write_pieces(place, grad_low, grads)


def mlp_back_kernel(outs, place, norm_ref, vec_ref, dlow_ref, slope_ref, down_ref, *refs):
    dpre_ref, dbias_ref = refs[:2]
    grads = refs[2 : 2 + outs]
    low_ref, grad_low = refs[2 + outs :]
    slot = pl.program_id(0)
    own = place[place.shape[0] - 1]

    @pl.when(slot == 0)
    def _():
        low_ref[...] = middle_rows(norm_ref, vec_ref).astype(BF)

    dpre = (dot(dlow_ref[...], flat(down_ref[0])) * slope_ref[0].astype(F32)).astype(BF)
    dpre_ref[0] = dpre
    dbias_ref[pl.ds(own ^ slot, 1), :] = column_sum(dpre.astype(F32))
    grad_low[...] = dot_tn(low_ref[...], dpre).astype(BF).reshape(grad_low.shape)
    write_pieces(place, grad_low, grads)


def norm_back_kernel(place, norm_ref, inv_ref, vec_ref, dres_ref, dpre_ref, up_ref, *refs):
    dfirst_ref, dout_ref, sums_ref, total = refs
    slot = pl.program_id(0)
    added = dot_nt(dpre_ref[0], flat(up_ref[0]))

    @pl.when(slot == 0)
    def _():
        total[...] = dres_ref[...] + added

    @pl.when(slot > 0)
    def _():
        total[...] += added

    @pl.when(slot == pl.num_programs(0) - 1)
    def _():
        cot = total[...]
        normed = norm_ref[...]
        dfirst = norm_back(cot, normed, inv_ref[...], rounded(vec_ref, GAIN_ONE))
        dfirst_ref[...] = dfirst
        low = dfirst.astype(BF)
        dout_ref[...] = low
        sums_ref[0:1, :] = column_sum(dfirst)
        sums_ref[1:2, :] = column_sum(cot * normed)
        sums_ref[2:3, :] = column_sum(cot)


def attn_back_kernel(
    outs, groups, start, place, x_ref, dout_ref, qkv_ref, probs_ref, ctx_ref, weight_ref, *refs
):
    dqkv_ref, dbias_ref = refs[:2]
    grads = refs[2 : 2 + outs]
    grad_low = refs[2 + outs]
    step = pl.program_id(0)
    slot = (step + start) % groups
    own = place[place.shape[0] - 1]
    width = qkv_ref.shape[2]
    part = width // 3
    block = grad_low.shape[0:2]

    @pl.when(step == 0)
    def _():
        dbias_ref[...] = jnp.zeros_like(dbias_ref)

    context = ctx_ref[0]
    grad_out = dot_tn(dout_ref[...], context).astype(BF)
    grad_low[:, :, width:] = grad_out.reshape(block + (part,))
    dctx = dot(dout_ref[...], flat(weight_ref[0, :, :, width:])).astype(BF)
    dctx_t = dctx.T
    row_dots = dctx.astype(F32) * context.astype(F32)
    q_t = qkv_ref[0, :, 0:part].T
    dq, dk_t, dv_t = [], [], []
    for h in range(part // HEAD_DIM):
        at = slice(h * HEAD_DIM, (h + 1) * HEAD_DIM)
        k = qkv_ref[0, :, part + h * HEAD_DIM : part + (h + 1) * HEAD_DIM]
        v = qkv_ref[0, :, 2 * part + h * HEAD_DIM : 2 * part + (h + 1) * HEAD_DIM]
        probs = probs_ref[0, h]
        row_dot = jnp.sum(row_dots[:, at], axis=-1, keepdims=True)
        dprobs = dot_nt(dctx[:, at], v)
        dscores = (probs.astype(F32) * (dprobs - row_dot)).astype(BF)
        dv_t.append(dot(dctx_t[at], probs))
        dq.append(dot(dscores, k) * SCALE)
        dk_t.append(dot(q_t[at], dscores) * SCALE)
    dqkv = jnp.concatenate(
        [
            jnp.concatenate(dq, axis=1).astype(BF),
            jnp.concatenate(dk_t, axis=0).astype(BF).T,
            jnp.concatenate(dv_t, axis=0).astype(BF).T,
        ],
        axis=1,
    )
    dqkv_ref[0] = dqkv
    dbias = column_sum(dqkv.astype(F32))
    for z in range(dbias_ref.shape[1] // part):
        cols = slice(z * part, (z + 1) * part)
        mine = own ^ slot == z
        dbias_ref[0:1, cols] += jnp.where(mine, dbias[:, 0:part], 0.0)
        dbias_ref[1:2, cols] += jnp.where(mine, dbias[:, 2 * part :], 0.0)
    grad_low[:, :, 0:width] = dot_tn(x_ref[...], dqkv).astype(BF).reshape(block + (width,))
    write_pieces(place, grad_low, grads)


def input_grad_kernel(place, dfirst_ref, dqkv_ref, weight_ref, out_ref, total):
    slot = pl.program_id(0)
    width = dqkv_ref.shape[2]
    added = dot_nt(dqkv_ref[0], flat(weight_ref[0, :, :, 0:width]))

    @pl.when(slot == 0)
    def _():
        total[...] = dfirst_ref[...] + added

    @pl.when(slot > 0)
    def _():
        total[...] += added

    @pl.when(slot == pl.num_programs(0) - 1)
    def _():
        out_ref[...] = total[...].astype(out_ref.dtype)


def whole(shape):
    return pl.BlockSpec(shape, lambda i, place: (0,) * len(shape))


def by_slot(shape, index=lambda i: i):
    return pl.BlockSpec((1,) + shape, lambda i, place: (index(i),) + (0,) * len(shape))


def by_piece(shape, index=lambda i, place: i):
    return pl.BlockSpec(
        (shape[0], 1) + shape[2:], lambda i, place: (0, index(i, place)) + (0,) * len(shape[2:])
    )


ANY = pl.BlockSpec(memory_space=pltpu.HBM)
FREE = pl.BlockSpec(memory_space=pl.ANY)
VMEM_LIMIT = 28 * MIB


def pinned(value, spec, space=None):
    if space == "vmem":
        return pltpu.with_memory_space_constraint(value, pltpu.VMEM)
    if space == "hbm":
        return pltpu.with_memory_space_constraint(value, pltpu.HBM)
    return value


def placed(shape, dtype, space=None):
    if space == "vmem":
        return pltpu.VMEM(shape, dtype)
    if space == "hbm":
        return pltpu.HBM(shape, dtype)
    return jax.ShapeDtypeStruct(shape, dtype)


def call(kernel, name, grid, place, inputs, outputs, scratch, aliases=None):
    return pl.pallas_call(
        kernel,
        name=name,
        out_shape=[placed(out[0], out[1], *out[3:]) for out in outputs],
        grid_spec=pltpu.PrefetchScalarGridSpec(
            num_scalar_prefetch=1,
            grid=(grid,),
            in_specs=[given[1] for given in inputs],
            out_specs=[out[2] for out in outputs],
            scratch_shapes=scratch,
        ),
        compiler_params=pltpu.CompilerParams(
            dimension_semantics=("arbitrary",), vmem_limit_bytes=VMEM_LIMIT
        ),
        input_output_aliases=aliases or {},
        cost_estimate=pl.CostEstimate(flops=1000, bytes_accessed=1000, transcendentals=0),
    )(place, *[pinned(*given) for given in inputs])


def after(value, *deps):
    deps = [dep for dep in deps if dep is not None]
    return lax.optimization_barrier((value, *deps))[0] if deps else value


def after_all(values, *deps):
    return list(lax.optimization_barrier((*values, *deps)))[: len(values)]


def xor_pairs(count, mask):
    return [(i, i ^ mask) for i in range(count)]


class PlaneTransfers:
    forms = ("pieces", "pieces", "pieces")

    def __init__(self, tp_count):
        self.count = 8
        self.groups = tp_count
        self.first = [(i, i ^ (4 if i & 1 else 2)) for i in range(8)]
        self.second = [(i, i ^ (2 if i & 1 else 4)) for i in range(8)]
        self.cores = xor_pairs(8, 1)
        me = lax.axis_index("dp")
        one = jnp.where(me % 2 == 1, 4, 2)
        two = 6 - one
        self.place = jnp.stack(
            [
                me,
                me ^ one,
                me ^ two,
                me ^ 6,
                me ^ 1,
                me ^ 1 ^ two,
                me ^ 1 ^ one,
                me ^ 7,
                lax.axis_index("tp"),
            ]
        ).astype(jnp.int32)
        self.out_counts = (4, 2, 2)
        self.last_counts = (4, 4)

    def shifted(self, shard, mask):
        return lax.ppermute(shard, "tp", xor_pairs(self.groups, mask))

    def across(self, shard):
        return [self.shifted(shard, k) for k in range(1, self.groups)]

    def cores_of(self, mine):
        return [lax.ppermute(piece, "dp", self.cores) for piece in mine]

    def both(self, mine):
        return mine + [lax.ppermute(piece, "dp", self.cores) for piece in mine]

    def first_chip(self, shards):
        return lax.ppermute(shards, "dp", self.first)

    def second_chip(self, shards):
        return lax.ppermute(shards, "dp", self.second)

    def vec_step(self, vec, axis, mask):
        size = self.count if axis == "dp" else self.groups
        return vec + lax.ppermute(vec, axis, xor_pairs(size, mask))


    def swap_far(self, grads):
        return lax.ppermute(grads[2], "dp", self.cores)

    def swap_near(self, grads):
        return lax.ppermute(grads[1], "dp", self.cores)

    def pair_ready(self, grads, far):
        return (grads[0][2:4].astype(F32) + far.astype(F32)).astype(BF)

    def pair(self, sent):
        return lax.ppermute(sent, "dp", self.second)

    def near_ready(self, grads, other, pair):
        one = grads[0][1].astype(F32) + other[1].astype(F32) + pair[1].astype(F32)
        return one.astype(BF)

    def near(self, sent):
        return lax.ppermute(sent, "dp", self.first)

    def own_ready(self, grads, other, pair):
        return grads[0][0].astype(F32) + other[0].astype(F32) + pair[0].astype(F32)

    def block(self, grads, other, pair, near):
        return self.own_ready(grads, other, pair) + near.astype(F32)


    def across_first(self, block):
        return self.shifted(jnp.stack([block[1], block[3]]).astype(BF), 1)

    def across_half(self, block, got):
        return block[0] + got[0].astype(F32), (block[2] + got[1].astype(F32)).astype(BF)

    def across_last(self, half):
        return self.shifted(half[1], 2)


class PlainTransfers:
    forms = ("one", "one", "one")

    def __init__(self, dp_count, tp_count):
        self.dp = dp_count
        self.tp = tp_count
        self.count = 1
        self.groups = tp_count
        self.place = jnp.zeros((2,), jnp.int32)
        self.out_counts = (1,)

    def one(self, shards):
        rows, columns = shards.shape
        out = lax.all_gather(shards, ("dp", "tp"), axis=0, tiled=False)
        out = out.reshape(self.dp, self.tp, rows, columns).transpose(1, 0, 2, 3)
        return [out.reshape(self.tp, self.dp * rows, columns)]

    def gather(self, attn, mlp):
        return self.one(attn), self.one(mlp[0]), self.one(mlp[1])

    def total(self, vec):
        return lax.psum(vec, ("dp", "tp"))

    def sum(self, grads):
        _, groups, rows, columns = grads[0].shape
        parts = grads[0].reshape(groups, self.dp, rows // self.dp, columns).transpose(1, 0, 2, 3)
        parts = parts.reshape(self.dp * groups, rows // self.dp, columns)
        out = lax.psum_scatter(parts, ("dp", "tp"), scatter_dimension=0, tiled=True)
        return out[0].astype(F32)


def on_device(
    tokens,
    out_grad,
    segment_ids,
    attn_master,
    attn_first,
    attn_second,
    mlp_master,
    mlp_first,
    mlp_second,
    vec_master,
    vec_first,
    vec_second,
):
    rows, width = tokens.shape
    dp_count = lax.axis_size("dp")
    groups = lax.axis_size("tp")
    mats, row_dev, col_dev = attn_master.shape
    hidden = mlp_master.shape[2]
    docs = rows // SEQ
    heads = col_dev // HEAD_DIM
    wide = 3 * col_dev
    cols = mats * col_dev
    plane = dp_count == 8 and groups == 4 and row_dev % 16 == 0
    moves = PlaneTransfers(groups) if plane else PlainTransfers(dp_count, groups)
    place = moves.place
    count = moves.count
    outs = len(moves.out_counts)
    block = width // count

    attn_low = jnp.concatenate([attn_master[k] for k in range(mats)], axis=1).astype(BF)
    vecs = vec_master.reshape(-1, width)
    mlp_low = mlp_master.astype(BF)
    forms = moves.forms

    full = (rows, width)
    row_vec = (rows, 1)
    weight = (groups, count, block, cols)
    hid_weight = (groups, count, block, hidden)
    slot_weight = by_slot((count, block, cols))
    slot_hid_weight = by_slot((count, block, hidden))
    slot_hid = by_slot((rows, hidden))
    slot_wide = by_slot((rows, wide))
    base = 2 * rows * width
    dma = pltpu.SemaphoreType.DMA
    vec_in = (vecs, whole(vecs.shape))

    def arriving(pieces):
        return [(piece, ANY, "hbm") for piece in pieces]

    def grad_outs(columns, base_step=0):
        def index(i, place):
            return jnp.maximum(i - base_step, 0)

        return [
            ((k, groups, block, columns), BF, by_piece((k, groups, block, columns), index), "hbm")
            for k in moves.out_counts
        ]

    def attn_forward(given, pieces):
        return call(
            functools.partial(attn_forward_kernel, forms[0], len(pieces)),
            "attn_forward",
            groups,
            place,
            [(given, whole(full)), vec_in] + arriving(pieces),
            [
                ((groups, rows, wide), BF, slot_wide, "hbm"),
                ((groups, heads, rows, rows), BF, by_slot((heads, rows, rows)), "hbm"),
                ((groups, rows, col_dev), BF, by_slot((rows, col_dev)), "hbm"),
                (weight, BF, ANY, "hbm"),
                (full, F32, whole(full), "vmem"),
                (row_vec, F32, whole(row_vec), "vmem"),
            ],
            [pltpu.VMEM(weight, BF), pltpu.VMEM(full, F32), dma((max(2 * count, groups),)), dma],
        )

    def mlp_up(given, pieces):
        return call(
            functools.partial(mlp_up_kernel, forms[1], len(pieces)),
            "mlp_up",
            groups,
            place,
            [(given, whole(full), "vmem"), vec_in] + arriving(pieces),
            [((groups, rows, hidden), BF, slot_hid, "hbm")] * 2 + [(hid_weight, BF, ANY, "hbm")],
            [pltpu.VMEM(hid_weight, BF), pltpu.VMEM(full, BF), dma((max(2 * count, groups),)), dma],
        )

    if plane:
        own = jnp.concatenate([attn_low[None], mlp_low])
        own_one, own_two = moves.first_chip(own), moves.second_chip(own)
        own_one, own_two, *attn_far = after_all((own_one, own_two, *moves.across(attn_low)))

        attn_far = jnp.stack(attn_far)
        attn_one = moves.first_chip(attn_far)
        own_three = moves.second_chip(own_one)
        up_far = moves.across(after(mlp_low[0], attn_far))
        attn_one, own_three, *up_far = after_all((attn_one, own_three, *up_far))

        attn_pair = moves.second_chip(jnp.stack([attn_far, attn_one]))
        up_far = jnp.stack(up_far)
        up_one = moves.first_chip(up_far)
        down_far = moves.across(after(mlp_low[1], up_far))
        attn_pair, up_one, *down_far = after_all((attn_pair, up_one, *down_far))

        up_sent = jnp.stack([up_far, up_one])
        up_pair = moves.second_chip(up_sent)
        down_far = jnp.stack(down_far)
        down_one = moves.first_chip(down_far)
        own_pieces = moves.both(after_all([own, own_one, own_two, own_three], attn_pair))
        attn_pieces = own_pieces + moves.both(after_all([attn_far, attn_one, attn_pair], attn_pair))
        qkv, probs, context, attn_kept, norm_one, inv_one = attn_forward(
            after(tokens, down_far), attn_pieces
        )
        up_swapped = moves.cores_of([up_far, up_one])
        norm_one, up_pair, down_one, *up_swapped = after_all(
            (norm_one, up_pair, down_one, *up_swapped)
        )

        down_sent = jnp.stack([down_far, down_one])
        down_pair = moves.second_chip(down_sent)
        up_pieces = own_pieces + [up_far, up_one, up_pair, *up_swapped, *moves.cores_of([up_pair])]
        down_swapped = moves.cores_of([after(down_far, norm_one), down_one])
        hid, slope, up_kept = mlp_up(after(norm_one, down_sent), up_pieces)
        hid, down_pair, *down_swapped = after_all((hid, down_pair, *down_swapped))
        down_pieces = own_pieces + [down_far, down_one, down_pair]
        down_pieces += down_swapped + moves.cores_of([down_pair])
    else:
        attn_pieces, up_pieces, down_pieces = moves.gather(attn_low, mlp_low)
        qkv, probs, context, attn_kept, norm_one, inv_one = attn_forward(tokens, attn_pieces)
        hid, slope, up_kept = mlp_up(norm_one, up_pieces)
    down_in = arriving(down_pieces)
    layer_out, pooled, dres, dres_low, sums_two, down_kept, *down_grads = call(
        functools.partial(mlp_down_kernel, forms[2], len(down_in), outs),
        "mlp_down",
        2 * groups,
        place,
        [
            (norm_one, whole(full), "vmem"),
            vec_in,
            (out_grad, whole(full)),
            (segment_ids.reshape(docs, SEQ), whole((docs, SEQ))),
            (hid, by_slot((rows, hidden), lambda i: i % groups), "hbm"),
        ]
        + down_in,
        [
            (full, BF, whole(full)),
            ((docs * SEGS, width), F32, whole((docs * SEGS, width))),
            (full, F32, whole(full), "vmem"),
            (full, BF, whole(full), "vmem"),
            ((3, width), F32, whole((3, width))),
            (hid_weight, BF, ANY, "hbm"),
        ]
        + grad_outs(hidden, groups),
        [
            pltpu.VMEM(hid_weight, BF),
            pltpu.VMEM(full, F32),
            pltpu.VMEM((count, block, hidden), BF),
            dma((max(2 * count, groups),)),
            dma,
        ],
    )
    down_far = moves.swap_far(down_grads) if plane else None
    down_other = moves.swap_near(down_grads) if plane else None
    dpre, dbias_hidden, *up_grads = call(
        functools.partial(mlp_back_kernel, outs),
        "mlp_back",
        groups,
        place,
        [
            (norm_one, whole(full), "vmem"),
            vec_in,
            (dres_low, whole(full), "vmem"),
            (slope, slot_hid, "hbm"),
            (down_kept, slot_hid_weight, "hbm"),
        ],
        [
            ((groups, rows, hidden), BF, slot_hid, "vmem"),
            ((groups, hidden), F32, whole((groups, hidden))),
        ]
        + grad_outs(hidden),
        [pltpu.VMEM(full, BF), pltpu.VMEM((count, block, hidden), BF)],
    )
    if plane:
        down_sent = moves.pair_ready(down_grads, down_far)
        dres = after(dres, down_sent)
        down_pair = moves.pair(down_sent)
        up_far = moves.swap_far(up_grads)
        up_other = moves.swap_near(up_grads)
    dfirst, dout, sums_one = call(
        norm_back_kernel,
        "norm_back",
        groups,
        place,
        [
            (norm_one, whole(full), "vmem"),
            (inv_one, whole(row_vec), "vmem"),
            vec_in,
            (dres, whole(full), "vmem"),
            (dpre, slot_hid, "vmem"),
            (up_kept, slot_hid_weight, "hbm"),
        ],
        [
            (full, F32, whole(full), "vmem"),
            (full, BF, whole(full), "vmem"),
            ((3, width), F32, whole((3, width))),
        ],
        [pltpu.VMEM(full, F32)],
    )
    def attn_back(start, slots, dout, counts=moves.out_counts):
        def shifted(shape):
            return by_slot(shape, lambda i: (i + start) % groups)

        outputs = [
            ((slots, rows, wide), BF, slot_wide, "hbm"),
            ((2, width), F32, whole((2, width))),
        ]
        for k in counts:
            shape = (k, slots, block, cols)
            outputs.append((shape, BF, by_piece(shape), "hbm"))
        inputs = [
            (tokens, whole(full)),
            (dout, whole(full), "vmem"),
            (qkv, shifted((rows, wide)), "hbm"),
            (probs, shifted((heads, rows, rows)), "hbm"),
            (context, shifted((rows, col_dev)), "hbm"),
            (attn_kept, shifted((count, block, cols)), "hbm"),
        ]
        return call(
            functools.partial(attn_back_kernel, len(counts), groups, start),
            "attn_back",
            slots,
            place,
            inputs,
            outputs,
            [pltpu.VMEM((count, block, cols), BF)],
        )

    def vec_grads(dbias_qv):
        return jnp.concatenate(
            [
                dbias_qv,
                dbias_hidden,
                sums_one[0:1],
                sums_two[0:1],
                sums_one[1:3],
                sums_two[1:3],
            ],
            axis=0,
        )

    if plane:
        dout, up_far = after_all((dout, up_far))
        up_sent = moves.pair_ready(up_grads, up_far)
        up_pair = moves.pair(up_sent)
        half = groups // 2
        dqkv_a, dbias_a, *a_grads = attn_back(half, half, after(dout, up_sent))
        dbias_a, down_pair, down_other, *a_grads = after_all(
            (dbias_a, down_pair, down_other, *a_grads)
        )

        down_near_sent = moves.near_ready(down_grads, down_other, down_pair)
        down_near = moves.near(down_near_sent)
        down_own = moves.own_ready(down_grads, down_other, down_pair)
        a_far = moves.swap_far(a_grads)
        a_other = moves.swap_near(a_grads)
        dqkv_b, dbias_b, *b_grads = attn_back(
            0, half, after(dout, down_near_sent, down_own), moves.last_counts
        )
        dbias_b, down_near, up_pair, up_other, a_far, a_other, *b_grads = after_all(
            (dbias_b, down_near, up_pair, up_other, a_far, a_other, *b_grads)
        )

        b_other = moves.swap_near(b_grads)
        up_near_sent = moves.near_ready(up_grads, up_other, up_pair)
        up_near = moves.near(up_near_sent)
        a_sent = moves.pair_ready(a_grads, a_far)
        a_pair = moves.pair(a_sent)
        down_block = down_own + down_near.astype(F32)
        down_got = moves.across_first(down_block)
        vec_one = moves.vec_step(vec_grads(dbias_a + dbias_b), "dp", 1)
        dfirst = after(dfirst, up_near_sent, a_sent, down_block)
    else:
        dqkv_a, dbias_qv, *a_grads = attn_back(0, groups, dout)

    def input_part(given, part, start, space):
        slots = part.shape[0]
        out = (full, F32, whole(full), space) if space else (full, BF, whole(full))
        return call(
            input_grad_kernel,
            "input_grad",
            slots,
            place,
            [
                (given, whole(full), "vmem"),
                (part, slot_wide, "hbm"),
                (attn_kept, by_slot((count, block, cols), lambda i: (i + start) % groups), "hbm"),
            ],
            [out],
            [pltpu.VMEM(full, F32)],
        )[0]

    if plane:
        input_grad = input_part(dfirst, dqkv_a, half, "vmem")
        input_grad, vec_one = after_all((input_grad, vec_one))
        vec_two = moves.vec_step(vec_one, "tp", 1)
        input_grad = input_part(input_grad, dqkv_b, 0, None)
        input_grad, b_other, up_near, down_got, vec_two = after_all(
            (input_grad, b_other, up_near, down_got, vec_two)
        )

        b_sent = moves.pair_ready(b_grads, b_other[2:4])
        b_pair = moves.pair(b_sent)
        up_block = moves.block(up_grads, up_other, up_pair, up_near)
        up_got = moves.across_first(up_block)
        down_half = moves.across_half(down_block, down_got)
        down_got = moves.across_last(down_half)
        vec_three = moves.vec_step(vec_two, "tp", 2)
        a_pair = after(a_pair, b_sent, up_block)
        a_near_sent = moves.near_ready(a_grads, a_other, a_pair)
        a_near = moves.near(a_near_sent)
        a_near, b_pair, up_got, down_got, vec_three = after_all(
            (a_near, b_pair, up_got, down_got, vec_three)
        )

        b_near_sent = moves.near_ready(b_grads, b_other, b_pair)
        b_near = moves.near(b_near_sent)
        a_block = moves.block(a_grads, a_other, a_pair, after(a_near, b_near_sent))
        a_got = moves.shifted(a_block[1].astype(BF), 1)
        up_half = moves.across_half(up_block, up_got)
        up_got = moves.across_last(up_half)
        vec_four = moves.vec_step(after(vec_three, a_block), "dp", 2)
        b_near, a_got, vec_four = after_all((b_near, a_got, vec_four), *up_half)

        a_half = (a_block[0] + a_got.astype(F32)).astype(BF)
        a_got = moves.shifted(a_half, 2)
        b_block = moves.block(b_grads, b_other, b_pair, b_near)
        b_part = moves.shifted(b_block[1].astype(BF), 1)
        vec_grad = moves.vec_step(after(vec_four, a_half, b_block), "dp", 4).reshape(-1)
        up_got, vec_grad = after_all((up_got, vec_grad))
        down_sum = down_half[0] + down_got.astype(F32)
        up_sum = up_half[0] + up_got.astype(F32)
        attn_sum = b_block[0]
        for part in (a_got, b_part):
            attn_sum = attn_sum + part.astype(F32)
    else:
        input_grad = input_part(dfirst, dqkv_a, 0, None)
        down_sum, up_sum, attn_sum = (moves.sum(part) for part in (down_grads, up_grads, a_grads))
        vec_grad = moves.total(vec_grads(dbias_qv)).reshape(-1)
    attn_grad = jnp.stack([attn_sum[:, k * col_dev : (k + 1) * col_dev] for k in range(mats)])
    mlp_grad = jnp.stack([up_sum, down_sum])
    attn_step = adam_update(
        attn_master, attn_first, attn_second, attn_grad, MATRIX_RATE, MATRIX_DECAY
    )
    mlp_step = adam_update(mlp_master, mlp_first, mlp_second, mlp_grad, MATRIX_RATE, MATRIX_DECAY)
    vec_step = adam_update(vec_master, vec_first, vec_second, vec_grad, VECTOR_RATE, 0.0)
    return (layer_out, pooled, input_grad, *attn_step, *mlp_step, *vec_step)


def solution(mesh):
    in_specs = (
        P(("dp", "tp"), None),
        P(("dp", "tp"), None),
        P(("dp", "tp")),
        P(None, "dp", "tp"),
        P(None, "dp", "tp"),
        P(None, "dp", "tp"),
        P(None, "dp", "tp"),
        P(None, "dp", "tp"),
        P(None, "dp", "tp"),
        P(),
        P(),
        P(),
    )
    out_specs = (
        P(("dp", "tp"), None),
        P(("dp", "tp"), None),
        P(("dp", "tp"), None),
        P(None, "dp", "tp"),
        P(None, "dp", "tp"),
        P(None, "dp", "tp"),
        P(None, "dp", "tp"),
        P(None, "dp", "tp"),
        P(None, "dp", "tp"),
        P(None, "dp", "tp"),
        P(None, "dp", "tp"),
        P(),
        P(),
        P(),
        P(),
    )
    return jax.shard_map(
        on_device, mesh=mesh, in_specs=in_specs, out_specs=out_specs, check_vma=False
    )
```

```python
import functools

import jax
import jax.numpy as jnp
from jax import lax
from jax.experimental import pallas as pl
from jax.experimental.pallas import tpu as pltpu
from jax.sharding import PartitionSpec as P

HEAD_DIM = 64
SEQ = 512
SEGS = 128
STEP = 10


NORM_EPS = 1e-12
BETA_ONE = 0.9
BETA_TWO = 0.999
ADAM_EPS = 1e-06
MATRIX_RATE = 0.1
VECTOR_RATE = 0.3
MATRIX_DECAY = 0.01
SCALE = HEAD_DIM ** (-0.5)
HALF_ROOT = 0.7071067811865476
PDF_SCALE = 0.3989422804014327
NT = (((1,), (1,)), ((), ()))
TN = (((0,), (0,)), ((), ()))
BF = jnp.bfloat16
F32 = jnp.float32
MIB = 1 << 20
ROW_PART = 128
BIAS_OUT, BIAS_TWO, GAIN_ONE, SHIFT_ONE, GAIN_TWO, SHIFT_TWO = range(-6, 0)


def dot(left, right):
    return jnp.dot(left, right, preferred_element_type=F32)


def dot_tn(left, right):
    return lax.dot_general(left, right, TN, preferred_element_type=F32)


def dot_nt(left, right):
    return lax.dot_general(left, right, NT, preferred_element_type=F32)


def adam_update(weight, moment_one, moment_two, gradient, step_rate, decay_rate):
    first_new = BETA_ONE * moment_one + (1.0 - BETA_ONE) * gradient
    second_new = BETA_TWO * moment_two + (1.0 - BETA_TWO) * gradient * gradient
    fix_one = 1.0 - BETA_ONE**STEP
    fix_two = 1.0 - BETA_TWO**STEP
    direction = first_new / fix_one / (jnp.sqrt(second_new / fix_two) + ADAM_EPS)
    weight_new = weight - step_rate * (direction + decay_rate * weight)
    return (first_new, second_new, weight_new, weight_new.astype(BF))


def split_blocks(pieces):
    blocks = []
    for piece in pieces:
        blocks += [piece.at[k] for k in range(piece.shape[0])] if len(piece.shape) == 4 else [piece]
    return blocks


def weight_copies(form, first, place, pieces, held, sems):
    groups, count = held.shape[0], held.shape[1]
    if form == "one":
        return [
            pltpu.make_async_copy(pieces[0].at[k], held.at[k, 0], sems.at[k]) for k in range(groups)
        ], 1
    near = [
        pltpu.make_async_copy(piece.at[first], held.at[0, place[j]], sems.at[j])
        for j, piece in enumerate(pieces[:count])
    ]
    far = [
        pltpu.make_async_copy(piece, held.at[pl.ds(1, groups - 1), place[j]], sems.at[count + j])
        for j, piece in enumerate(split_blocks(pieces[count:]))
    ]
    return near + far, count


def start_weight(copies, step):
    @pl.when(step == 0)
    def _():
        for copy in copies:
            copy.start()


def wait_weight(copies, first_part, step):
    @pl.when(step == 0)
    def _():
        for copy in copies[:first_part]:
            copy.wait()

    @pl.when(step == 1)
    def _():
        for copy in copies[first_part:]:
            copy.wait()


def keep_weight(held, out, sem, step, last):
    copy = pltpu.make_async_copy(held, out, sem)
    pl.when(step == 1)(copy.start)
    pl.when(step == last)(copy.wait)


def flat(value):
    return value.reshape(value.shape[0] * value.shape[1], value.shape[2])


def rounded(vec_ref, row):
    at = row % vec_ref.shape[0]
    return vec_ref[at : at + 1, :].astype(BF).astype(F32)


def own_part(row, own, size):
    out = row[:, 0:size]
    for k in range(1, row.shape[1] // size):
        out = jnp.where(own == k, row[:, k * size : (k + 1) * size], out)
    return out


def write_pieces(place, grad, outs):
    j = 0
    for out in outs:
        for k in range(out.shape[0]):
            out[k, 0] = grad[place[j]]
            j += 1


def normed_rows(value):
    centred = value - jnp.mean(value, axis=-1, keepdims=True)
    inverse = lax.rsqrt(jnp.mean(centred * centred, axis=-1, keepdims=True) + NORM_EPS)
    return centred * inverse, inverse


def norm_back(cot, normed, inverse, gain):
    scaled = cot * gain
    mean_one = jnp.mean(scaled, axis=-1, keepdims=True)
    mean_two = jnp.mean(scaled * normed, axis=-1, keepdims=True)
    return (scaled - mean_one - normed * mean_two) * inverse


def column_sum(value):
    return jnp.sum(value, axis=0, keepdims=True)


def attn_forward_kernel(form, n, place, x_ref, vec_ref, *refs):
    pieces = refs[:n]
    qkv_ref, probs_ref, ctx_ref, kept_ref, norm_ref, inv_ref = refs[n : n + 6]
    held, total, sems, kept_sem = refs[n + 6 :]
    slot = step = pl.program_id(0)
    steps = pl.num_programs(0)
    own = place[place.shape[0] - 1]
    width = qkv_ref.shape[2]
    part = width // 3

    copies, first_part = weight_copies(form, 0, place, pieces, held, sems)
    start_weight(copies, step)

    @pl.when(step == 0)
    def _():
        total[...] = x_ref[...].astype(F32) + rounded(vec_ref, BIAS_OUT)

    wait_weight(copies, first_part, step)
    keep_weight(held, kept_ref, kept_sem, step, steps - 1)
    bias_q = own_part(rounded(vec_ref, 0), own ^ slot, part)
    bias_v = own_part(rounded(vec_ref, 1), own ^ slot, part)
    bias = jnp.concatenate([bias_q, jnp.zeros_like(bias_q), bias_v], axis=1)
    projected = dot(x_ref[...], flat(held[slot, :, :, 0:width])) + bias
    low = projected.astype(BF)
    qkv_ref[0] = low
    heads = range(part // HEAD_DIM)

    def head(k, h):
        return low[:, k * part + h * HEAD_DIM : k * part + (h + 1) * HEAD_DIM]

    scores = [dot_nt(head(0, h) * BF(SCALE), head(1, h)) for h in heads]
    for h in heads:
        expanded = jnp.exp(scores[h] - jnp.max(scores[h], axis=-1, keepdims=True))
        inverse = 1.0 / jnp.sum(expanded, axis=-1, keepdims=True)
        probs_ref[0, h] = (expanded * inverse).astype(BF)
    parts = [dot(probs_ref[0, h], head(2, h)) for h in heads]
    context = jnp.concatenate(parts, axis=1).astype(BF)
    ctx_ref[0] = context
    added = dot_nt(context, flat(held[slot, :, :, width:]))

    total[...] += added

    @pl.when(step == steps - 1)
    def _():
        norm_ref[...], inv_ref[...] = normed_rows(total[...])


def middle_rows(norm_ref, vec_ref):
    return norm_ref[...] * rounded(vec_ref, GAIN_ONE) + rounded(vec_ref, SHIFT_ONE)


def mlp_up_kernel(form, n, place, norm_ref, vec_ref, *refs):
    pieces = refs[:n]
    hid_ref, slope_ref, kept_ref = refs[n : n + 3]
    held, low_ref, sems, kept_sem = refs[n + 3 :]
    step = pl.program_id(0)
    slot = step
    own = place[place.shape[0] - 1]

    copies, first_part = weight_copies(form, 1, place, pieces, held, sems)
    start_weight(copies, step)

    @pl.when(step == 0)
    def _():
        low_ref[...] = middle_rows(norm_ref, vec_ref).astype(BF)

    wait_weight(copies, first_part, step)
    keep_weight(held, kept_ref, kept_sem, step, pl.num_programs(0) - 1)

    bias = vec_ref[pl.ds(2 + (own ^ slot), 1), :].astype(BF).astype(F32)

    weight = flat(held[slot])
    for start in range(0, low_ref.shape[0], ROW_PART):
        at = slice(start, start + ROW_PART)
        u = dot(low_ref[at, :], weight) + bias
        cdf = 0.5 + 0.5 * lax.erf(u * HALF_ROOT)
        hid_ref[0, at, :] = (u * cdf).astype(BF)
        slope_ref[0, at, :] = (cdf + u * (jnp.exp(u * u * -0.5) * PDF_SCALE)).astype(BF)


def mlp_down_kernel(form, n, outs, place, norm_ref, vec_ref, og_ref, ids_ref, hid_ref, *refs):
    pieces = refs[:n]
    out_ref, pool_ref, dres_ref, dlow_ref, sums_ref, kept_ref = refs[n : n + 6]
    grads = refs[n + 6 : n + 6 + outs]
    held, total, grad_low, sems, kept_sem = refs[n + 6 + outs :]
    step = pl.program_id(0)
    groups = held.shape[0]

    copies, first_part = weight_copies(form, 2, place, pieces, held, sems)
    start_weight(copies, step)

    @pl.when(step == 0)
    def _():
        total[...] = middle_rows(norm_ref, vec_ref) + rounded(vec_ref, BIAS_TWO)

    wait_weight(copies, first_part, step)
    keep_weight(held, kept_ref, kept_sem, step, 2 * groups - 1)

    @pl.when(step < groups)
    def _():
        total[...] += dot_nt(hid_ref[0], flat(held[step]))

    @pl.when(step == groups - 1)
    def _():
        normed, inverse = normed_rows(total[...])
        gain = rounded(vec_ref, GAIN_TWO)
        final = normed * gain + rounded(vec_ref, SHIFT_TWO)
        high = final.astype(BF)
        out_ref[...] = high
        docs = pool_ref.shape[0] // SEGS
        for d in range(docs):
            slots = lax.broadcasted_iota(jnp.int32, (SEGS, SEQ), 0)
            onehot = jnp.where(slots == ids_ref[d : d + 1, :], 1.0, 0.0)
            counts = jnp.sum(onehot, axis=1, keepdims=True)
            marks = onehot.astype(BF)
            at = slice(d * SEQ, (d + 1) * SEQ)
            rest = (final[at] - high[at].astype(F32)).astype(BF)
            sums = dot(marks, high[at]) + dot(marks, rest)
            pool_ref[d * SEGS : (d + 1) * SEGS, :] = sums / jnp.maximum(counts, 1.0)
        cot = og_ref[...].astype(F32)
        dres = norm_back(cot, normed, inverse, gain)
        dres_ref[...] = dres
        low = dres.astype(BF)
        dlow_ref[...] = low
        sums_ref[0:1, :] = column_sum(dres)
        sums_ref[1:2, :] = column_sum(cot * normed)
        sums_ref[2:3, :] = column_sum(cot)

    @pl.when(step >= groups)
    def _():
        grad_low[...] = dot_tn(dlow_ref[...], hid_ref[0]).astype(BF).reshape(grad_low.shape)
        write_pieces(place, grad_low, grads)


def mlp_back_kernel(outs, place, norm_ref, vec_ref, dlow_ref, slope_ref, down_ref, *refs):
    dpre_ref, dbias_ref = refs[:2]
    grads = refs[2 : 2 + outs]
    low_ref, grad_low = refs[2 + outs :]
    slot = pl.program_id(0)
    own = place[place.shape[0] - 1]

    @pl.when(slot == 0)
    def _():
        low_ref[...] = middle_rows(norm_ref, vec_ref).astype(BF)

    dpre = (dot(dlow_ref[...], flat(down_ref[0])) * slope_ref[0].astype(F32)).astype(BF)
    dpre_ref[0] = dpre
    dbias_ref[pl.ds(own ^ slot, 1), :] = column_sum(dpre.astype(F32))
    grad_low[...] = dot_tn(low_ref[...], dpre).astype(BF).reshape(grad_low.shape)
    write_pieces(place, grad_low, grads)


def norm_back_kernel(place, norm_ref, inv_ref, vec_ref, dres_ref, dpre_ref, up_ref, *refs):
    dfirst_ref, dout_ref, sums_ref, total = refs
    slot = pl.program_id(0)
    added = dot_nt(dpre_ref[0], flat(up_ref[0]))

    @pl.when(slot == 0)
    def _():
        total[...] = dres_ref[...] + added

    @pl.when(slot > 0)
    def _():
        total[...] += added

    @pl.when(slot == pl.num_programs(0) - 1)
    def _():
        cot = total[...]
        normed = norm_ref[...]
        dfirst = norm_back(cot, normed, inv_ref[...], rounded(vec_ref, GAIN_ONE))
        dfirst_ref[...] = dfirst
        low = dfirst.astype(BF)
        dout_ref[...] = low
        sums_ref[0:1, :] = column_sum(dfirst)
        sums_ref[1:2, :] = column_sum(cot * normed)
        sums_ref[2:3, :] = column_sum(cot)


def attn_back_kernel(
    outs, groups, start, place, x_ref, dout_ref, qkv_ref, probs_ref, ctx_ref, weight_ref, *refs
):
    dqkv_ref, dbias_ref = refs[:2]
    grads = refs[2 : 2 + outs]
    grad_low = refs[2 + outs]
    step = pl.program_id(0)
    slot = (step + start) % groups
    own = place[place.shape[0] - 1]
    width = qkv_ref.shape[2]
    part = width // 3
    block = grad_low.shape[0:2]

    @pl.when(step == 0)
    def _():
        dbias_ref[...] = jnp.zeros_like(dbias_ref)

    context = ctx_ref[0]
    grad_out = dot_tn(dout_ref[...], context).astype(BF)
    grad_low[:, :, width:] = grad_out.reshape(block + (part,))
    dctx = dot(dout_ref[...], flat(weight_ref[0, :, :, width:])).astype(BF)
    dctx_t = dctx.T
    row_dots = dctx.astype(F32) * context.astype(F32)
    q_t = qkv_ref[0, :, 0:part].T
    heads = range(part // HEAD_DIM)

    def head(k, h):
        return qkv_ref[0, :, k * part + h * HEAD_DIM : k * part + (h + 1) * HEAD_DIM]

    at = [slice(h * HEAD_DIM, (h + 1) * HEAD_DIM) for h in heads]
    dprobs = [dot_nt(dctx[:, at[h]], head(2, h)) for h in heads]
    dv_t = [dot(dctx_t[at[h]], probs_ref[0, h]) for h in heads]
    dq, dk_t = [], []
    for h in heads:
        row_dot = jnp.sum(row_dots[:, at[h]], axis=-1, keepdims=True)
        dscores = (probs_ref[0, h].astype(F32) * (dprobs[h] - row_dot)).astype(BF)
        dq.append(dot(dscores, head(1, h)) * SCALE)
        dk_t.append(dot(q_t[at[h]], dscores) * SCALE)
    dqkv = jnp.concatenate(
        [
            jnp.concatenate(dq, axis=1).astype(BF),
            jnp.concatenate(dk_t, axis=0).astype(BF).T,
            jnp.concatenate(dv_t, axis=0).astype(BF).T,
        ],
        axis=1,
    )
    dqkv_ref[0] = dqkv
    dbias = column_sum(dqkv.astype(F32))
    for z in range(dbias_ref.shape[1] // part):
        cols = slice(z * part, (z + 1) * part)
        mine = own ^ slot == z
        dbias_ref[0:1, cols] += jnp.where(mine, dbias[:, 0:part], 0.0)
        dbias_ref[1:2, cols] += jnp.where(mine, dbias[:, 2 * part :], 0.0)
    grad_low[:, :, 0:width] = dot_tn(x_ref[...], dqkv).astype(BF).reshape(block + (width,))
    write_pieces(place, grad_low, grads)


def input_grad_kernel(place, dfirst_ref, dqkv_ref, weight_ref, out_ref, total):
    slot = pl.program_id(0)
    width = dqkv_ref.shape[2]
    added = dot_nt(dqkv_ref[0], flat(weight_ref[0, :, :, 0:width]))

    @pl.when(slot == 0)
    def _():
        total[...] = dfirst_ref[...] + added

    @pl.when(slot > 0)
    def _():
        total[...] += added

    @pl.when(slot == pl.num_programs(0) - 1)
    def _():
        out_ref[...] = total[...].astype(out_ref.dtype)


def whole(shape):
    return pl.BlockSpec(shape, lambda i, place: (0,) * len(shape))


def by_slot(shape, index=lambda i: i):
    return pl.BlockSpec((1,) + shape, lambda i, place: (index(i),) + (0,) * len(shape))


def by_piece(shape, index=lambda i, place: i):
    return pl.BlockSpec(
        (shape[0], 1) + shape[2:], lambda i, place: (0, index(i, place)) + (0,) * len(shape[2:])
    )


ANY = pl.BlockSpec(memory_space=pltpu.HBM)
FREE = pl.BlockSpec(memory_space=pl.ANY)
VMEM_LIMIT = 28 * MIB


def pinned(value, spec, space=None):
    if space == "vmem":
        return pltpu.with_memory_space_constraint(value, pltpu.VMEM)
    if space == "hbm":
        return pltpu.with_memory_space_constraint(value, pltpu.HBM)
    return value


def placed(shape, dtype, space=None):
    if space == "vmem":
        return pltpu.VMEM(shape, dtype)
    if space == "hbm":
        return pltpu.HBM(shape, dtype)
    return jax.ShapeDtypeStruct(shape, dtype)


def call(kernel, name, grid, place, inputs, outputs, scratch, aliases=None):
    return pl.pallas_call(
        kernel,
        name=name,
        out_shape=[placed(out[0], out[1], *out[3:]) for out in outputs],
        grid_spec=pltpu.PrefetchScalarGridSpec(
            num_scalar_prefetch=1,
            grid=(grid,),
            in_specs=[given[1] for given in inputs],
            out_specs=[out[2] for out in outputs],
            scratch_shapes=scratch,
        ),
        compiler_params=pltpu.CompilerParams(
            dimension_semantics=("arbitrary",), vmem_limit_bytes=VMEM_LIMIT
        ),
        input_output_aliases=aliases or {},
        cost_estimate=pl.CostEstimate(flops=1000, bytes_accessed=1000, transcendentals=0),
    )(place, *[pinned(*given) for given in inputs])


def after(value, *deps):
    deps = [dep for dep in deps if dep is not None]
    return lax.optimization_barrier((value, *deps))[0] if deps else value


def after_all(values, *deps):
    return list(lax.optimization_barrier((*values, *deps)))[: len(values)]


def xor_pairs(count, mask):
    return [(i, i ^ mask) for i in range(count)]


class PlaneTransfers:
    forms = ("pieces", "pieces", "pieces")

    def __init__(self, tp_count):
        self.count = 8
        self.groups = tp_count
        self.first = [(i, i ^ (4 if i & 1 else 2)) for i in range(8)]
        self.second = [(i, i ^ (2 if i & 1 else 4)) for i in range(8)]
        self.cores = xor_pairs(8, 1)
        me = lax.axis_index("dp")
        one = jnp.where(me % 2 == 1, 4, 2)
        two = 6 - one
        self.place = jnp.stack(
            [
                me,
                me ^ one,
                me ^ two,
                me ^ 6,
                me ^ 1,
                me ^ 1 ^ two,
                me ^ 1 ^ one,
                me ^ 7,
                lax.axis_index("tp"),
            ]
        ).astype(jnp.int32)
        self.out_counts = (4, 2, 2)
        self.last_counts = (4, 4)

    def shifted(self, shard, mask):
        return lax.ppermute(shard, "tp", xor_pairs(self.groups, mask))

    def across(self, shard):
        return [self.shifted(shard, k) for k in range(1, self.groups)]

    def cores_of(self, mine):
        return [lax.ppermute(piece, "dp", self.cores) for piece in mine]

    def both(self, mine):
        return mine + [lax.ppermute(piece, "dp", self.cores) for piece in mine]

    def first_chip(self, shards):
        return lax.ppermute(shards, "dp", self.first)

    def second_chip(self, shards):
        return lax.ppermute(shards, "dp", self.second)

    def vec_step(self, vec, axis, mask):
        size = self.count if axis == "dp" else self.groups
        return vec + lax.ppermute(vec, axis, xor_pairs(size, mask))


    def swap_far(self, grads):
        return lax.ppermute(grads[2], "dp", self.cores)

    def swap_near(self, grads):
        return lax.ppermute(grads[1], "dp", self.cores)

    def pair_ready(self, grads, far):
        return (grads[0][2:4].astype(F32) + far.astype(F32)).astype(BF)

    def pair(self, sent):
        return lax.ppermute(sent, "dp", self.second)

    def near_ready(self, grads, other, pair):
        one = grads[0][1].astype(F32) + other[1].astype(F32) + pair[1].astype(F32)
        return one.astype(BF)

    def near(self, sent):
        return lax.ppermute(sent, "dp", self.first)

    def own_ready(self, grads, other, pair):
        return grads[0][0].astype(F32) + other[0].astype(F32) + pair[0].astype(F32)

    def block(self, grads, other, pair, near):
        return self.own_ready(grads, other, pair) + near.astype(F32)


    def across_first(self, block):
        return self.shifted(jnp.stack([block[1], block[3]]).astype(BF), 1)

    def across_half(self, block, got):
        return block[0] + got[0].astype(F32), (block[2] + got[1].astype(F32)).astype(BF)

    def across_last(self, half):
        return self.shifted(half[1], 2)


class PlainTransfers:
    forms = ("one", "one", "one")

    def __init__(self, dp_count, tp_count):
        self.dp = dp_count
        self.tp = tp_count
        self.count = 1
        self.groups = tp_count
        self.place = jnp.zeros((2,), jnp.int32)
        self.out_counts = (1,)

    def one(self, shards):
        rows, columns = shards.shape
        out = lax.all_gather(shards, ("dp", "tp"), axis=0, tiled=False)
        out = out.reshape(self.dp, self.tp, rows, columns).transpose(1, 0, 2, 3)
        return [out.reshape(self.tp, self.dp * rows, columns)]

    def gather(self, attn, mlp):
        return self.one(attn), self.one(mlp[0]), self.one(mlp[1])

    def total(self, vec):
        return lax.psum(vec, ("dp", "tp"))

    def sum(self, grads):
        _, groups, rows, columns = grads[0].shape
        parts = grads[0].reshape(groups, self.dp, rows // self.dp, columns).transpose(1, 0, 2, 3)
        parts = parts.reshape(self.dp * groups, rows // self.dp, columns)
        out = lax.psum_scatter(parts, ("dp", "tp"), scatter_dimension=0, tiled=True)
        return out[0].astype(F32)


def on_device(
    tokens,
    out_grad,
    segment_ids,
    attn_master,
    attn_first,
    attn_second,
    mlp_master,
    mlp_first,
    mlp_second,
    vec_master,
    vec_first,
    vec_second,
):
    rows, width = tokens.shape
    dp_count = lax.axis_size("dp")
    groups = lax.axis_size("tp")
    mats, row_dev, col_dev = attn_master.shape
    hidden = mlp_master.shape[2]
    docs = rows // SEQ
    heads = col_dev // HEAD_DIM
    wide = 3 * col_dev
    cols = mats * col_dev
    plane = dp_count == 8 and groups == 4 and row_dev % 16 == 0
    moves = PlaneTransfers(groups) if plane else PlainTransfers(dp_count, groups)
    place = moves.place
    count = moves.count
    outs = len(moves.out_counts)
    block = width // count

    attn_low = jnp.concatenate([attn_master[k] for k in range(mats)], axis=1).astype(BF)
    vecs = vec_master.reshape(-1, width)
    mlp_low = mlp_master.astype(BF)
    forms = moves.forms

    full = (rows, width)
    row_vec = (rows, 1)
    weight = (groups, count, block, cols)
    hid_weight = (groups, count, block, hidden)
    slot_weight = by_slot((count, block, cols))
    slot_hid_weight = by_slot((count, block, hidden))
    slot_hid = by_slot((rows, hidden))
    slot_wide = by_slot((rows, wide))
    base = 2 * rows * width
    dma = pltpu.SemaphoreType.DMA
    vec_in = (vecs, whole(vecs.shape))

    def arriving(pieces):
        return [(piece, ANY, "hbm") for piece in pieces]

    def grad_outs(columns, base_step=0):
        def index(i, place):
            return jnp.maximum(i - base_step, 0)

        return [
            ((k, groups, block, columns), BF, by_piece((k, groups, block, columns), index), "hbm")
            for k in moves.out_counts
        ]

    def attn_forward(given, pieces):
        return call(
            functools.partial(attn_forward_kernel, forms[0], len(pieces)),
            "attn_forward",
            groups,
            place,
            [(given, whole(full)), vec_in] + arriving(pieces),
            [
                ((groups, rows, wide), BF, slot_wide, "hbm"),
                ((groups, heads, rows, rows), BF, by_slot((heads, rows, rows)), "hbm"),
                ((groups, rows, col_dev), BF, by_slot((rows, col_dev)), "hbm"),
                (weight, BF, ANY, "hbm"),
                (full, F32, whole(full), "vmem"),
                (row_vec, F32, whole(row_vec), "vmem"),
            ],
            [pltpu.VMEM(weight, BF), pltpu.VMEM(full, F32), dma((max(2 * count, groups),)), dma],
        )

    def mlp_up(given, pieces):
        return call(
            functools.partial(mlp_up_kernel, forms[1], len(pieces)),
            "mlp_up",
            groups,
            place,
            [(given, whole(full), "vmem"), vec_in] + arriving(pieces),
            [((groups, rows, hidden), BF, slot_hid, "hbm")] * 2 + [(hid_weight, BF, ANY, "hbm")],
            [pltpu.VMEM(hid_weight, BF), pltpu.VMEM(full, BF), dma((max(2 * count, groups),)), dma],
        )

    if plane:
        own = jnp.concatenate([attn_low[None], mlp_low])
        own_one, own_two = moves.first_chip(own), moves.second_chip(own)
        own_one, own_two, *attn_far = after_all((own_one, own_two, *moves.across(attn_low)))

        attn_far = jnp.stack(attn_far)
        attn_one = moves.first_chip(attn_far)
        own_three = moves.second_chip(own_one)
        up_far = moves.across(after(mlp_low[0], attn_far))
        attn_one, own_three, *up_far = after_all((attn_one, own_three, *up_far))

        attn_pair = moves.second_chip(jnp.stack([attn_far, attn_one]))
        up_far = jnp.stack(up_far)
        up_one = moves.first_chip(up_far)
        down_far = moves.across(after(mlp_low[1], up_far))
        attn_pair, up_one, *down_far = after_all((attn_pair, up_one, *down_far))

        up_sent = jnp.stack([up_far, up_one])
        up_pair = moves.second_chip(up_sent)
        down_far = jnp.stack(down_far)
        down_one = moves.first_chip(down_far)
        own_pieces = moves.both(after_all([own, own_one, own_two, own_three], attn_pair))
        attn_pieces = own_pieces + moves.both(after_all([attn_far, attn_one, attn_pair], attn_pair))
        qkv, probs, context, attn_kept, norm_one, inv_one = attn_forward(
            after(tokens, down_far), attn_pieces
        )
        up_swapped = moves.cores_of([up_far, up_one])
        norm_one, up_pair, down_one, *up_swapped = after_all(
            (norm_one, up_pair, down_one, *up_swapped)
        )

        down_sent = jnp.stack([down_far, down_one])
        down_pair = moves.second_chip(down_sent)
        up_pieces = own_pieces + [up_far, up_one, up_pair, *up_swapped, *moves.cores_of([up_pair])]
        down_swapped = moves.cores_of([after(down_far, norm_one), down_one])
        hid, slope, up_kept = mlp_up(after(norm_one, down_sent), up_pieces)
        hid, down_pair, *down_swapped = after_all((hid, down_pair, *down_swapped))
        down_pieces = own_pieces + [down_far, down_one, down_pair]
        down_pieces += down_swapped + moves.cores_of([down_pair])
    else:
        attn_pieces, up_pieces, down_pieces = moves.gather(attn_low, mlp_low)
        qkv, probs, context, attn_kept, norm_one, inv_one = attn_forward(tokens, attn_pieces)
        hid, slope, up_kept = mlp_up(norm_one, up_pieces)
    down_in = arriving(down_pieces)
    layer_out, pooled, dres, dres_low, sums_two, down_kept, *down_grads = call(
        functools.partial(mlp_down_kernel, forms[2], len(down_in), outs),
        "mlp_down",
        2 * groups,
        place,
        [
            (norm_one, whole(full), "vmem"),
            vec_in,
            (out_grad, whole(full)),
            (segment_ids.reshape(docs, SEQ), whole((docs, SEQ))),
            (hid, by_slot((rows, hidden), lambda i: i % groups), "hbm"),
        ]
        + down_in,
        [
            (full, BF, whole(full)),
            ((docs * SEGS, width), F32, whole((docs * SEGS, width))),
            (full, F32, whole(full), "vmem"),
            (full, BF, whole(full), "vmem"),
            ((3, width), F32, whole((3, width))),
            (hid_weight, BF, ANY, "hbm"),
        ]
        + grad_outs(hidden, groups),
        [
            pltpu.VMEM(hid_weight, BF),
            pltpu.VMEM(full, F32),
            pltpu.VMEM((count, block, hidden), BF),
            dma((max(2 * count, groups),)),
            dma,
        ],
    )
    down_far = moves.swap_far(down_grads) if plane else None
    down_other = moves.swap_near(down_grads) if plane else None
    dpre, dbias_hidden, *up_grads = call(
        functools.partial(mlp_back_kernel, outs),
        "mlp_back",
        groups,
        place,
        [
            (norm_one, whole(full), "vmem"),
            vec_in,
            (dres_low, whole(full), "vmem"),
            (slope, slot_hid, "hbm"),
            (down_kept, slot_hid_weight, "hbm"),
        ],
        [
            ((groups, rows, hidden), BF, slot_hid, "vmem"),
            ((groups, hidden), F32, whole((groups, hidden))),
        ]
        + grad_outs(hidden),
        [pltpu.VMEM(full, BF), pltpu.VMEM((count, block, hidden), BF)],
    )
    if plane:
        down_sent = moves.pair_ready(down_grads, down_far)
        dres = after(dres, down_sent)
        down_pair = moves.pair(down_sent)
        up_far = moves.swap_far(up_grads)
        up_other = moves.swap_near(up_grads)
    dfirst, dout, sums_one = call(
        norm_back_kernel,
        "norm_back",
        groups,
        place,
        [
            (norm_one, whole(full), "vmem"),
            (inv_one, whole(row_vec), "vmem"),
            vec_in,
            (dres, whole(full), "vmem"),
            (dpre, slot_hid, "vmem"),
            (up_kept, slot_hid_weight, "hbm"),
        ],
        [
            (full, F32, whole(full), "vmem"),
            (full, BF, whole(full), "vmem"),
            ((3, width), F32, whole((3, width))),
        ],
        [pltpu.VMEM(full, F32)],
    )
    def attn_back(start, slots, dout, counts=moves.out_counts):
        def shifted(shape):
            return by_slot(shape, lambda i: (i + start) % groups)

        outputs = [
            ((slots, rows, wide), BF, slot_wide, "hbm"),
            ((2, width), F32, whole((2, width))),
        ]
        for k in counts:
            shape = (k, slots, block, cols)
            outputs.append((shape, BF, by_piece(shape), "hbm"))
        inputs = [
            (tokens, whole(full)),
            (dout, whole(full), "vmem"),
            (qkv, shifted((rows, wide)), "hbm"),
            (probs, shifted((heads, rows, rows)), "hbm"),
            (context, shifted((rows, col_dev)), "hbm"),
            (attn_kept, shifted((count, block, cols)), "hbm"),
        ]
        return call(
            functools.partial(attn_back_kernel, len(counts), groups, start),
            "attn_back",
            slots,
            place,
            inputs,
            outputs,
            [pltpu.VMEM((count, block, cols), BF)],
        )

    def vec_grads(dbias_qv):
        return jnp.concatenate(
            [
                dbias_qv,
                dbias_hidden,
                sums_one[0:1],
                sums_two[0:1],
                sums_one[1:3],
                sums_two[1:3],
            ],
            axis=0,
        )

    if plane:
        dout, up_far = after_all((dout, up_far))
        up_sent = moves.pair_ready(up_grads, up_far)
        up_pair = moves.pair(up_sent)
        half = groups // 2
        dqkv_a, dbias_a, *a_grads = attn_back(half, half, after(dout, up_sent))
        dbias_a, down_pair, down_other, *a_grads = after_all(
            (dbias_a, down_pair, down_other, *a_grads)
        )

        down_near_sent = moves.near_ready(down_grads, down_other, down_pair)
        down_near = moves.near(down_near_sent)
        down_own = moves.own_ready(down_grads, down_other, down_pair)
        a_far = moves.swap_far(a_grads)
        a_other = moves.swap_near(a_grads)
        dqkv_b, dbias_b, *b_grads = attn_back(
            0, half, after(dout, down_near_sent, down_own), moves.last_counts
        )
        dbias_b, down_near, up_pair, up_other, a_far, a_other, *b_grads = after_all(
            (dbias_b, down_near, up_pair, up_other, a_far, a_other, *b_grads)
        )

        b_other = moves.swap_near(b_grads)
        up_near_sent = moves.near_ready(up_grads, up_other, up_pair)
        up_near = moves.near(up_near_sent)
        a_sent = moves.pair_ready(a_grads, a_far)
        a_pair = moves.pair(a_sent)
        down_block = down_own + down_near.astype(F32)
        down_got = moves.across_first(down_block)
        vec_one = moves.vec_step(vec_grads(dbias_a + dbias_b), "dp", 1)
        dfirst = after(dfirst, up_near_sent, a_sent, down_block)
    else:
        dqkv_a, dbias_qv, *a_grads = attn_back(0, groups, dout)

    def input_part(given, part, start, space):
        slots = part.shape[0]
        out = (full, F32, whole(full), space) if space else (full, BF, whole(full))
        return call(
            input_grad_kernel,
            "input_grad",
            slots,
            place,
            [
                (given, whole(full), "vmem"),
                (part, slot_wide, "hbm"),
                (attn_kept, by_slot((count, block, cols), lambda i: (i + start) % groups), "hbm"),
            ],
            [out],
            [pltpu.VMEM(full, F32)],
        )[0]

    if plane:
        input_grad = input_part(dfirst, dqkv_a, half, "vmem")
        input_grad, vec_one = after_all((input_grad, vec_one))
        vec_two = moves.vec_step(vec_one, "tp", 1)
        input_grad = input_part(input_grad, dqkv_b, 0, None)
        input_grad, b_other, up_near, down_got, vec_two = after_all(
            (input_grad, b_other, up_near, down_got, vec_two)
        )

        b_sent = moves.pair_ready(b_grads, b_other[2:4])
        b_pair = moves.pair(b_sent)
        up_block = moves.block(up_grads, up_other, up_pair, up_near)
        up_got = moves.across_first(up_block)
        down_half = moves.across_half(down_block, down_got)
        down_got = moves.across_last(down_half)
        vec_three = moves.vec_step(vec_two, "tp", 2)
        a_pair = after(a_pair, b_sent, up_block)
        a_near_sent = moves.near_ready(a_grads, a_other, a_pair)
        a_near = moves.near(a_near_sent)
        a_near, b_pair, up_got, down_got, vec_three = after_all(
            (a_near, b_pair, up_got, down_got, vec_three)
        )

        b_near_sent = moves.near_ready(b_grads, b_other, b_pair)
        b_near = moves.near(b_near_sent)
        a_block = moves.block(a_grads, a_other, a_pair, after(a_near, b_near_sent))
        a_got = moves.shifted(a_block[1].astype(BF), 1)
        up_half = moves.across_half(up_block, up_got)
        up_got = moves.across_last(up_half)
        vec_four = moves.vec_step(after(vec_three, a_block), "dp", 2)
        b_near, a_got, vec_four = after_all((b_near, a_got, vec_four), *up_half)

        a_half = (a_block[0] + a_got.astype(F32)).astype(BF)
        a_got = moves.shifted(a_half, 2)
        b_block = moves.block(b_grads, b_other, b_pair, b_near)
        b_part = moves.shifted(b_block[1].astype(BF), 1)
        vec_grad = moves.vec_step(after(vec_four, a_half, b_block), "dp", 4).reshape(-1)
        up_got, vec_grad = after_all((up_got, vec_grad))
        down_sum = down_half[0] + down_got.astype(F32)
        up_sum = up_half[0] + up_got.astype(F32)
        attn_sum = b_block[0]
        for part in (a_got, b_part):
            attn_sum = attn_sum + part.astype(F32)
    else:
        input_grad = input_part(dfirst, dqkv_a, 0, None)
        down_sum, up_sum, attn_sum = (moves.sum(part) for part in (down_grads, up_grads, a_grads))
        vec_grad = moves.total(vec_grads(dbias_qv)).reshape(-1)
    attn_grad = jnp.stack([attn_sum[:, k * col_dev : (k + 1) * col_dev] for k in range(mats)])
    mlp_grad = jnp.stack([up_sum, down_sum])
    attn_step = adam_update(
        attn_master, attn_first, attn_second, attn_grad, MATRIX_RATE, MATRIX_DECAY
    )
    mlp_step = adam_update(mlp_master, mlp_first, mlp_second, mlp_grad, MATRIX_RATE, MATRIX_DECAY)
    vec_step = adam_update(vec_master, vec_first, vec_second, vec_grad, VECTOR_RATE, 0.0)
    return (layer_out, pooled, input_grad, *attn_step, *mlp_step, *vec_step)


def solution(mesh):
    in_specs = (
        P(("dp", "tp"), None),
        P(("dp", "tp"), None),
        P(("dp", "tp")),
        P(None, "dp", "tp"),
        P(None, "dp", "tp"),
        P(None, "dp", "tp"),
        P(None, "dp", "tp"),
        P(None, "dp", "tp"),
        P(None, "dp", "tp"),
        P(),
        P(),
        P(),
    )
    out_specs = (
        P(("dp", "tp"), None),
        P(("dp", "tp"), None),
        P(("dp", "tp"), None),
        P(None, "dp", "tp"),
        P(None, "dp", "tp"),
        P(None, "dp", "tp"),
        P(None, "dp", "tp"),
        P(None, "dp", "tp"),
        P(None, "dp", "tp"),
        P(None, "dp", "tp"),
        P(None, "dp", "tp"),
        P(),
        P(),
        P(),
        P(),
    )
    return jax.shard_map(
        on_device, mesh=mesh, in_specs=in_specs, out_specs=out_specs, check_vma=False
    )
```

```python
import functools

import jax
import jax.numpy as jnp
from jax import lax
from jax.experimental import pallas as pl
from jax.experimental.pallas import tpu as pltpu
from jax.sharding import PartitionSpec as P

HEAD_DIM = 64
SEQ = 512
SEGS = 128
STEP = 10


NORM_EPS = 1e-12
BETA_ONE = 0.9
BETA_TWO = 0.999
ADAM_EPS = 1e-06
MATRIX_RATE = 0.1
VECTOR_RATE = 0.3
MATRIX_DECAY = 0.01
SCALE = HEAD_DIM ** (-0.5)
HALF_ROOT = 0.7071067811865476
PDF_SCALE = 0.3989422804014327
NT = (((1,), (1,)), ((), ()))
TN = (((0,), (0,)), ((), ()))
BF = jnp.bfloat16
F32 = jnp.float32
MIB = 1 << 20
ROW_PART = 128
BIAS_OUT, BIAS_TWO, GAIN_ONE, SHIFT_ONE, GAIN_TWO, SHIFT_TWO = range(-6, 0)


def dot(left, right):
    return jnp.dot(left, right, preferred_element_type=F32)


def dot_tn(left, right):
    return lax.dot_general(left, right, TN, preferred_element_type=F32)


def dot_nt(left, right):
    return lax.dot_general(left, right, NT, preferred_element_type=F32)


def adam_update(weight, moment_one, moment_two, gradient, step_rate, decay_rate):
    first_new = BETA_ONE * moment_one + (1.0 - BETA_ONE) * gradient
    second_new = BETA_TWO * moment_two + (1.0 - BETA_TWO) * gradient * gradient
    fix_one = 1.0 - BETA_ONE**STEP
    fix_two = 1.0 - BETA_TWO**STEP
    direction = first_new / fix_one / (jnp.sqrt(second_new / fix_two) + ADAM_EPS)
    weight_new = weight - step_rate * (direction + decay_rate * weight)
    return (first_new, second_new, weight_new, weight_new.astype(BF))


def split_blocks(pieces):
    blocks = []
    for piece in pieces:
        blocks += [piece.at[k] for k in range(piece.shape[0])] if len(piece.shape) == 4 else [piece]
    return blocks


def weight_copies(form, first, place, pieces, held, sems):
    groups, count = held.shape[0], held.shape[1]
    if form == "one":
        return [
            pltpu.make_async_copy(pieces[0].at[k], held.at[k, 0], sems.at[k]) for k in range(groups)
        ], 1
    near = [
        pltpu.make_async_copy(piece.at[first], held.at[0, place[j]], sems.at[j])
        for j, piece in enumerate(pieces[:count])
    ]
    far = [
        pltpu.make_async_copy(piece, held.at[pl.ds(1, groups - 1), place[j]], sems.at[count + j])
        for j, piece in enumerate(split_blocks(pieces[count:]))
    ]
    return near + far, count


def start_weight(copies, step):
    @pl.when(step == 0)
    def _():
        for copy in copies:
            copy.start()


def wait_weight(copies, first_part, step):
    @pl.when(step == 0)
    def _():
        for copy in copies[:first_part]:
            copy.wait()

    @pl.when(step == 1)
    def _():
        for copy in copies[first_part:]:
            copy.wait()


def keep_weight(held, out, sem, step, last):
    copy = pltpu.make_async_copy(held, out, sem)
    pl.when(step == 1)(copy.start)
    pl.when(step == last)(copy.wait)


def flat(value):
    return value.reshape(value.shape[0] * value.shape[1], value.shape[2])


def rounded(vec_ref, row):
    at = row % vec_ref.shape[0]
    return vec_ref[at : at + 1, :].astype(BF).astype(F32)


def own_part(row, own, size):
    out = row[:, 0:size]
    for k in range(1, row.shape[1] // size):
        out = jnp.where(own == k, row[:, k * size : (k + 1) * size], out)
    return out


def write_pieces(place, grad, outs):
    j = 0
    for out in outs:
        for k in range(out.shape[0]):
            out[k, 0] = grad[place[j]]
            j += 1


def normed_rows(value):
    centred = value - jnp.mean(value, axis=-1, keepdims=True)
    inverse = lax.rsqrt(jnp.mean(centred * centred, axis=-1, keepdims=True) + NORM_EPS)
    return centred * inverse, inverse


def norm_back(cot, normed, inverse, gain):
    scaled = cot * gain
    mean_one = jnp.mean(scaled, axis=-1, keepdims=True)
    mean_two = jnp.mean(scaled * normed, axis=-1, keepdims=True)
    return (scaled - mean_one - normed * mean_two) * inverse


def column_sum(value):
    return jnp.sum(value, axis=0, keepdims=True)


def attn_forward_kernel(form, n, place, x_ref, vec_ref, *refs):
    pieces = refs[:n]
    qkv_ref, probs_ref, ctx_ref, kept_ref, norm_ref, inv_ref = refs[n : n + 6]
    held, total, sems, kept_sem = refs[n + 6 :]
    slot = step = pl.program_id(0)
    steps = pl.num_programs(0)
    own = place[place.shape[0] - 1]
    width = qkv_ref.shape[2]
    part = width // 3

    copies, first_part = weight_copies(form, 0, place, pieces, held, sems)
    start_weight(copies, step)

    @pl.when(step == 0)
    def _():
        total[...] = x_ref[...].astype(F32) + rounded(vec_ref, BIAS_OUT)

    wait_weight(copies, first_part, step)
    keep_weight(held, kept_ref, kept_sem, step, steps - 1)
    bias_q = own_part(rounded(vec_ref, 0), own ^ slot, part)
    bias_v = own_part(rounded(vec_ref, 1), own ^ slot, part)
    bias = jnp.concatenate([bias_q, jnp.zeros_like(bias_q), bias_v], axis=1)
    projected = dot(x_ref[...], flat(held[slot, :, :, 0:width])) + bias
    low = projected.astype(BF)
    qkv_ref[0] = low
    heads = range(part // HEAD_DIM)

    def head(k, h):
        return low[:, k * part + h * HEAD_DIM : k * part + (h + 1) * HEAD_DIM]

    scores = [dot_nt(head(0, h) * BF(SCALE), head(1, h)) for h in heads]
    for h in heads:
        expanded = jnp.exp(scores[h] - jnp.max(scores[h], axis=-1, keepdims=True))
        inverse = 1.0 / jnp.sum(expanded, axis=-1, keepdims=True)
        probs_ref[0, h] = (expanded * inverse).astype(BF)
    parts = [dot(probs_ref[0, h], head(2, h)) for h in heads]
    context = jnp.concatenate(parts, axis=1).astype(BF)
    ctx_ref[0] = context
    added = dot_nt(context, flat(held[slot, :, :, width:]))

    total[...] += added

    @pl.when(step == steps - 1)
    def _():
        norm_ref[...], inv_ref[...] = normed_rows(total[...])


def middle_rows(norm_ref, vec_ref):
    return norm_ref[...] * rounded(vec_ref, GAIN_ONE) + rounded(vec_ref, SHIFT_ONE)


def mlp_up_kernel(form, n, place, norm_ref, vec_ref, *refs):
    pieces = refs[:n]
    hid_ref, slope_ref, kept_ref = refs[n : n + 3]
    held, low_ref, sems, kept_sem = refs[n + 3 :]
    step = pl.program_id(0)
    slot = step
    own = place[place.shape[0] - 1]

    copies, first_part = weight_copies(form, 1, place, pieces, held, sems)
    start_weight(copies, step)

    @pl.when(step == 0)
    def _():
        low_ref[...] = middle_rows(norm_ref, vec_ref).astype(BF)

    wait_weight(copies, first_part, step)
    keep_weight(held, kept_ref, kept_sem, step, pl.num_programs(0) - 1)

    bias = vec_ref[pl.ds(2 + (own ^ slot), 1), :].astype(BF).astype(F32)

    weight = flat(held[slot])
    for start in range(0, low_ref.shape[0], ROW_PART):
        at = slice(start, start + ROW_PART)
        u = dot(low_ref[at, :], weight) + bias
        cdf = 0.5 + 0.5 * lax.erf(u * HALF_ROOT)
        hid_ref[0, at, :] = (u * cdf).astype(BF)
        slope_ref[0, at, :] = (cdf + u * (jnp.exp(u * u * -0.5) * PDF_SCALE)).astype(BF)


def mlp_down_kernel(form, n, outs, place, norm_ref, vec_ref, og_ref, ids_ref, hid_ref, *refs):
    pieces = refs[:n]
    out_ref, pool_ref, dres_ref, dlow_ref, sums_ref, kept_ref = refs[n : n + 6]
    grads = refs[n + 6 : n + 6 + outs]
    held, total, grad_low, sems, kept_sem = refs[n + 6 + outs :]
    step = pl.program_id(0)
    groups = held.shape[0]

    copies, first_part = weight_copies(form, 2, place, pieces, held, sems)
    start_weight(copies, step)

    @pl.when(step == 0)
    def _():
        total[...] = middle_rows(norm_ref, vec_ref) + rounded(vec_ref, BIAS_TWO)

    wait_weight(copies, first_part, step)
    keep_weight(held, kept_ref, kept_sem, step, 2 * groups - 1)

    @pl.when(step < groups)
    def _():
        total[...] += dot_nt(hid_ref[0], flat(held[step]))

    @pl.when(step == groups - 1)
    def _():
        normed, inverse = normed_rows(total[...])
        gain = rounded(vec_ref, GAIN_TWO)
        final = normed * gain + rounded(vec_ref, SHIFT_TWO)
        high = final.astype(BF)
        out_ref[...] = high
        docs = pool_ref.shape[0] // SEGS
        for d in range(docs):
            slots = lax.broadcasted_iota(jnp.int32, (SEGS, SEQ), 0)
            onehot = jnp.where(slots == ids_ref[d : d + 1, :], 1.0, 0.0)
            counts = jnp.sum(onehot, axis=1, keepdims=True)
            marks = onehot.astype(BF)
            at = slice(d * SEQ, (d + 1) * SEQ)
            rest = (final[at] - high[at].astype(F32)).astype(BF)
            sums = dot(marks, high[at]) + dot(marks, rest)
            pool_ref[d * SEGS : (d + 1) * SEGS, :] = sums / jnp.maximum(counts, 1.0)
        cot = og_ref[...].astype(F32)
        dres = norm_back(cot, normed, inverse, gain)
        dres_ref[...] = dres
        low = dres.astype(BF)
        dlow_ref[...] = low
        sums_ref[0:1, :] = column_sum(dres)
        sums_ref[1:2, :] = column_sum(cot * normed)
        sums_ref[2:3, :] = column_sum(cot)

    @pl.when(step >= groups)
    def _():
        grad_low[...] = dot_tn(dlow_ref[...], hid_ref[0]).astype(BF).reshape(grad_low.shape)
        write_pieces(place, grad_low, grads)


def mlp_back_kernel(outs, place, norm_ref, vec_ref, dlow_ref, slope_ref, down_ref, *refs):
    dpre_ref, dbias_ref = refs[:2]
    grads = refs[2 : 2 + outs]
    low_ref, grad_low = refs[2 + outs :]
    slot = pl.program_id(0)
    own = place[place.shape[0] - 1]

    @pl.when(slot == 0)
    def _():
        low_ref[...] = middle_rows(norm_ref, vec_ref).astype(BF)

    dpre = (dot(dlow_ref[...], flat(down_ref[0])) * slope_ref[0].astype(F32)).astype(BF)
    dpre_ref[0] = dpre
    grad_low[...] = dot_tn(low_ref[...], dpre).astype(BF).reshape(grad_low.shape)
    write_pieces(place, grad_low, grads)
    dbias_ref[pl.ds(own ^ slot, 1), :] = column_sum(dpre.astype(F32))


def norm_back_kernel(place, norm_ref, inv_ref, vec_ref, dres_ref, dpre_ref, up_ref, *refs):
    dfirst_ref, dout_ref, sums_ref, total = refs
    slot = pl.program_id(0)
    added = dot_nt(dpre_ref[0], flat(up_ref[0]))

    @pl.when(slot == 0)
    def _():
        total[...] = dres_ref[...] + added

    @pl.when(slot > 0)
    def _():
        total[...] += added

    @pl.when(slot == pl.num_programs(0) - 1)
    def _():
        cot = total[...]
        normed = norm_ref[...]
        dfirst = norm_back(cot, normed, inv_ref[...], rounded(vec_ref, GAIN_ONE))
        dfirst_ref[...] = dfirst
        low = dfirst.astype(BF)
        dout_ref[...] = low
        sums_ref[0:1, :] = column_sum(dfirst)
        sums_ref[1:2, :] = column_sum(cot * normed)
        sums_ref[2:3, :] = column_sum(cot)


def attn_back_kernel(
    outs, groups, start, place, x_ref, dout_ref, qkv_ref, probs_ref, ctx_ref, weight_ref, *refs
):
    dqkv_ref, dbias_ref = refs[:2]
    grads = refs[2 : 2 + outs]
    grad_low = refs[2 + outs]
    step = pl.program_id(0)
    slot = (step + start) % groups
    own = place[place.shape[0] - 1]
    width = qkv_ref.shape[2]
    part = width // 3
    block = grad_low.shape[0:2]

    @pl.when(step == 0)
    def _():
        dbias_ref[...] = jnp.zeros_like(dbias_ref)

    context = ctx_ref[0]
    grad_out = dot_tn(dout_ref[...], context).astype(BF)
    grad_low[:, :, width:] = grad_out.reshape(block + (part,))
    dctx = dot(dout_ref[...], flat(weight_ref[0, :, :, width:])).astype(BF)
    dctx_t = dctx.T
    row_dots = dctx.astype(F32) * context.astype(F32)
    q_t = qkv_ref[0, :, 0:part].T
    heads = range(part // HEAD_DIM)

    def head(k, h):
        return qkv_ref[0, :, k * part + h * HEAD_DIM : k * part + (h + 1) * HEAD_DIM]

    at = [slice(h * HEAD_DIM, (h + 1) * HEAD_DIM) for h in heads]
    dprobs = [dot_nt(dctx[:, at[h]], head(2, h)) for h in heads]
    dv_t = [dot(dctx_t[at[h]], probs_ref[0, h]) for h in heads]
    dq, dk_t = [], []
    for h in heads:
        row_dot = jnp.sum(row_dots[:, at[h]], axis=-1, keepdims=True)
        dscores = (probs_ref[0, h].astype(F32) * (dprobs[h] - row_dot)).astype(BF)
        dq.append(dot(dscores, head(1, h)) * SCALE)
        dk_t.append(dot(q_t[at[h]], dscores) * SCALE)
    dqkv = jnp.concatenate(
        [
            jnp.concatenate(dq, axis=1).astype(BF),
            jnp.concatenate(dk_t, axis=0).astype(BF).T,
            jnp.concatenate(dv_t, axis=0).astype(BF).T,
        ],
        axis=1,
    )
    dqkv_ref[0] = dqkv
    dbias = column_sum(dqkv.astype(F32))
    for z in range(dbias_ref.shape[1] // part):
        cols = slice(z * part, (z + 1) * part)
        mine = own ^ slot == z
        dbias_ref[0:1, cols] += jnp.where(mine, dbias[:, 0:part], 0.0)
        dbias_ref[1:2, cols] += jnp.where(mine, dbias[:, 2 * part :], 0.0)
    grad_low[:, :, 0:width] = dot_tn(x_ref[...], dqkv).astype(BF).reshape(block + (width,))
    write_pieces(place, grad_low, grads)


def input_grad_kernel(place, dfirst_ref, dqkv_ref, weight_ref, out_ref, total):
    slot = pl.program_id(0)
    width = dqkv_ref.shape[2]
    added = dot_nt(dqkv_ref[0], flat(weight_ref[0, :, :, 0:width]))

    @pl.when(slot == 0)
    def _():
        total[...] = dfirst_ref[...] + added

    @pl.when(slot > 0)
    def _():
        total[...] += added

    @pl.when(slot == pl.num_programs(0) - 1)
    def _():
        out_ref[...] = total[...].astype(out_ref.dtype)


def whole(shape):
    return pl.BlockSpec(shape, lambda i, place: (0,) * len(shape))


def by_slot(shape, index=lambda i: i):
    return pl.BlockSpec((1,) + shape, lambda i, place: (index(i),) + (0,) * len(shape))


def by_piece(shape, index=lambda i, place: i):
    return pl.BlockSpec(
        (shape[0], 1) + shape[2:], lambda i, place: (0, index(i, place)) + (0,) * len(shape[2:])
    )


ANY = pl.BlockSpec(memory_space=pltpu.HBM)
FREE = pl.BlockSpec(memory_space=pl.ANY)
VMEM_LIMIT = 28 * MIB


def pinned(value, spec, space=None):
    if space == "vmem":
        return pltpu.with_memory_space_constraint(value, pltpu.VMEM)
    if space == "hbm":
        return pltpu.with_memory_space_constraint(value, pltpu.HBM)
    return value


def placed(shape, dtype, space=None):
    if space == "vmem":
        return pltpu.VMEM(shape, dtype)
    if space == "hbm":
        return pltpu.HBM(shape, dtype)
    return jax.ShapeDtypeStruct(shape, dtype)


def call(kernel, name, grid, place, inputs, outputs, scratch, aliases=None):
    return pl.pallas_call(
        kernel,
        name=name,
        out_shape=[placed(out[0], out[1], *out[3:]) for out in outputs],
        grid_spec=pltpu.PrefetchScalarGridSpec(
            num_scalar_prefetch=1,
            grid=(grid,),
            in_specs=[given[1] for given in inputs],
            out_specs=[out[2] for out in outputs],
            scratch_shapes=scratch,
        ),
        compiler_params=pltpu.CompilerParams(
            dimension_semantics=("arbitrary",), vmem_limit_bytes=VMEM_LIMIT
        ),
        input_output_aliases=aliases or {},
        cost_estimate=pl.CostEstimate(flops=1000, bytes_accessed=1000, transcendentals=0),
    )(place, *[pinned(*given) for given in inputs])


def after(value, *deps):
    deps = [dep for dep in deps if dep is not None]
    return lax.optimization_barrier((value, *deps))[0] if deps else value


def after_all(values, *deps):
    return list(lax.optimization_barrier((*values, *deps)))[: len(values)]


def xor_pairs(count, mask):
    return [(i, i ^ mask) for i in range(count)]


class PlaneTransfers:
    forms = ("pieces", "pieces", "pieces")

    def __init__(self, tp_count):
        self.count = 8
        self.groups = tp_count
        self.first = [(i, i ^ (4 if i & 1 else 2)) for i in range(8)]
        self.second = [(i, i ^ (2 if i & 1 else 4)) for i in range(8)]
        self.cores = xor_pairs(8, 1)
        me = lax.axis_index("dp")
        one = jnp.where(me % 2 == 1, 4, 2)
        two = 6 - one
        self.place = jnp.stack(
            [
                me,
                me ^ one,
                me ^ two,
                me ^ 6,
                me ^ 1,
                me ^ 1 ^ two,
                me ^ 1 ^ one,
                me ^ 7,
                lax.axis_index("tp"),
            ]
        ).astype(jnp.int32)
        self.out_counts = (4, 2, 2)
        self.last_counts = (4, 4)

    def shifted(self, shard, mask):
        return lax.ppermute(shard, "tp", xor_pairs(self.groups, mask))

    def across(self, shard):
        return [self.shifted(shard, k) for k in range(1, self.groups)]

    def cores_of(self, mine):
        return [lax.ppermute(piece, "dp", self.cores) for piece in mine]

    def both(self, mine):
        return mine + [lax.ppermute(piece, "dp", self.cores) for piece in mine]

    def first_chip(self, shards):
        return lax.ppermute(shards, "dp", self.first)

    def second_chip(self, shards):
        return lax.ppermute(shards, "dp", self.second)

    def vec_step(self, vec, axis, mask):
        size = self.count if axis == "dp" else self.groups
        return vec + lax.ppermute(vec, axis, xor_pairs(size, mask))


    def swap_far(self, grads):
        return lax.ppermute(grads[2], "dp", self.cores)

    def swap_near(self, grads):
        return lax.ppermute(grads[1], "dp", self.cores)

    def pair_ready(self, grads, far):
        return (grads[0][2:4].astype(F32) + far.astype(F32)).astype(BF)

    def pair(self, sent):
        return lax.ppermute(sent, "dp", self.second)

    def near_ready(self, grads, other, pair):
        one = grads[0][1].astype(F32) + other[1].astype(F32) + pair[1].astype(F32)
        return one.astype(BF)

    def near(self, sent):
        return lax.ppermute(sent, "dp", self.first)

    def own_ready(self, grads, other, pair):
        return grads[0][0].astype(F32) + other[0].astype(F32) + pair[0].astype(F32)

    def block(self, grads, other, pair, near):
        return self.own_ready(grads, other, pair) + near.astype(F32)


    def across_first(self, block):
        return self.shifted(jnp.stack([block[1], block[3]]).astype(BF), 1)

    def across_half(self, block, got):
        return block[0] + got[0].astype(F32), (block[2] + got[1].astype(F32)).astype(BF)

    def across_last(self, half):
        return self.shifted(half[1], 2)


class PlainTransfers:
    forms = ("one", "one", "one")

    def __init__(self, dp_count, tp_count):
        self.dp = dp_count
        self.tp = tp_count
        self.count = 1
        self.groups = tp_count
        self.place = jnp.zeros((2,), jnp.int32)
        self.out_counts = (1,)

    def one(self, shards):
        rows, columns = shards.shape
        out = lax.all_gather(shards, ("dp", "tp"), axis=0, tiled=False)
        out = out.reshape(self.dp, self.tp, rows, columns).transpose(1, 0, 2, 3)
        return [out.reshape(self.tp, self.dp * rows, columns)]

    def gather(self, attn, mlp):
        return self.one(attn), self.one(mlp[0]), self.one(mlp[1])

    def total(self, vec):
        return lax.psum(vec, ("dp", "tp"))

    def sum(self, grads):
        _, groups, rows, columns = grads[0].shape
        parts = grads[0].reshape(groups, self.dp, rows // self.dp, columns).transpose(1, 0, 2, 3)
        parts = parts.reshape(self.dp * groups, rows // self.dp, columns)
        out = lax.psum_scatter(parts, ("dp", "tp"), scatter_dimension=0, tiled=True)
        return out[0].astype(F32)


def on_device(
    tokens,
    out_grad,
    segment_ids,
    attn_master,
    attn_first,
    attn_second,
    mlp_master,
    mlp_first,
    mlp_second,
    vec_master,
    vec_first,
    vec_second,
):
    rows, width = tokens.shape
    dp_count = lax.axis_size("dp")
    groups = lax.axis_size("tp")
    mats, row_dev, col_dev = attn_master.shape
    hidden = mlp_master.shape[2]
    docs = rows // SEQ
    heads = col_dev // HEAD_DIM
    wide = 3 * col_dev
    cols = mats * col_dev
    plane = dp_count == 8 and groups == 4 and row_dev % 16 == 0
    moves = PlaneTransfers(groups) if plane else PlainTransfers(dp_count, groups)
    place = moves.place
    count = moves.count
    outs = len(moves.out_counts)
    block = width // count

    attn_low = jnp.concatenate([attn_master[k] for k in range(mats)], axis=1).astype(BF)
    vecs = vec_master.reshape(-1, width)
    mlp_low = mlp_master.astype(BF)
    forms = moves.forms

    full = (rows, width)
    row_vec = (rows, 1)
    weight = (groups, count, block, cols)
    hid_weight = (groups, count, block, hidden)
    slot_weight = by_slot((count, block, cols))
    slot_hid_weight = by_slot((count, block, hidden))
    slot_hid = by_slot((rows, hidden))
    slot_wide = by_slot((rows, wide))
    base = 2 * rows * width
    dma = pltpu.SemaphoreType.DMA
    vec_in = (vecs, whole(vecs.shape))

    def arriving(pieces):
        return [(piece, ANY, "hbm") for piece in pieces]

    def grad_outs(columns, base_step=0):
        def index(i, place):
            return jnp.maximum(i - base_step, 0)

        return [
            ((k, groups, block, columns), BF, by_piece((k, groups, block, columns), index), "hbm")
            for k in moves.out_counts
        ]

    def attn_forward(given, pieces):
        return call(
            functools.partial(attn_forward_kernel, forms[0], len(pieces)),
            "attn_forward",
            groups,
            place,
            [(given, whole(full)), vec_in] + arriving(pieces),
            [
                ((groups, rows, wide), BF, slot_wide, "hbm"),
                ((groups, heads, rows, rows), BF, by_slot((heads, rows, rows)), "hbm"),
                ((groups, rows, col_dev), BF, by_slot((rows, col_dev)), "hbm"),
                (weight, BF, ANY, "hbm"),
                (full, F32, whole(full), "vmem"),
                (row_vec, F32, whole(row_vec), "vmem"),
            ],
            [pltpu.VMEM(weight, BF), pltpu.VMEM(full, F32), dma((max(2 * count, groups),)), dma],
        )

    def mlp_up(given, pieces):
        return call(
            functools.partial(mlp_up_kernel, forms[1], len(pieces)),
            "mlp_up",
            groups,
            place,
            [(given, whole(full), "vmem"), vec_in] + arriving(pieces),
            [((groups, rows, hidden), BF, slot_hid, "hbm")] * 2 + [(hid_weight, BF, ANY, "hbm")],
            [pltpu.VMEM(hid_weight, BF), pltpu.VMEM(full, BF), dma((max(2 * count, groups),)), dma],
        )

    if plane:
        own = jnp.concatenate([attn_low[None], mlp_low])
        own_one, own_two = moves.first_chip(own), moves.second_chip(own)
        own_one, own_two, *attn_far = after_all((own_one, own_two, *moves.across(attn_low)))

        attn_far = jnp.stack(attn_far)
        attn_one = moves.first_chip(attn_far)
        own_three = moves.second_chip(own_one)
        up_far = moves.across(after(mlp_low[0], attn_far))
        attn_one, own_three, *up_far = after_all((attn_one, own_three, *up_far))

        attn_pair = moves.second_chip(jnp.stack([attn_far, attn_one]))
        up_far = jnp.stack(up_far)
        up_one = moves.first_chip(up_far)
        down_far = moves.across(after(mlp_low[1], up_far))
        attn_pair, up_one, *down_far = after_all((attn_pair, up_one, *down_far))

        up_sent = jnp.stack([up_far, up_one])
        up_pair = moves.second_chip(up_sent)
        down_far = jnp.stack(down_far)
        down_one = moves.first_chip(down_far)
        own_pieces = moves.both(after_all([own, own_one, own_two, own_three], attn_pair))
        attn_pieces = own_pieces + moves.both(after_all([attn_far, attn_one, attn_pair], attn_pair))
        qkv, probs, context, attn_kept, norm_one, inv_one = attn_forward(
            after(tokens, down_far), attn_pieces
        )
        up_swapped = moves.cores_of([up_far, up_one])
        norm_one, up_pair, down_one, *up_swapped = after_all(
            (norm_one, up_pair, down_one, *up_swapped)
        )

        down_sent = jnp.stack([down_far, down_one])
        down_pair = moves.second_chip(down_sent)
        up_pieces = own_pieces + [up_far, up_one, up_pair, *up_swapped, *moves.cores_of([up_pair])]
        down_swapped = moves.cores_of([after(down_far, norm_one), down_one])
        hid, slope, up_kept = mlp_up(after(norm_one, down_sent), up_pieces)
        hid, down_pair, *down_swapped = after_all((hid, down_pair, *down_swapped))
        down_pieces = own_pieces + [down_far, down_one, down_pair]
        down_pieces += down_swapped + moves.cores_of([down_pair])
    else:
        attn_pieces, up_pieces, down_pieces = moves.gather(attn_low, mlp_low)
        qkv, probs, context, attn_kept, norm_one, inv_one = attn_forward(tokens, attn_pieces)
        hid, slope, up_kept = mlp_up(norm_one, up_pieces)
    down_in = arriving(down_pieces)
    layer_out, pooled, dres, dres_low, sums_two, down_kept, *down_grads = call(
        functools.partial(mlp_down_kernel, forms[2], len(down_in), outs),
        "mlp_down",
        2 * groups,
        place,
        [
            (norm_one, whole(full), "vmem"),
            vec_in,
            (out_grad, whole(full)),
            (segment_ids.reshape(docs, SEQ), whole((docs, SEQ))),
            (hid, by_slot((rows, hidden), lambda i: i % groups), "hbm"),
        ]
        + down_in,
        [
            (full, BF, whole(full)),
            ((docs * SEGS, width), F32, whole((docs * SEGS, width))),
            (full, F32, whole(full), "vmem"),
            (full, BF, whole(full), "vmem"),
            ((3, width), F32, whole((3, width))),
            (hid_weight, BF, ANY, "hbm"),
        ]
        + grad_outs(hidden, groups),
        [
            pltpu.VMEM(hid_weight, BF),
            pltpu.VMEM(full, F32),
            pltpu.VMEM((count, block, hidden), BF),
            dma((max(2 * count, groups),)),
            dma,
        ],
    )
    down_far = moves.swap_far(down_grads) if plane else None
    down_other = moves.swap_near(down_grads) if plane else None
    dpre, dbias_hidden, *up_grads = call(
        functools.partial(mlp_back_kernel, outs),
        "mlp_back",
        groups,
        place,
        [
            (norm_one, whole(full), "vmem"),
            vec_in,
            (dres_low, whole(full), "vmem"),
            (slope, slot_hid, "hbm"),
            (down_kept, slot_hid_weight, "hbm"),
        ],
        [
            ((groups, rows, hidden), BF, slot_hid, "vmem"),
            ((groups, hidden), F32, whole((groups, hidden))),
        ]
        + grad_outs(hidden),
        [pltpu.VMEM(full, BF), pltpu.VMEM((count, block, hidden), BF)],
    )
    if plane:
        down_sent = moves.pair_ready(down_grads, down_far)
        dres = after(dres, down_sent)
        down_pair = moves.pair(down_sent)
        up_far = moves.swap_far(up_grads)
        up_other = moves.swap_near(up_grads)
    dfirst, dout, sums_one = call(
        norm_back_kernel,
        "norm_back",
        groups,
        place,
        [
            (norm_one, whole(full), "vmem"),
            (inv_one, whole(row_vec), "vmem"),
            vec_in,
            (dres, whole(full), "vmem"),
            (dpre, slot_hid, "vmem"),
            (up_kept, slot_hid_weight, "hbm"),
        ],
        [
            (full, F32, whole(full), "vmem"),
            (full, BF, whole(full), "vmem"),
            ((3, width), F32, whole((3, width))),
        ],
        [pltpu.VMEM(full, F32)],
    )
    def attn_back(start, slots, dout, counts=moves.out_counts):
        def shifted(shape):
            return by_slot(shape, lambda i: (i + start) % groups)

        outputs = [
            ((slots, rows, wide), BF, slot_wide, "hbm"),
            ((2, width), F32, whole((2, width))),
        ]
        for k in counts:
            shape = (k, slots, block, cols)
            outputs.append((shape, BF, by_piece(shape), "hbm"))
        inputs = [
            (tokens, whole(full)),
            (dout, whole(full), "vmem"),
            (qkv, shifted((rows, wide)), "hbm"),
            (probs, shifted((heads, rows, rows)), "hbm"),
            (context, shifted((rows, col_dev)), "hbm"),
            (attn_kept, shifted((count, block, cols)), "hbm"),
        ]
        return call(
            functools.partial(attn_back_kernel, len(counts), groups, start),
            "attn_back",
            slots,
            place,
            inputs,
            outputs,
            [pltpu.VMEM((count, block, cols), BF)],
        )

    def vec_grads(dbias_qv):
        return jnp.concatenate(
            [
                dbias_qv,
                dbias_hidden,
                sums_one[0:1],
                sums_two[0:1],
                sums_one[1:3],
                sums_two[1:3],
            ],
            axis=0,
        )

    if plane:
        dout, up_far = after_all((dout, up_far))
        up_sent = moves.pair_ready(up_grads, up_far)
        up_pair = moves.pair(up_sent)
        half = groups // 2
        dqkv_a, dbias_a, *a_grads = attn_back(half, half, after(dout, up_sent))
        dbias_a, down_pair, down_other, *a_grads = after_all(
            (dbias_a, down_pair, down_other, *a_grads)
        )

        down_near_sent = moves.near_ready(down_grads, down_other, down_pair)
        down_near = moves.near(down_near_sent)
        down_own = moves.own_ready(down_grads, down_other, down_pair)
        a_far = moves.swap_far(a_grads)
        a_other = moves.swap_near(a_grads)
        dqkv_b, dbias_b, *b_grads = attn_back(
            0, half, after(dout, down_near_sent, down_own), moves.last_counts
        )
        dbias_b, down_near, up_pair, up_other, a_far, a_other, *b_grads = after_all(
            (dbias_b, down_near, up_pair, up_other, a_far, a_other, *b_grads)
        )

        b_other = moves.swap_near(b_grads)
        up_near_sent = moves.near_ready(up_grads, up_other, up_pair)
        up_near = moves.near(up_near_sent)
        a_sent = moves.pair_ready(a_grads, a_far)
        a_pair = moves.pair(a_sent)
        down_block = down_own + down_near.astype(F32)
        down_got = moves.across_first(down_block)
        vec_one = moves.vec_step(vec_grads(dbias_a + dbias_b), "dp", 1)
        dfirst = after(dfirst, up_near_sent, a_sent, down_block)
    else:
        dqkv_a, dbias_qv, *a_grads = attn_back(0, groups, dout)

    def input_part(given, part, start, space):
        slots = part.shape[0]
        out = (full, F32, whole(full), space) if space else (full, BF, whole(full))
        return call(
            input_grad_kernel,
            "input_grad",
            slots,
            place,
            [
                (given, whole(full), "vmem"),
                (part, slot_wide, "hbm"),
                (attn_kept, by_slot((count, block, cols), lambda i: (i + start) % groups), "hbm"),
            ],
            [out],
            [pltpu.VMEM(full, F32)],
        )[0]

    if plane:
        input_grad = input_part(dfirst, dqkv_a, half, "vmem")
        input_grad, vec_one = after_all((input_grad, vec_one))
        vec_two = moves.vec_step(vec_one, "tp", 1)
        input_grad = input_part(input_grad, dqkv_b, 0, None)
        input_grad, b_other, up_near, down_got, vec_two = after_all(
            (input_grad, b_other, up_near, down_got, vec_two)
        )

        b_sent = moves.pair_ready(b_grads, b_other[2:4])
        b_pair = moves.pair(b_sent)
        up_block = moves.block(up_grads, up_other, up_pair, up_near)
        up_got = moves.across_first(up_block)
        down_half = moves.across_half(down_block, down_got)
        down_got = moves.across_last(down_half)
        vec_three = moves.vec_step(vec_two, "tp", 2)
        a_pair = after(a_pair, b_sent, up_block)
        a_near_sent = moves.near_ready(a_grads, a_other, a_pair)
        a_near = moves.near(a_near_sent)
        a_own = moves.own_ready(a_grads, a_other, a_pair)
        a_near, b_pair, up_got, down_got, vec_three = after_all(
            (a_near, b_pair, up_got, down_got, vec_three)
        )

        b_near_sent = moves.near_ready(b_grads, b_other, b_pair)
        b_near = moves.near(b_near_sent)
        a_block = a_own + after(a_near, b_near_sent).astype(F32)
        a_got = moves.shifted(a_block[1].astype(BF), 1)
        up_half = moves.across_half(up_block, up_got)
        up_got = moves.across_last(up_half)
        vec_four = moves.vec_step(after(vec_three, a_block), "dp", 2)
        b_near, a_got, vec_four = after_all((b_near, a_got, vec_four), *up_half)

        a_half = (a_block[0] + a_got.astype(F32)).astype(BF)
        a_got = moves.shifted(a_half, 2)
        b_block = moves.block(b_grads, b_other, b_pair, b_near)
        b_part = moves.shifted(b_block[1].astype(BF), 1)
        vec_grad = moves.vec_step(after(vec_four, a_half, b_block), "dp", 4).reshape(-1)
        up_got, vec_grad = after_all((up_got, vec_grad))
        down_sum = down_half[0] + down_got.astype(F32)
        up_sum = up_half[0] + up_got.astype(F32)
        attn_sum = b_block[0]
        for part in (a_got, b_part):
            attn_sum = attn_sum + part.astype(F32)
    else:
        input_grad = input_part(dfirst, dqkv_a, 0, None)
        down_sum, up_sum, attn_sum = (moves.sum(part) for part in (down_grads, up_grads, a_grads))
        vec_grad = moves.total(vec_grads(dbias_qv)).reshape(-1)
    attn_grad = jnp.stack([attn_sum[:, k * col_dev : (k + 1) * col_dev] for k in range(mats)])
    mlp_grad = jnp.stack([up_sum, down_sum])
    attn_step = adam_update(
        attn_master, attn_first, attn_second, attn_grad, MATRIX_RATE, MATRIX_DECAY
    )
    mlp_step = adam_update(mlp_master, mlp_first, mlp_second, mlp_grad, MATRIX_RATE, MATRIX_DECAY)
    vec_step = adam_update(vec_master, vec_first, vec_second, vec_grad, VECTOR_RATE, 0.0)
    return (layer_out, pooled, input_grad, *attn_step, *mlp_step, *vec_step)


def solution(mesh):
    in_specs = (
        P(("dp", "tp"), None),
        P(("dp", "tp"), None),
        P(("dp", "tp")),
        P(None, "dp", "tp"),
        P(None, "dp", "tp"),
        P(None, "dp", "tp"),
        P(None, "dp", "tp"),
        P(None, "dp", "tp"),
        P(None, "dp", "tp"),
        P(),
        P(),
        P(),
    )
    out_specs = (
        P(("dp", "tp"), None),
        P(("dp", "tp"), None),
        P(("dp", "tp"), None),
        P(None, "dp", "tp"),
        P(None, "dp", "tp"),
        P(None, "dp", "tp"),
        P(None, "dp", "tp"),
        P(None, "dp", "tp"),
        P(None, "dp", "tp"),
        P(None, "dp", "tp"),
        P(None, "dp", "tp"),
        P(),
        P(),
        P(),
        P(),
    )
    return jax.shard_map(
        on_device, mesh=mesh, in_specs=in_specs, out_specs=out_specs, check_vma=False
    )
```
